32 devices in a mesh: row: 4 (over z), col: 8 (over y, x, core).
Axes of the slice: x: 2, y: 2, z: 4, core: 2. Of those that a mesh axis runs over, the one named last changes fastest.
Arguments:
- matrix: float32 [3072, 3072], P('row', 'col'), may hold values from -6 to 6
- panel_t: float32 [512, 3072], P('col', 'row'), may hold values from -0.25 to 0.25
- inverse_lower: float32 [512, 512], replicated, as said below
- pivot_rows: int32 [512], replicated, may hold values from 0 to 3071, as said below
Outputs:
- updated: float32 [3072, 3072], P('row', 'col')
The draws below stay inside these ranges and needn't reach their ends.
Inputs may be any that keep to these rules, and one draw needn't show every extreme that they name: `pivot_rows`: entries are distinct; entry j is either j itself or a row at or past 768, so the interchanges are disjoint swaps. Exactly 256 entries differ from their position. The rows of one index of row are named by at most 128 entries, and in every draw some index of row is named by exactly 128. `inverse_lower`: zero above the diagonal and one on it.
All inputs are finite; a program needn't handle non-finite values.
Results may differ from the reference program's by a relative error of at most 0.000058.
Values sent between devices are 32-bit elements; how exact they have to be, the bound alone decides.
No kernel may reach another device: no remote copies, remote signals or barrier semaphores. Data moves between devices by JAX's collectives and lax.ppermute only.
A program may use at most 64 MiB of HBM per device.

```python
import jax
import jax.numpy as jnp
from jax import lax

NB = 512
ROWS_DEV = 768
NR = 3072
NC = 3072
N_ROW = 4


def draw_inverse_lower(key, part):
    values = jax.random.normal(key, (NB, NB), jnp.float32) / NB ** 0.5
    return jnp.tril(values, -1) + jnp.eye(NB, dtype=jnp.float32)


def draw_pivot_rows(key, part):
    slot_count = NB // N_ROW
    other_count = N_ROW - 1
    first_key, second_key, third_key, fourth_key = jax.random.split(key, 4)
    device_keys = jax.random.split(first_key, other_count)
    offsets = jax.vmap(lambda k: jax.random.permutation(k, ROWS_DEV)[:slot_count])(device_keys).astype(jnp.int32)
    fullest = jax.random.randint(second_key, (), 0, other_count).astype(jnp.int32)
    order = (fullest + jnp.arange(other_count, dtype=jnp.int32)) % other_count
    devices = 1 + order
    candidates = devices[:, None] * ROWS_DEV + jnp.take(offsets, order, axis=0)
    leading = candidates[0]
    others = jax.random.permutation(third_key, candidates[1:].reshape(-1)).astype(jnp.int32)
    pool = jnp.concatenate([leading, others]).astype(jnp.int32)
    column_order = jax.random.permutation(fourth_key, NB).astype(jnp.int32)
    rank = jnp.zeros((NB,), jnp.int32).at[column_order].set(jnp.arange(NB, dtype=jnp.int32))
    half = NB // 2
    moved = rank < half
    chosen = jnp.take(pool, jnp.clip(rank, 0, half - 1), axis=0)
    places = jnp.arange(NB, dtype=jnp.int32)
    return jnp.where(moved, chosen, places).astype(jnp.int32)


def levels(key, shape, cuts, least, high):
    def one(dim, blocks):
        steps = jax.random.uniform(jax.random.fold_in(jax.random.fold_in(key, 6), dim), (blocks,), jnp.float32, least / len(cuts), high / len(cuts))
        return jnp.repeat(jnp.exp(steps), shape[dim] // blocks).reshape((-1,) + (1,) * (len(shape) - dim - 1))

    level = one(*cuts[0])
    for cut in cuts[1:]:
        level = level * one(*cut)
    return level


def bell_draw(stream_key, extent, scale, reach, cuts=(), kind=jnp.bfloat16):
    entries = jax.random.normal(stream_key, extent, jnp.float32) * scale
    if len(cuts) > 0:
        entries = levels(stream_key, extent, cuts, -0.22, 0.18) * entries
    return jnp.clip(entries, min=-reach, max=reach).astype(kind)


def setup_inputs(seed: int = 0) -> dict:
    arg_keys = jax.random.split(jax.random.key(seed), 5)
    matrix = bell_draw(arg_keys[0], (NR, NC), 1.0, 6.0, ((0, 4), (1, 8)), jnp.float32)
    panel_t = bell_draw(arg_keys[1], (NB, NR), NB ** -0.5, 0.25, ((0, 8), (1, 4)), jnp.float32)
    inverse_lower = draw_inverse_lower(jax.random.fold_in(arg_keys[4], 71), 0)
    pivot_rows = draw_pivot_rows(jax.random.fold_in(arg_keys[4], 71), 0)
    return dict(matrix=matrix, panel_t=panel_t, inverse_lower=inverse_lower, pivot_rows=pivot_rows)


def reference(matrix, panel_t, inverse_lower, pivot_rows):
    total_rows = matrix.shape[0]
    width = inverse_lower.shape[0]
    places = jnp.arange(width, dtype=jnp.int32)
    moved = pivot_rows != places
    picked = jnp.take(matrix, pivot_rows, axis=0)
    initial = matrix[:width]
    target = jnp.where(moved, pivot_rows, total_rows).astype(jnp.int32)
    swapped = matrix.at[target].set(initial, mode="drop")
    upper = jnp.dot(inverse_lower, picked, precision=lax.Precision.HIGHEST, preferred_element_type=jnp.float32)
    product = jnp.dot(panel_t.T, upper, precision=lax.Precision.HIGHEST, preferred_element_type=jnp.float32)
    updated = swapped - product
    updated = updated.at[:width].set(upper)
    return updated
```

```python
import functools

import jax
import jax.numpy as jnp
from jax import lax
from jax.experimental import pallas as pl
from jax.experimental.pallas import tpu as pltpu
from jax.sharding import PartitionSpec as P

F32 = jnp.float32
BF16 = jnp.bfloat16
VMEM = pl.BlockSpec(memory_space=pltpu.VMEM)
SMEM = pl.BlockSpec(memory_space=pltpu.SMEM)
LIMIT = 48 * 1024 * 1024


def halves(x):
    high = x.astype(BF16)
    low = (x - high.astype(F32)).astype(BF16)
    return high, low


def thirds(x):
    high = x.astype(BF16)
    rest = x - high.astype(F32)
    middle = rest.astype(BF16)
    low = (rest - middle.astype(F32)).astype(BF16)
    return high, middle, low


def mm(a, b):
    return jnp.dot(a, b, preferred_element_type=F32)


def mm_nt(a, b):
    return lax.dot_general(a, b, (((1,), (1,)), ((), ())), preferred_element_type=F32)


def mm_tn(a, b):
    return lax.dot_general(a, b, (((0,), (0,)), ((), ())), preferred_element_type=F32)


def classify(pivot, count, rows):
    width = pivot.shape[1]
    lanes = lax.broadcasted_iota(jnp.int32, (1, width), 1)
    kind = jnp.where(pivot != lanes, pivot // rows, 0)
    padded = -(-count // 16) * 16
    owner = lax.broadcasted_iota(jnp.int32, (padded, width), 0)
    member = owner == kind
    before = lax.broadcasted_iota(jnp.int32, (width, width), 0) < lax.broadcasted_iota(
        jnp.int32, (width, width), 1
    )
    ranks = mm(member.astype(BF16), before.astype(BF16))
    place = jnp.sum(jnp.where(member, ranks, 0.0), axis=0, keepdims=True)
    return kind, place.astype(jnp.int32)


def one_hot(position, slots):
    slot = lax.broadcasted_iota(jnp.int32, (slots, position.shape[1]), 0)
    return slot == position


def pick_kernel(count, me_ref, pivot_ref, matrix_ref, stay_ref, send_ref):
    rows, cols = matrix_ref.shape
    width = pivot_ref.shape[1]
    slot = width // count
    me = me_ref[0]
    pivot = pivot_ref[...]
    kind, place = classify(pivot, count, rows)

    @pl.when(me == 0)
    def _():
        parts = thirds(matrix_ref[:width, :])
        stay = one_hot(jnp.where(kind == 0, place, -1), stay_ref.shape[0]).astype(BF16)
        stay_ref[...] = sum(mm(stay, part) for part in reversed(parts))
        moved = one_hot(jnp.where(kind == 0, -1, kind * slot + place), width).astype(BF16)
        send_ref[...] = sum(mm(moved, part) for part in reversed(parts))

    @pl.when(me != 0)
    def _():
        parts = thirds(matrix_ref[...])
        mine = one_hot(jnp.where(kind == me, place, -1), slot)
        source = jnp.sum(jnp.where(mine, pivot - me * rows, 0), axis=1, keepdims=True)
        pick = lax.broadcasted_iota(jnp.int32, (slot, rows), 1) == source
        pick = pick.astype(BF16)
        got = sum(mm(pick, part) for part in reversed(parts))
        stay_ref[...] = jnp.zeros_like(stay_ref)
        for d in range(count):
            send_ref[pl.ds(d * slot, slot), :] = got


def coefficient_kernel(count, me_ref, shard_ids, pivot_ref, inverse_ref, matrix_ref, *refs):
    shards = refs[:-3]
    base_ref, high_ref, low_ref = refs[-3:]
    rows, cols = matrix_ref.shape
    width = pivot_ref.shape[1]
    slot = width // count
    stay = width // 2
    depth = shards[0].shape[0]
    total = stay + width
    me = me_ref[0]
    pivot = pivot_ref[...]
    kind, place = classify(pivot, count, rows)
    position = jnp.where(kind == 0, place, stay + kind * slot + place)
    spread = one_hot(position, total).astype(BF16)
    inv_high, inv_low = halves(inverse_ref[...])
    col_high = mm_nt(inv_high, spread).astype(BF16)
    col_low = mm_nt(inv_low, spread).astype(BF16)

    acc = jnp.zeros((rows, total), F32)
    pan = jnp.concatenate([s[...] for s in shards], axis=0)
    pan_high, pan_low = halves(pan)
    order_a, order_b = [], []
    for k in range(len(shards)):
        start = pl.multiple_of(shard_ids[k] * depth, depth)
        order_a.append(start)
    shard_of = lax.broadcasted_iota(jnp.int32, (width, 1), 0)
    source = jnp.zeros((width, 1), jnp.int32)
    for k in range(len(shards)):
        inside = (shard_of >= k * depth) & (shard_of < (k + 1) * depth)
        source = jnp.where(inside, shard_of - k * depth + shard_ids[k] * depth, source)
    order = (lax.broadcasted_iota(jnp.int32, (width, width), 1) == source).astype(BF16)
    ord_high = mm(order, col_high).astype(BF16)
    ord_low = mm(order, col_low).astype(BF16)
    acc = mm_tn(pan_low, ord_high) + mm_tn(pan_high, ord_low) + mm_tn(pan_high, ord_high)
    value = -acc

    local = pivot - me * rows
    row_ids = lax.broadcasted_iota(jnp.int32, (rows, width), 0)
    landing = (row_ids == local) & (kind == me) & (kind != 0)
    mine = one_hot(jnp.where((kind == me) & (kind != 0), place, -1), slot).astype(BF16)
    land = mm_nt(landing.astype(BF16), mine)
    value = jnp.concatenate([value[:, :stay], land, value[:, stay + slot :]], axis=1)
    taken = jnp.sum(landing.astype(F32), axis=1, keepdims=True)
    high, low = halves(value)
    high_ref[...] = high
    low_ref[...] = low
    base_ref[...] = jnp.where(taken > 0.5, 0.0, matrix_ref[...])

    @pl.when(me == 0)
    def _():
        high_ref[:width, :] = col_high
        low_ref[:width, :] = col_low
        base_ref[:width, :] = jnp.zeros((width, cols), F32)


def update_kernel(base_ref, high_ref, low_ref, moved_ref, *refs):
    stays, out_ref = refs[:-1], refs[-1]
    stay_rows = stays[0].shape[0]
    stay = stays[0][...]
    for other in stays[1:]:
        stay = stay + other[...]
    s_high, s_low = halves(stay)
    m_high, m_low = halves(moved_ref[...])
    high, low = high_ref[...], low_ref[...]
    s_part = mm(low[:, :stay_rows], s_high) + mm(high[:, :stay_rows], s_low) + mm(high[:, :stay_rows], s_high)
    m_part = mm(low[:, stay_rows:], m_high) + mm(high[:, stay_rows:], m_low) + mm(high[:, stay_rows:], m_high)
    out_ref[...] = base_ref[...] + (s_part + m_part)


def gather_shards(shard, count):
    held, masks = [shard], [0]
    bits = []
    bit = 1
    while bit < count:
        bits.append(bit)
        bit *= 2
    while bits:
        group = [bits.pop()]
        if bits and bits[-1] > 1:
            group.append(bits.pop())
        steps = [group[0]] if len(group) == 1 else [group[0], group[1], group[0] | group[1]]
        new, new_masks = [], []
        for step in steps:
            pairs = [(i, i ^ step) for i in range(count)]
            for piece, mask in zip(held, masks):
                new.append(lax.ppermute(piece, "col", pairs))
                new_masks.append(mask ^ step)
        held, masks = held + new, masks + new_masks
    return held, masks


def spread_rows(stay, count):
    middle = count // 2
    first = lax.ppermute(stay, "row", [(0, middle)])
    parts = [stay, first]
    up = down = first
    for k in range(1, count):
        if middle + k < count:
            up = lax.ppermute(up, "row", [(middle + k - 1, middle + k)])
            parts.append(up)
        if middle - k > 0:
            down = lax.ppermute(down, "row", [(middle - k + 1, middle - k)])
            parts.append(down)
    return parts


def local(row_count, col_count, matrix, panel_t, inverse_lower, pivot_rows):
    rows, cols = matrix.shape
    width = inverse_lower.shape[0]
    slot = width // row_count
    stay = width // 2
    me = lax.axis_index("row").astype(jnp.int32).reshape(1)
    column = lax.axis_index("col").astype(jnp.int32)
    pivot = pivot_rows.reshape(1, width)
    params = pltpu.CompilerParams(vmem_limit_bytes=LIMIT)

    stayed, sent = pl.pallas_call(
        functools.partial(pick_kernel, row_count),
        out_shape=(
            jax.ShapeDtypeStruct((stay, cols), F32),
            jax.ShapeDtypeStruct((width, cols), F32),
        ),
        in_specs=[SMEM, VMEM, VMEM],
        out_specs=(VMEM, VMEM),
        compiler_params=params,
        name="pick",
    )(me, pivot, matrix)

    stays = spread_rows(stayed, row_count)
    moved = lax.all_to_all(sent, "row", split_axis=0, concat_axis=0, tiled=True)
    shards, masks = gather_shards(panel_t, col_count)
    ids = column ^ jnp.array(masks, jnp.int32)

    base, high, low = pl.pallas_call(
        functools.partial(coefficient_kernel, row_count),
        out_shape=(
            jax.ShapeDtypeStruct((rows, cols), F32),
            jax.ShapeDtypeStruct((rows, stay + width), BF16),
            jax.ShapeDtypeStruct((rows, stay + width), BF16),
        ),
        in_specs=[SMEM, SMEM] + [VMEM] * (3 + len(shards)),
        out_specs=(VMEM, VMEM, VMEM),
        compiler_params=params,
        name="coefficients",
    )(me, ids, pivot, inverse_lower, matrix, *shards)

    return pl.pallas_call(
        update_kernel,
        out_shape=jax.ShapeDtypeStruct((rows, cols), F32),
        in_specs=[VMEM] * (4 + len(stays)),
        out_specs=VMEM,
        compiler_params=params,
        name="update",
    )(base, high, low, moved, *stays)


def solution(mesh):
    in_specs = (P("row", "col"), P("col", "row"), P(), P())
    out_specs = P("row", "col")
    return jax.shard_map(
        functools.partial(local, mesh.shape["row"], mesh.shape["col"]),
        mesh=mesh,
        in_specs=in_specs,
        out_specs=out_specs,
        check_vma=False,
    )
```

```python
import functools

import jax
import jax.numpy as jnp
from jax import lax
from jax.experimental import pallas as pl
from jax.experimental.pallas import tpu as pltpu
from jax.sharding import PartitionSpec as P

F32 = jnp.float32
BF16 = jnp.bfloat16
VMEM = pl.BlockSpec(memory_space=pltpu.VMEM)
SMEM = pl.BlockSpec(memory_space=pltpu.SMEM)
HBM = pl.BlockSpec(memory_space=pltpu.HBM)
PARAMS = pltpu.CompilerParams(vmem_limit_bytes=20 * 1024 * 1024)


def halves(x):
    high = x.astype(BF16)
    low = (x - high.astype(F32)).astype(BF16)
    return high, low


def thirds(x):
    high = x.astype(BF16)
    rest = x - high.astype(F32)
    middle = rest.astype(BF16)
    low = (rest - middle.astype(F32)).astype(BF16)
    return high, middle, low


def mm(a, b):
    return jnp.dot(a, b, preferred_element_type=F32)


def mm_nt(a, b):
    return lax.dot_general(a, b, (((1,), (1,)), ((), ())), preferred_element_type=F32)


def mm_tn(a, b):
    return lax.dot_general(a, b, (((0,), (0,)), ((), ())), preferred_element_type=F32)


def classify(pivot, count, rows):
    width = pivot.shape[1]
    lanes = lax.broadcasted_iota(jnp.int32, (1, width), 1)
    kind = jnp.where(pivot != lanes, pivot // rows, 0)
    padded = -(-count // 16) * 16
    owner = lax.broadcasted_iota(jnp.int32, (padded, width), 0)
    member = owner == kind
    before = lax.broadcasted_iota(jnp.int32, (width, width), 0) < lax.broadcasted_iota(
        jnp.int32, (width, width), 1
    )
    ranks = mm(member.astype(BF16), before.astype(BF16))
    place = jnp.sum(jnp.where(member, ranks, 0.0), axis=0, keepdims=True)
    return kind, place.astype(jnp.int32)


def one_hot(position, slots):
    slot = lax.broadcasted_iota(jnp.int32, (slots, position.shape[1]), 0)
    return (slot == position).astype(BF16)


def picked(pick, rows):
    high, middle, low = thirds(rows)
    return mm(pick, low) + mm(pick, middle) + mm(pick, high)


def plan(count):
    middle, chunks = count // 2, count // 2
    first = [(0, middle, ("stay", c)) for c in range(chunks)]
    relays, down, late = [], [], []
    for c in range(chunks):
        for k in range(1, count):
            if middle + k < count:
                relays.append((middle + k - 1, middle + k, ("stay", c)))
            if middle - k > 0:
                relays.append((middle - k + 1, middle - k, ("stay", c)))
    for gap in range(count - 1, 0, -1):
        down += [(r, r - gap, ("pick", r)) for r in range(count - 1, gap - 1, -1) if r > 0]
    for gap in range(1, count):
        down += [(r, r + gap, ("pick", r)) for r in range(middle, count - gap)]
    for s in [1] + list(range(count - 1, 1, -1)):
        late.append((0, s, ("moved", s)))
    for gap in range(1, count):
        late += [(r, r + gap, ("pick", r)) for r in range(1, min(middle, count - gap))]
    ready = {(0, ("stay", c)): 0 for c in range(chunks)}
    rounds = []
    while first or relays or down or late:
        now, senders, targets = [], set(), set()
        waiting = len(rounds) <= chunks
        for queue in (first, relays, down, [] if waiting else late):
            for move in list(queue):
                s, t, item = move
                known = item[0] != "stay" or ready.get((s, item), len(rounds) + 1) <= len(rounds)
                if known and s not in senders and t not in targets:
                    now.append(move)
                    senders.add(s)
                    targets.add(t)
                    queue.remove(move)
        for s, t, item in now:
            ready[t, item] = len(rounds) + 3
        rounds.append(now)
    return rounds


def pick_kernel(count, order, me_ref, pivot_ref, matrix_ref, *refs):
    outs, (rows_ref, pivot_v, sem) = refs[:-3], refs[-3:]
    rows, cols = matrix_ref.shape
    width = pivot_ref.shape[1]
    slot = width // count
    me = me_ref[0]
    point = pltpu.make_async_copy(pivot_ref, pivot_v, sem.at[0])
    head = pltpu.make_async_copy(matrix_ref.at[:width], rows_ref.at[:width], sem.at[1])
    tail = pltpu.make_async_copy(matrix_ref.at[width:], rows_ref.at[width:], sem.at[2])
    point.start()
    head.start()
    tail.start()
    point.wait()
    pivot = pivot_v[...]
    kind, place = classify(pivot, count, rows)
    head.wait()
    tail.wait()

    @pl.when(me == 0)
    def _():
        start = jnp.full(kind.shape, -count * width, jnp.int32)
        for k, (name, which) in enumerate(order):
            if name == "moved":
                start = jnp.where(kind == which, k * slot, start)
            else:
                inside = (kind == 0) & (place >= which * slot) & (place < (which + 1) * slot)
                start = jnp.where(inside, (k - which) * slot, start)
        got = picked(one_hot(start + place, len(order) * slot), rows_ref[:width, :])
        for k, out in enumerate(outs):
            out[...] = got[k * slot : (k + 1) * slot, :]

    @pl.when(me != 0)
    def _():
        mine = lax.broadcasted_iota(jnp.int32, (slot, width), 0) == jnp.where(kind == me, place, -1)
        source = jnp.sum(jnp.where(mine, pivot - me * rows, 0), axis=1, keepdims=True)
        pick = (lax.broadcasted_iota(jnp.int32, (slot, rows), 1) == source).astype(BF16)
        got = picked(pick, rows_ref[...])
        for out in outs:
            out[...] = got


def coefficient_kernel(count, me_ref, ids_ref, pivot_ref, inverse_ref, matrix_ref, *refs):
    shards = refs[:-8]
    base_ref, high_ref, low_ref, pivot_v, inv_ref, pan_ref, rows_ref, sem = refs[-8:]
    rows, cols = matrix_ref.shape
    width = pivot_ref.shape[1]
    slot = width // count
    stay = width // 2
    depth = shards[0].shape[0]
    total = stay + width
    me = me_ref[0]
    copies = [
        pltpu.make_async_copy(pivot_ref, pivot_v, sem.at[0]),
        pltpu.make_async_copy(inverse_ref, inv_ref, sem.at[1]),
        pltpu.make_async_copy(matrix_ref, rows_ref, sem.at[2]),
    ]
    for copy in copies:
        copy.start()
    for k, shard in enumerate(shards):
        pan_ref[pl.ds(pl.multiple_of(ids_ref[k] * depth, depth), depth), :] = shard[...]
    copies[0].wait()
    pivot = pivot_v[...]
    kind, place = classify(pivot, count, rows)
    spread = one_hot(jnp.where(kind == 0, place, stay + kind * slot + place), total)

    local_row = jnp.where((kind == me) & (kind != 0), pivot - me * rows, -1)
    landing = (lax.broadcasted_iota(jnp.int32, (rows, width), 0) == local_row).astype(BF16)
    mine = one_hot(jnp.where((kind == me) & (kind != 0), place, -1), slot)
    land = mm_nt(landing, mine)
    taken = jnp.sum(land, axis=1, keepdims=True)
    copies[1].wait()
    inv_high, inv_low = halves(inv_ref[...])
    col_high = mm_nt(inv_high, spread).astype(BF16)
    col_low = mm_nt(inv_low, spread).astype(BF16)
    copies[2].wait()
    base_ref[...] = jnp.where(taken > 0.5, 0.0, rows_ref[...])

    pan_high, pan_low = halves(pan_ref[...])
    value = mm_tn(pan_low, col_high) + mm_tn(pan_high, col_low) + mm_tn(pan_high, col_high)
    high, low = halves(-value)
    high_ref[...] = high
    low_ref[...] = low
    high_ref[:, stay : stay + slot] = land.astype(BF16)
    low_ref[:, stay : stay + slot] = jnp.zeros((rows, slot), BF16)

    @pl.when(me == 0)
    def _():
        high_ref[:width, :] = col_high
        low_ref[:width, :] = col_low
        base_ref[:width, :] = jnp.zeros((width, cols), F32)


def update_kernel(count, places, me_ref, base_ref, high_ref, low_ref, *refs):
    arrays, (out_ref, row_high, row_low) = refs[:-3], refs[-3:]
    slot = arrays[0].shape[0]
    me = me_ref[0]
    for r in range(count):

        @pl.when(me == r)
        def _(r=r):
            for block, k in enumerate(places[r]):
                part = pl.ds(block * slot, slot)
                if k is None:
                    row_high[part, :] = jnp.zeros(arrays[0].shape, BF16)
                    row_low[part, :] = jnp.zeros(arrays[0].shape, BF16)
                else:
                    row_high[part, :], row_low[part, :] = halves(arrays[k][...])

    high = high_ref[...]
    part = mm(low_ref[...], row_high[...]) + mm(high, row_low[...]) + mm(high, row_high[...])
    out_ref[...] = base_ref[...] + part


def gather_shards(shard, count):
    held, masks = [shard], [0]
    bits = []
    bit = 1
    while bit < count:
        bits.append(bit)
        bit *= 2
    while bits:
        group = [bits.pop()]
        if bits and bits[-1] > 1:
            group.append(bits.pop())
        steps = [group[0]] if len(group) == 1 else [group[0], group[1], group[0] | group[1]]
        new, new_masks = [], []
        for step in steps:
            pairs = [(i, i ^ step) for i in range(count)]
            for piece, mask in zip(held, masks):
                new.append(lax.ppermute(piece, "col", pairs))
                new_masks.append(mask ^ step)
        held, masks = held + new, masks + new_masks
    return held, masks


def local(row_count, col_count, matrix, panel_t, inverse_lower, pivot_rows):
    rows, cols = matrix.shape
    width = inverse_lower.shape[0]
    slot = width // row_count
    stay = width // 2
    me = lax.axis_index("row").astype(jnp.int32)
    column = lax.axis_index("col").astype(jnp.int32)
    here = me.reshape(1)
    pivot = pivot_rows.reshape(1, width)
    item_shape = jax.ShapeDtypeStruct((slot, cols), F32)

    rounds = plan(row_count)
    order = [item for moves in rounds for s, t, item in moves if s == 0]
    own = pl.pallas_call(
        functools.partial(pick_kernel, row_count, order),
        out_shape=(item_shape,) * len(order),
        in_specs=[SMEM, HBM, HBM],
        out_specs=(VMEM,) * len(order),
        scratch_shapes=[
            pltpu.VMEM((rows, cols), F32),
            pltpu.VMEM((1, width), jnp.int32),
            pltpu.SemaphoreType.DMA((3,)),
        ],
        compiler_params=PARAMS,
        name="pick",
    )(here, pivot, matrix)

    arrays = list(own)
    found = [{} for _ in range(row_count)]
    for k, item in enumerate(order):
        found[0][item] = k
    for r in range(1, row_count):
        found[r]["pick", r] = 0
    for moves in rounds:
        leaving = [item for s, t, item in moves if s == 0]
        operand = own[order.index(leaving[0])] if leaving else own[0]
        for s, t, item in moves:
            if s != 0 and item[0] == "stay":
                operand = jnp.where(me == s, arrays[found[s][item]], operand)
        for s, t, item in moves:
            found[t][item] = len(arrays)
        arrays.append(lax.ppermute(operand, "row", [(s, t) for s, t, item in moves]))
    blocks = [("stay", c) for c in range(row_count // 2)]
    places = [
        [found[r].get(item) for item in blocks + [("moved", r)] + [("pick", p) for p in range(1, row_count)]]
        for r in range(row_count)
    ]

    shards, masks = gather_shards(panel_t, col_count)
    ids = column ^ jnp.array(masks, jnp.int32)

    total = stay + width
    base, high, low = pl.pallas_call(
        functools.partial(coefficient_kernel, row_count),
        out_shape=(
            jax.ShapeDtypeStruct((rows, cols), F32),
            jax.ShapeDtypeStruct((rows, total), BF16),
            jax.ShapeDtypeStruct((rows, total), BF16),
        ),
        in_specs=[SMEM, SMEM, HBM, HBM, HBM] + [VMEM] * len(shards),
        out_specs=(VMEM,) * 3,
        scratch_shapes=[
            pltpu.VMEM((1, width), jnp.int32),
            pltpu.VMEM((width, width), F32),
            pltpu.VMEM((width, rows), F32),
            pltpu.VMEM((rows, cols), F32),
            pltpu.SemaphoreType.DMA((3,)),
        ],
        compiler_params=PARAMS,
        name="coefficients",
    )(here, ids, pivot, inverse_lower, matrix, *shards)

    return pl.pallas_call(
        functools.partial(update_kernel, row_count, places),
        out_shape=jax.ShapeDtypeStruct((rows, cols), F32),
        in_specs=[SMEM] + [VMEM] * (3 + len(arrays)),
        out_specs=VMEM,
        scratch_shapes=[pltpu.VMEM((total, cols), BF16), pltpu.VMEM((total, cols), BF16)],
        compiler_params=PARAMS,
        name="update",
    )(here, base, high, low, *arrays)


def solution(mesh):
    in_specs = (P("row", "col"), P("col", "row"), P(), P())
    out_specs = P("row", "col")
    return jax.shard_map(
        functools.partial(local, mesh.shape["row"], mesh.shape["col"]),
        mesh=mesh,
        in_specs=in_specs,
        out_specs=out_specs,
        check_vma=False,
    )
```

```python
import functools

import jax
import jax.numpy as jnp
from jax import lax
from jax.experimental import pallas as pl
from jax.experimental.pallas import tpu as pltpu
from jax.sharding import PartitionSpec as P

F32 = jnp.float32
BF16 = jnp.bfloat16
VMEM = pl.BlockSpec(memory_space=pltpu.VMEM)
SMEM = pl.BlockSpec(memory_space=pltpu.SMEM)
ANY = pl.BlockSpec(memory_space=pl.ANY)
HBM = pl.BlockSpec(memory_space=pltpu.HBM)
LONG = pl.CostEstimate(flops=40_000_000_000, transcendentals=0, bytes_accessed=100_000_000)
PARAMS = pltpu.CompilerParams(vmem_limit_bytes=20 * 1024 * 1024)


def halves(x):
    high = x.astype(BF16)
    low = (x - high.astype(F32)).astype(BF16)
    return high, low


def thirds(x):
    high = x.astype(BF16)
    rest = x - high.astype(F32)
    middle = rest.astype(BF16)
    low = (rest - middle.astype(F32)).astype(BF16)
    return high, middle, low


def mm(a, b):
    return jnp.dot(a, b, preferred_element_type=F32)


def mm_nt(a, b):
    return lax.dot_general(a, b, (((1,), (1,)), ((), ())), preferred_element_type=F32)


def mm_tn(a, b):
    return lax.dot_general(a, b, (((0,), (0,)), ((), ())), preferred_element_type=F32)


def classify(pivot, count, rows):
    width = pivot.shape[1]
    lanes = lax.broadcasted_iota(jnp.int32, (1, width), 1)
    kind = jnp.where(pivot != lanes, pivot // rows, 0)
    padded = -(-count // 16) * 16
    owner = lax.broadcasted_iota(jnp.int32, (padded, width), 0)
    member = owner == kind
    before = lax.broadcasted_iota(jnp.int32, (width, width), 0) < lax.broadcasted_iota(
        jnp.int32, (width, width), 1
    )
    ranks = mm(member.astype(BF16), before.astype(BF16))
    place = jnp.sum(jnp.where(member, ranks, 0.0), axis=0, keepdims=True)
    return kind, place.astype(jnp.int32)


def one_hot(position, slots):
    slot = lax.broadcasted_iota(jnp.int32, (slots, position.shape[1]), 0)
    return (slot == position).astype(BF16)


def picked(pick, rows):
    high, middle, low = thirds(rows)
    return mm(pick, low) + mm(pick, middle) + mm(pick, high)


def plan(count):
    middle, chunks = count // 2, count // 2
    first = [(0, middle, ("stay", c)) for c in range(chunks)]
    relays, down, late = [], [], []
    for c in range(chunks):
        for k in range(1, count):
            if middle + k < count:
                relays.append((middle + k - 1, middle + k, ("stay", c)))
            if middle - k > 0:
                relays.append((middle - k + 1, middle - k, ("stay", c)))
    for gap in range(count - 1, 0, -1):
        down += [(r, r - gap, ("pick", r)) for r in range(count - 1, gap - 1, -1) if r > 0]
    for gap in range(1, count):
        down += [(r, r + gap, ("pick", r)) for r in range(middle, count - gap)]
    for s in [1] + list(range(count - 1, 1, -1)):
        late.append((0, s, ("moved", s)))
    for gap in range(1, count):
        late += [(r, r + gap, ("pick", r)) for r in range(1, min(middle, count - gap))]
    ready = {(0, ("stay", c)): 0 for c in range(chunks)}
    rounds = []
    while first or relays or down or late:
        now, senders, targets = [], set(), set()
        waiting = len(rounds) <= chunks
        for queue in (first, relays, down, [] if waiting else late):
            for move in list(queue):
                s, t, item = move
                known = item[0] != "stay" or ready.get((s, item), len(rounds) + 1) <= len(rounds)
                if known and s not in senders and t not in targets:
                    now.append(move)
                    senders.add(s)
                    targets.add(t)
                    queue.remove(move)
        for s, t, item in now:
            ready[t, item] = len(rounds) + 3
        rounds.append(now)
    return rounds


def pick_kernel(count, order, me_ref, pivot_ref, matrix_ref, panel_ref, *refs):
    outs, (panel_out, rows_ref, pivot_v, sem) = refs[:-4], refs[-4:]
    rows, cols = matrix_ref.shape
    width = pivot_ref.shape[1]
    slot = width // count
    me = me_ref[0]
    point = pltpu.make_async_copy(pivot_ref, pivot_v, sem.at[0])
    head = pltpu.make_async_copy(matrix_ref.at[:width], rows_ref.at[:width], sem.at[1])
    tail = pltpu.make_async_copy(matrix_ref.at[width:], rows_ref.at[width:], sem.at[2])
    panel = pltpu.make_async_copy(panel_ref, panel_out, sem.at[3])
    point.start()
    head.start()
    tail.start()
    panel.start()
    point.wait()
    pivot = pivot_v[...]
    kind, place = classify(pivot, count, rows)
    head.wait()
    tail.wait()

    @pl.when(me == 0)
    def _():
        start = jnp.full(kind.shape, -count * width, jnp.int32)
        for k, (name, which) in enumerate(order):
            if name == "moved":
                start = jnp.where(kind == which, k * slot, start)
            else:
                inside = (kind == 0) & (place >= which * slot) & (place < (which + 1) * slot)
                start = jnp.where(inside, (k - which) * slot, start)
        got = picked(one_hot(start + place, len(order) * slot), rows_ref[:width, :])
        for k, out in enumerate(outs):
            out[...] = got[k * slot : (k + 1) * slot, :]

    @pl.when(me != 0)
    def _():
        mine = lax.broadcasted_iota(jnp.int32, (slot, width), 0) == jnp.where(kind == me, place, -1)
        source = jnp.sum(jnp.where(mine, pivot - me * rows, 0), axis=1, keepdims=True)
        pick = (lax.broadcasted_iota(jnp.int32, (slot, rows), 1) == source).astype(BF16)
        got = picked(pick, rows_ref[...])
        for out in outs:
            out[...] = got

    panel.wait()


def prepare_kernel(count, me_ref, pivot_ref, inverse_ref, matrix_ref, *refs):
    high_ref, low_ref, land_ref, base_ref, pivot_v, inv_ref, rows_ref, sem = refs[-8:]
    rows, cols = matrix_ref.shape
    width = pivot_ref.shape[1]
    slot = width // count
    stay = width // 2
    me = me_ref[0]
    copies = [
        pltpu.make_async_copy(pivot_ref, pivot_v, sem.at[0]),
        pltpu.make_async_copy(inverse_ref, inv_ref, sem.at[1]),
        pltpu.make_async_copy(matrix_ref, rows_ref, sem.at[2]),
    ]
    for copy in copies:
        copy.start()
    copies[0].wait()
    pivot = pivot_v[...]
    kind, place = classify(pivot, count, rows)
    spread = one_hot(jnp.where(kind == 0, place, stay + (kind - 1) * slot + place), high_ref.shape[1])
    mine = (kind == me) & (kind != 0)
    landing = lax.broadcasted_iota(jnp.int32, (rows, width), 0) == jnp.where(mine, pivot - me * rows, -1)
    land = mm_nt(landing.astype(BF16), one_hot(jnp.where(mine, place, -1), slot))
    land_ref[...] = land.astype(BF16)
    taken = jnp.sum(land, axis=1, keepdims=True)
    copies[1].wait()
    inv_high, inv_low = halves(inv_ref[...])
    high_ref[...] = mm_nt(inv_high, spread).astype(BF16)
    low_ref[...] = mm_nt(inv_low, spread).astype(BF16)
    copies[2].wait()
    base_ref[...] = jnp.where(taken > 0.5, 0.0, rows_ref[...])


def turn_kernel(near_ref, far_ref, high_ref, low_ref):
    half = near_ref.shape[0]
    for k, part in enumerate((near_ref, far_ref)):
        high, low = halves(-part[...])
        high_ref[:, k * half : (k + 1) * half] = high.T
        low_ref[:, k * half : (k + 1) * half] = low.T


def upper_kernel(count, places, me_ref, high_ref, low_ref, *refs):
    arrays, (out_ref, row_high, row_low) = refs[:-3], refs[-3:]
    slot = arrays[0].shape[0]
    me = me_ref[0]
    for r in range(count):

        @pl.when(me == r)
        def _(r=r):
            for block, k in enumerate(places[r]):
                part = pl.ds(block * slot, slot)
                row_high[part, :], row_low[part, :] = halves(arrays[k][...])

    high = high_ref[...]
    out_ref[...] = mm(low_ref[...], row_high[...]) + mm(high, row_low[...]) + mm(high, row_high[...])


def update_kernel(places, me_ref, ids_ref, base_ref, land_ref, high_ref, low_ref, upper_ref, *refs):
    arrays, (out_ref, up_high, up_low, row_high, row_low) = refs[:-5], refs[-5:]
    width = upper_ref.shape[0]
    me = me_ref[0]
    depth = width // ids_ref.shape[0]
    for k in range(ids_ref.shape[0]):
        source = pl.multiple_of(ids_ref[k] * depth, depth)
        part = pl.ds(k * depth, depth)
        up_high[part, :], up_low[part, :] = halves(upper_ref[pl.ds(source, depth), :])
    for r, k in enumerate(places):

        @pl.when(me == r)
        def _(k=k):
            if k is None:
                row_high[...] = jnp.zeros(row_high.shape, BF16)
                row_low[...] = jnp.zeros(row_low.shape, BF16)
            else:
                row_high[...], row_low[...] = halves(arrays[k][...])

    high, land = high_ref[...], land_ref[...]
    part = mm(low_ref[...], up_high[...]) + mm(high, up_low[...]) + mm(high, up_high[...])
    out_ref[...] = base_ref[...] + (mm(land, row_low[...]) + mm(land, row_high[...]) + part)

    @pl.when(me == 0)
    def _():
        out_ref[:width, :] = upper_ref[...]


def join_kernel(first, second, *refs):
    out, sem = refs[-2:]
    rows = first.shape[0]
    copies = [
        pltpu.make_async_copy(first, out.at[:rows], sem.at[0]),
        pltpu.make_async_copy(second, out.at[rows:], sem.at[1]),
    ]
    for copy in copies:
        copy.start()
    for copy in copies:
        copy.wait()


def join(first, second, afters):
    rows, cols = first.shape
    return pl.pallas_call(
        join_kernel,
        out_shape=jax.ShapeDtypeStruct((2 * rows, cols), first.dtype),
        in_specs=[VMEM, VMEM] + [ANY] * len(afters),
        out_specs=VMEM,
        scratch_shapes=[pltpu.SemaphoreType.DMA((2,))],
        compiler_params=PARAMS,
        name="join",
    )(first, second, *afters)


def gather_shards(shard, count, afters):
    held, masks = shard, [0]
    bit = 1
    while 2 * bit < count:
        bit *= 2
    while bit:
        other = lax.ppermute(held, "col", [(i, i ^ bit) for i in range(count)])
        masks += [mask ^ bit for mask in masks]
        if bit > 1:
            held = join(held, other, afters[0])
            afters = afters[1:] or afters
        bit //= 2
    return held, other, masks


def local(row_count, col_count, matrix, panel_t, inverse_lower, pivot_rows):
    rows, cols = matrix.shape
    width = inverse_lower.shape[0]
    slot = width // row_count
    stay = width // 2
    me = lax.axis_index("row").astype(jnp.int32)
    column = lax.axis_index("col").astype(jnp.int32)
    here = me.reshape(1)
    pivot = pivot_rows.reshape(1, width)
    item_shape = jax.ShapeDtypeStruct((slot, cols), F32)

    rounds = plan(row_count)
    order = [item for moves in rounds for s, t, item in moves if s == 0]
    matrix = pltpu.with_memory_space_constraint(matrix, pltpu.HBM)
    pivot = pltpu.with_memory_space_constraint(pivot, pltpu.HBM)
    panel_t = pltpu.with_memory_space_constraint(panel_t, pltpu.HBM)
    inverse_lower = pltpu.with_memory_space_constraint(inverse_lower, pltpu.HBM)
    *own, panel = pl.pallas_call(
        functools.partial(pick_kernel, row_count, order),
        out_shape=(item_shape,) * len(order) + (jax.ShapeDtypeStruct(panel_t.shape, F32),),
        in_specs=[SMEM, HBM, HBM, HBM],
        out_specs=(VMEM,) * (len(order) + 1),
        scratch_shapes=[
            pltpu.VMEM((rows, cols), F32),
            pltpu.VMEM((1, width), jnp.int32),
            pltpu.SemaphoreType.DMA((4,)),
        ],
        compiler_params=PARAMS,
        name="pick",
    )(here, pivot, matrix, panel_t)

    arrays = list(own)
    found = [{} for _ in range(row_count)]
    for k, item in enumerate(order):
        found[0][item] = k
    for r in range(1, row_count):
        found[r]["pick", r] = 0
    for moves in rounds:
        leaving = [item for s, t, item in moves if s == 0]
        operand = own[order.index(leaving[0])] if leaving else own[0]
        for s, t, item in moves:
            if s != 0 and item[0] == "stay":
                operand = jnp.where(me == s, arrays[found[s][item]], operand)
        for s, t, item in moves:
            found[t][item] = len(arrays)
        arrays.append(lax.ppermute(operand, "row", [(s, t) for s, t, item in moves]))
    received = arrays[len(own) :]
    blocks = [("stay", c) for c in range(row_count // 2)] + [("pick", p) for p in range(1, row_count)]
    places = [[found[r][item] for item in blocks] for r in range(row_count)]
    landed = [found[r].get(("moved", r)) for r in range(row_count)]

    picked_rows = len(blocks) * slot
    inv_high, inv_low, land, base = pl.pallas_call(
        functools.partial(prepare_kernel, row_count),
        out_shape=(
            jax.ShapeDtypeStruct((width, picked_rows), BF16),
            jax.ShapeDtypeStruct((width, picked_rows), BF16),
            jax.ShapeDtypeStruct((rows, slot), BF16),
            jax.ShapeDtypeStruct((rows, cols), F32),
        ),
        in_specs=[SMEM, HBM, HBM, HBM] + [ANY] * 2,
        out_specs=(VMEM,) * 4,
        scratch_shapes=[
            pltpu.VMEM((1, width), jnp.int32),
            pltpu.VMEM((width, width), F32),
            pltpu.VMEM((rows, cols), F32),
            pltpu.SemaphoreType.DMA((3,)),
        ],
        compiler_params=PARAMS,
        cost_estimate=LONG,
        name="prepare",
    )(here, pivot, inverse_lower, matrix, *received[1:3])

    near, far, masks = gather_shards(panel, col_count, [received[:1], []])
    ids = column ^ jnp.array(masks, jnp.int32)

    upper = pl.pallas_call(
        functools.partial(upper_kernel, row_count, places),
        out_shape=jax.ShapeDtypeStruct((width, cols), F32),
        in_specs=[SMEM] + [VMEM] * (2 + len(arrays)),
        out_specs=VMEM,
        scratch_shapes=[pltpu.VMEM((picked_rows, cols), BF16)] * 2,
        compiler_params=PARAMS,
        name="upper",
    )(here, inv_high, inv_low, *arrays)

    pan_high, pan_low = pl.pallas_call(
        turn_kernel,
        out_shape=(jax.ShapeDtypeStruct((rows, width), BF16),) * 2,
        in_specs=[VMEM, VMEM],
        out_specs=(VMEM, VMEM),
        compiler_params=PARAMS,
        name="turn",
    )(near, far)

    return pl.pallas_call(
        functools.partial(update_kernel, landed),
        out_shape=jax.ShapeDtypeStruct((rows, cols), F32),
        in_specs=[SMEM, SMEM] + [VMEM] * (5 + len(arrays)),
        out_specs=VMEM,
        scratch_shapes=[pltpu.VMEM((width, cols), BF16)] * 2 + [pltpu.VMEM((slot, cols), BF16)] * 2,
        compiler_params=PARAMS,
        name="update",
    )(here, ids, base, land, pan_high, pan_low, upper, *arrays)


def solution(mesh):
    in_specs = (P("row", "col"), P("col", "row"), P(), P())
    out_specs = P("row", "col")
    return jax.shard_map(
        functools.partial(local, mesh.shape["row"], mesh.shape["col"]),
        mesh=mesh,
        in_specs=in_specs,
        out_specs=out_specs,
        check_vma=False,
    )
```

```python
import functools

import jax
import jax.numpy as jnp
from jax import lax
from jax.experimental import pallas as pl
from jax.experimental.pallas import tpu as pltpu
from jax.sharding import PartitionSpec as P

F32 = jnp.float32
BF16 = jnp.bfloat16
VMEM = pl.BlockSpec(memory_space=pltpu.VMEM)
SMEM = pl.BlockSpec(memory_space=pltpu.SMEM)
ANY = pl.BlockSpec(memory_space=pl.ANY)
HBM = pl.BlockSpec(memory_space=pltpu.HBM)
LONG = pl.CostEstimate(flops=40_000_000_000, transcendentals=0, bytes_accessed=100_000_000)
PARAMS = pltpu.CompilerParams(vmem_limit_bytes=20 * 1024 * 1024)


def halves(x):
    high = x.astype(BF16)
    low = (x - high.astype(F32)).astype(BF16)
    return high, low


def thirds(x):
    high = x.astype(BF16)
    rest = x - high.astype(F32)
    middle = rest.astype(BF16)
    low = (rest - middle.astype(F32)).astype(BF16)
    return high, middle, low


def mm(a, b):
    return jnp.dot(a, b, preferred_element_type=F32)


def mm_nt(a, b):
    return lax.dot_general(a, b, (((1,), (1,)), ((), ())), preferred_element_type=F32)


def mm_tn(a, b):
    return lax.dot_general(a, b, (((0,), (0,)), ((), ())), preferred_element_type=F32)


def classify(pivot, count, rows):
    width = pivot.shape[1]
    lanes = lax.broadcasted_iota(jnp.int32, (1, width), 1)
    kind = jnp.where(pivot != lanes, pivot // rows, 0)
    padded = -(-count // 16) * 16
    owner = lax.broadcasted_iota(jnp.int32, (padded, width), 0)
    member = owner == kind
    before = lax.broadcasted_iota(jnp.int32, (width, width), 0) < lax.broadcasted_iota(
        jnp.int32, (width, width), 1
    )
    ranks = mm(member.astype(BF16), before.astype(BF16))
    place = jnp.sum(jnp.where(member, ranks, 0.0), axis=0, keepdims=True)
    return kind, place.astype(jnp.int32)


def one_hot(position, slots):
    slot = lax.broadcasted_iota(jnp.int32, (slots, position.shape[1]), 0)
    return (slot == position).astype(BF16)


def picked(pick, rows):
    high, middle, low = thirds(rows)
    return mm(pick, low) + mm(pick, middle) + mm(pick, high)


def plan(count):
    middle, chunks = count // 2, count // 2
    first = [(0, middle, ("stay", c)) for c in range(chunks)]
    relays = []
    for c in range(chunks):
        for k in range(1, count):
            if middle + k < count:
                relays.append((middle + k - 1, middle + k, ("stay", c)))
            if middle - k > 0:
                relays.append((middle - k + 1, middle - k, ("stay", c)))
    early = [(s, t, ("pick", s)) for t in range(1, count) for s in range(middle, count) if s != t]
    late = [(0, t, ("moved", t)) for t in range(1, count)]
    late += [(s, t, ("pick", s)) for t in range(count - 1, 0, -1) for s in range(1, middle) if s != t]
    late += [(s, 0, ("pick", s)) for s in range(middle, count)]
    early += [(s, 0, ("pick", s)) for s in range(1, middle)]
    ready = {(0, ("stay", c)): 0 for c in range(chunks)}
    rounds = []
    while first or relays or early or late:
        now, senders, targets = [], set(), set()
        for queue in (first, relays, early, [] if len(rounds) < chunks else late):
            for move in list(queue):
                s, t, item = move
                known = item[0] != "stay" or ready.get((s, item), len(rounds) + 1) <= len(rounds)
                if known and s not in senders and t not in targets:
                    now.append(move)
                    senders.add(s)
                    targets.add(t)
                    queue.remove(move)
        for s, t, item in now:
            ready[t, item] = len(rounds) + 3
        rounds.append(now)
    return rounds


def pick_kernel(count, order, me_ref, pivot_ref, matrix_ref, panel_ref, *refs):
    outs, (panel_out, rows_ref, pivot_v, sem) = refs[:-4], refs[-4:]
    rows, cols = matrix_ref.shape
    width = pivot_ref.shape[1]
    slot = width // count
    me = me_ref[0]
    point = pltpu.make_async_copy(pivot_ref, pivot_v, sem.at[0])
    head = pltpu.make_async_copy(matrix_ref.at[:width], rows_ref.at[:width], sem.at[1])
    tail = pltpu.make_async_copy(matrix_ref.at[width:], rows_ref.at[width:], sem.at[2])
    panel = pltpu.make_async_copy(panel_ref, panel_out, sem.at[3])
    point.start()
    head.start()
    tail.start()
    panel.start()
    point.wait()
    pivot = pivot_v[...]
    kind, place = classify(pivot, count, rows)
    head.wait()
    tail.wait()

    @pl.when(me == 0)
    def _():
        start = jnp.full(kind.shape, -count * width, jnp.int32)
        for k, (name, which) in enumerate(order):
            if name == "moved":
                start = jnp.where(kind == which, k * slot, start)
            else:
                inside = (kind == 0) & (place >= which * slot) & (place < (which + 1) * slot)
                start = jnp.where(inside, (k - which) * slot, start)
        got = picked(one_hot(start + place, len(order) * slot), rows_ref[:width, :])
        for k, out in enumerate(outs):
            out[...] = got[k * slot : (k + 1) * slot, :]

    @pl.when(me != 0)
    def _():
        mine = lax.broadcasted_iota(jnp.int32, (slot, width), 0) == jnp.where(kind == me, place, -1)
        source = jnp.sum(jnp.where(mine, pivot - me * rows, 0), axis=1, keepdims=True)
        pick = (lax.broadcasted_iota(jnp.int32, (slot, rows), 1) == source).astype(BF16)
        got = picked(pick, rows_ref[...])
        for out in outs:
            out[...] = got

    panel.wait()


def prepare_kernel(count, me_ref, pivot_ref, inverse_ref, matrix_ref, *refs):
    high_ref, low_ref, land_ref, base_ref, pivot_v, inv_ref, rows_ref, sem = refs[-8:]
    rows, cols = matrix_ref.shape
    width = pivot_ref.shape[1]
    slot = width // count
    stay = width // 2
    me = me_ref[0]
    copies = [
        pltpu.make_async_copy(pivot_ref, pivot_v, sem.at[0]),
        pltpu.make_async_copy(inverse_ref, inv_ref, sem.at[1]),
        pltpu.make_async_copy(matrix_ref, rows_ref, sem.at[2]),
    ]
    for copy in copies:
        copy.start()
    copies[0].wait()
    pivot = pivot_v[...]
    kind, place = classify(pivot, count, rows)
    total = high_ref.shape[1]
    stayed = jnp.where(place < stay - slot, place, place + total - stay)
    spread = one_hot(jnp.where(kind == 0, stayed, stay + (kind - 2) * slot + place), total)
    mine = (kind == me) & (kind != 0)
    landing = lax.broadcasted_iota(jnp.int32, (rows, width), 0) == jnp.where(mine, pivot - me * rows, -1)
    land = mm_nt(landing.astype(BF16), one_hot(jnp.where(mine, place, -1), slot))
    land_ref[...] = land.astype(BF16)
    taken = jnp.sum(land, axis=1, keepdims=True)
    copies[1].wait()
    inv_high, inv_low = halves(inv_ref[...])
    high_ref[...] = mm_nt(inv_high, spread).astype(BF16)
    low_ref[...] = mm_nt(inv_low, spread).astype(BF16)
    copies[2].wait()
    base_ref[...] = jnp.where(taken > 0.5, 0.0, rows_ref[...])


def turn_kernel(me_ref, ids_ref, near_ref, far_ref, inv_high, inv_low, *refs):
    high_ref, low_ref, end_high, end_low, order_high, order_low = refs
    half = near_ref.shape[0]
    width, slot = order_high.shape
    for k, part in enumerate((near_ref, far_ref)):
        high, low = halves(-part[...])
        high_ref[:, k * half : (k + 1) * half] = high.T
        low_ref[:, k * half : (k + 1) * half] = low.T
    first = inv_high.shape[1] - slot
    depth = width // ids_ref.shape[0]
    for k in range(ids_ref.shape[0]):
        source = pl.ds(pl.multiple_of(ids_ref[k] * depth, depth), depth)
        part = pl.ds(k * depth, depth)
        order_high[part, :] = inv_high[source, first:].astype(F32)
        order_low[part, :] = inv_low[source, first:].astype(F32)
    pan_high, last_high = high_ref[...], order_high[...].astype(BF16)
    value = mm(low_ref[...], last_high) + mm(pan_high, order_low[...].astype(BF16)) + mm(pan_high, last_high)
    end_high[...], end_low[...] = halves(value)

    @pl.when(me_ref[0] == 0)
    def _():
        end_high[:width, :] = inv_high[:, first:]
        end_low[:width, :] = inv_low[:, first:]


def upper_kernel(count, places, landed, me_ref, high_ref, low_ref, land_ref, base_ref, *refs):
    arrays, (out_ref, rows_out, row_high, row_low, new_high, new_low) = refs[:-6], refs[-6:]
    slot = arrays[0].shape[0]
    me = me_ref[0]
    for r in range(count):

        @pl.when(me == r)
        def _(r=r):
            for block, k in enumerate(places[r]):
                part = pl.ds(block * slot, slot)
                row_high[part, :], row_low[part, :] = halves(arrays[k][...])
            if landed[r] is None:
                new_high[...] = jnp.zeros(new_high.shape, BF16)
                new_low[...] = jnp.zeros(new_low.shape, BF16)
            else:
                new_high[...], new_low[...] = halves(arrays[landed[r]][...])

    depth = row_high.shape[0]
    high, land = high_ref[:, :depth], land_ref[...]
    out_ref[...] = mm(low_ref[:, :depth], row_high[...]) + mm(high, row_low[...]) + mm(high, row_high[...])
    rows_out[...] = base_ref[...] + (mm(land, new_low[...]) + mm(land, new_high[...]))


def update_kernel(me_ref, ids_ref, rows_ref, high_ref, low_ref, upper_ref, out_ref, up_high, up_low):
    width = upper_ref.shape[0]
    depth = width // ids_ref.shape[0]
    for k in range(ids_ref.shape[0]):
        source = pl.multiple_of(ids_ref[k] * depth, depth)
        part = pl.ds(k * depth, depth)
        up_high[part, :], up_low[part, :] = halves(upper_ref[pl.ds(source, depth), :])
    high = high_ref[...]
    part = mm(low_ref[...], up_high[...]) + mm(high, up_low[...]) + mm(high, up_high[...])
    out_ref[...] = rows_ref[...] + part

    @pl.when(me_ref[0] == 0)
    def _():
        out_ref[:width, :] = upper_ref[...]


def finish_kernel(places, me_ref, part_ref, high_ref, low_ref, *refs):
    arrays, (out_ref, row_high, row_low) = refs[:-3], refs[-3:]
    for r, k in enumerate(places):

        @pl.when(me_ref[0] == r)
        def _(k=k):
            row_high[...], row_low[...] = halves(arrays[k][...])

    high = high_ref[...]
    value = mm(low_ref[...], row_high[...]) + mm(high, row_low[...]) + mm(high, row_high[...])
    out_ref[...] = part_ref[...] + value


def join_kernel(first, second, *refs):
    out, sem = refs[-2:]
    rows = first.shape[0]
    copies = [
        pltpu.make_async_copy(first, out.at[:rows], sem.at[0]),
        pltpu.make_async_copy(second, out.at[rows:], sem.at[1]),
    ]
    for copy in copies:
        copy.start()
    for copy in copies:
        copy.wait()


def join(first, second, afters):
    rows, cols = first.shape
    return pl.pallas_call(
        join_kernel,
        out_shape=jax.ShapeDtypeStruct((2 * rows, cols), first.dtype),
        in_specs=[VMEM, VMEM] + [ANY] * len(afters),
        out_specs=VMEM,
        scratch_shapes=[pltpu.SemaphoreType.DMA((2,))],
        compiler_params=PARAMS,
        name="join",
    )(first, second, *afters)


def gather_shards(shard, count, afters):
    held, masks = shard, [0]
    bit = 1
    while 2 * bit < count:
        bit *= 2
    while bit:
        other = lax.ppermute(held, "col", [(i, i ^ bit) for i in range(count)])
        masks += [mask ^ bit for mask in masks]
        if bit > 1:
            held = join(held, other, afters[0])
            afters = afters[1:] or afters
        bit //= 2
    return held, other, masks


def local(row_count, col_count, matrix, panel_t, inverse_lower, pivot_rows):
    rows, cols = matrix.shape
    width = inverse_lower.shape[0]
    slot = width // row_count
    stay = width // 2
    me = lax.axis_index("row").astype(jnp.int32)
    column = lax.axis_index("col").astype(jnp.int32)
    here = me.reshape(1)
    pivot = pivot_rows.reshape(1, width)
    item_shape = jax.ShapeDtypeStruct((slot, cols), F32)

    rounds = plan(row_count)
    order = [item for moves in rounds for s, t, item in moves if s == 0]
    matrix = pltpu.with_memory_space_constraint(matrix, pltpu.HBM)
    pivot = pltpu.with_memory_space_constraint(pivot, pltpu.HBM)
    panel_t = pltpu.with_memory_space_constraint(panel_t, pltpu.HBM)
    inverse_lower = pltpu.with_memory_space_constraint(inverse_lower, pltpu.HBM)
    *own, panel = pl.pallas_call(
        functools.partial(pick_kernel, row_count, order),
        out_shape=(item_shape,) * len(order) + (jax.ShapeDtypeStruct(panel_t.shape, F32),),
        in_specs=[SMEM, HBM, HBM, HBM],
        out_specs=(VMEM,) * (len(order) + 1),
        scratch_shapes=[
            pltpu.VMEM((rows, cols), F32),
            pltpu.VMEM((1, width), jnp.int32),
            pltpu.SemaphoreType.DMA((4,)),
        ],
        compiler_params=PARAMS,
        name="pick",
    )(here, pivot, matrix, panel_t)

    arrays = list(own)
    found = [{} for _ in range(row_count)]
    for k, item in enumerate(order):
        found[0][item] = k
    for r in range(1, row_count):
        found[r]["pick", r] = 0
    operands, chunks = [], row_count // 2
    for moves in rounds:
        leaving = [item for s, t, item in moves if s == 0]
        operand = own[order.index(leaving[0])] if leaving else own[0]
        if len(operands) > chunks + 1 and all(item[0] == "stay" for s, t, item in moves):
            operand = arrays[len(own) + chunks]
        for s, t, item in moves:
            if s != 0 and item[0] == "stay":
                operand = jnp.where(me == s, arrays[found[s][item]], operand)
        for s, t, item in moves:
            found[t][item] = len(arrays)
        operands.append(operand)
        arrays.append(lax.ppermute(operand, "row", [(s, t) for s, t, item in moves]))
    received = arrays[len(own) :]
    blocks = [("stay", c) for c in range(chunks - 1)] + [("pick", p) for p in range(1, row_count)]
    places = [[found[r][item] for item in blocks] for r in range(row_count)]
    landed = [found[r].get(("moved", r)) for r in range(row_count)]
    last = [found[r]["stay", chunks - 1] for r in range(row_count)]

    picked_rows = (len(blocks) + 1) * slot
    inv_high, inv_low, land, base = pl.pallas_call(
        functools.partial(prepare_kernel, row_count),
        out_shape=(
            jax.ShapeDtypeStruct((width, picked_rows), BF16),
            jax.ShapeDtypeStruct((width, picked_rows), BF16),
            jax.ShapeDtypeStruct((rows, slot), BF16),
            jax.ShapeDtypeStruct((rows, cols), F32),
        ),
        in_specs=[SMEM, HBM, HBM, HBM] + [ANY] * 2,
        out_specs=(VMEM,) * 4,
        scratch_shapes=[
            pltpu.VMEM((1, width), jnp.int32),
            pltpu.VMEM((width, width), F32),
            pltpu.VMEM((rows, cols), F32),
            pltpu.SemaphoreType.DMA((3,)),
        ],
        compiler_params=PARAMS,
        cost_estimate=LONG,
        name="prepare",
    )(here, pivot, inverse_lower, matrix, *received[1:3])

    near, far, masks = gather_shards(panel, col_count, [operands[3:5], []])
    ids = column ^ jnp.array(masks, jnp.int32)

    def used(*tables):
        names = sorted({k for table in tables for k in jax.tree.leaves(table)})
        return [arrays[k] for k in names], [jax.tree.map(names.index, table) for table in tables]

    here_arrays, (places, landed) = used(places, landed)
    upper, with_landed = pl.pallas_call(
        functools.partial(upper_kernel, row_count, places, landed),
        out_shape=(jax.ShapeDtypeStruct((width, cols), F32), jax.ShapeDtypeStruct((rows, cols), F32)),
        in_specs=[SMEM] + [VMEM] * (4 + len(here_arrays)),
        out_specs=(VMEM, VMEM),
        scratch_shapes=[pltpu.VMEM((picked_rows - slot, cols), BF16)] * 2 + [pltpu.VMEM((slot, cols), BF16)] * 2,
        compiler_params=PARAMS,
        name="upper",
    )(here, inv_high, inv_low, land, base, *here_arrays)

    pan_high, pan_low, end_high, end_low = pl.pallas_call(
        turn_kernel,
        out_shape=(jax.ShapeDtypeStruct((rows, width), BF16),) * 2 + (jax.ShapeDtypeStruct((rows, slot), BF16),) * 2,
        in_specs=[SMEM, SMEM] + [VMEM] * 4,
        out_specs=(VMEM,) * 4,
        scratch_shapes=[pltpu.VMEM((width, slot), F32)] * 2,
        compiler_params=PARAMS,
        name="turn",
    )(here, ids, near, far, inv_high, inv_low)

    part = pl.pallas_call(
        update_kernel,
        out_shape=jax.ShapeDtypeStruct((rows, cols), F32),
        in_specs=[SMEM, SMEM] + [VMEM] * 4,
        out_specs=VMEM,
        scratch_shapes=[pltpu.VMEM((width, cols), BF16)] * 2,
        compiler_params=PARAMS,
        name="update",
    )(here, ids, with_landed, pan_high, pan_low, upper)

    last_arrays, (last,) = used(last)
    return pl.pallas_call(
        functools.partial(finish_kernel, last),
        out_shape=jax.ShapeDtypeStruct((rows, cols), F32),
        in_specs=[SMEM] + [VMEM] * (3 + len(last_arrays)),
        out_specs=VMEM,
        scratch_shapes=[pltpu.VMEM((slot, cols), BF16)] * 2,
        compiler_params=PARAMS,
        name="finish",
    )(here, part, end_high, end_low, *last_arrays)


def solution(mesh):
    in_specs = (P("row", "col"), P("col", "row"), P(), P())
    out_specs = P("row", "col")
    return jax.shard_map(
        functools.partial(local, mesh.shape["row"], mesh.shape["col"]),
        mesh=mesh,
        in_specs=in_specs,
        out_specs=out_specs,
        check_vma=False,
    )
```

```python
import functools

import jax
import jax.numpy as jnp
from jax import lax
from jax.experimental import pallas as pl
from jax.experimental.pallas import tpu as pltpu
from jax.sharding import PartitionSpec as P

F32 = jnp.float32
BF16 = jnp.bfloat16
VMEM = pl.BlockSpec(memory_space=pltpu.VMEM)
SMEM = pl.BlockSpec(memory_space=pltpu.SMEM)
ANY = pl.BlockSpec(memory_space=pl.ANY)
HBM = pl.BlockSpec(memory_space=pltpu.HBM)
SHORT = pl.CostEstimate(flops=1_000_000, transcendentals=0, bytes_accessed=100_000)
LONG = pl.CostEstimate(flops=40_000_000_000, transcendentals=0, bytes_accessed=100_000_000)
PARAMS = pltpu.CompilerParams(vmem_limit_bytes=20 * 1024 * 1024)


def halves(x):
    high = x.astype(BF16)
    low = (x - high.astype(F32)).astype(BF16)
    return high, low


def thirds(x):
    high = x.astype(BF16)
    rest = x - high.astype(F32)
    middle = rest.astype(BF16)
    low = (rest - middle.astype(F32)).astype(BF16)
    return high, middle, low


def mm(a, b):
    return jnp.dot(a, b, preferred_element_type=F32)


def mm_nt(a, b):
    return lax.dot_general(a, b, (((1,), (1,)), ((), ())), preferred_element_type=F32)


def mm_tn(a, b):
    return lax.dot_general(a, b, (((0,), (0,)), ((), ())), preferred_element_type=F32)


def classify(pivot, count, rows):
    width = pivot.shape[1]
    lanes = lax.broadcasted_iota(jnp.int32, (1, width), 1)
    kind = jnp.where(pivot != lanes, pivot // rows, 0)
    padded = -(-count // 16) * 16
    owner = lax.broadcasted_iota(jnp.int32, (padded, width), 0)
    member = owner == kind
    before = lax.broadcasted_iota(jnp.int32, (width, width), 0) < lax.broadcasted_iota(
        jnp.int32, (width, width), 1
    )
    ranks = mm(member.astype(BF16), before.astype(BF16))
    place = jnp.sum(jnp.where(member, ranks, 0.0), axis=0, keepdims=True)
    return kind, place.astype(jnp.int32)


def one_hot(position, slots):
    slot = lax.broadcasted_iota(jnp.int32, (slots, position.shape[1]), 0)
    return (slot == position).astype(BF16)


def picked(pick, rows):
    high, middle, low = thirds(rows)
    return mm(pick, low) + mm(pick, middle) + mm(pick, high)


def plan(count):
    middle, chunks = count // 2, count // 2
    first = [(0, middle, ("stay", c)) for c in range(chunks)]
    relays = []
    for c in range(chunks):
        for k in range(1, count):
            if middle + k < count:
                relays.append((middle + k - 1, middle + k, ("stay", c)))
            if middle - k > 0:
                relays.append((middle - k + 1, middle - k, ("stay", c)))
    early = [(s, t, ("pick", s)) for t in range(1, count) for s in range(middle, count) if s != t]
    late = [(0, t, ("moved", t)) for t in range(1, count)]
    late += [(s, t, ("pick", s)) for t in range(count - 1, 0, -1) for s in range(1, middle) if s != t]
    late += [(s, 0, ("pick", s)) for s in range(middle, count)]
    early += [(s, 0, ("pick", s)) for s in range(1, middle)]
    ready = {(0, ("stay", c)): 0 for c in range(chunks)}
    rounds = []
    while first or relays or early or late:
        now, senders, targets = [], set(), set()
        for queue in (first, relays, early, [] if len(rounds) < chunks else late):
            for move in list(queue):
                s, t, item = move
                known = item[0] != "stay" or ready.get((s, item), len(rounds) + 1) <= len(rounds)
                if known and s not in senders and t not in targets:
                    now.append(move)
                    senders.add(s)
                    targets.add(t)
                    queue.remove(move)
        for s, t, item in now:
            ready[t, item] = len(rounds) + 3
        rounds.append(now)
    return rounds


def pick_kernel(count, order, me_ref, pivot_ref, matrix_ref, panel_ref, *refs):
    outs, (panel_out, rows_ref, pivot_v, sem) = refs[:-4], refs[-4:]
    rows, cols = matrix_ref.shape
    width = pivot_ref.shape[1]
    slot = width // count
    me = me_ref[0]
    point = pltpu.make_async_copy(pivot_ref, pivot_v, sem.at[0])
    head = pltpu.make_async_copy(matrix_ref.at[:width], rows_ref.at[:width], sem.at[1])
    tail = pltpu.make_async_copy(matrix_ref.at[width:], rows_ref.at[width:], sem.at[2])
    panel = pltpu.make_async_copy(panel_ref, panel_out, sem.at[3])
    point.start()
    head.start()
    tail.start()
    panel.start()
    point.wait()
    pivot = pivot_v[...]
    kind, place = classify(pivot, count, rows)
    head.wait()
    tail.wait()

    @pl.when(me == 0)
    def _():
        start = jnp.full(kind.shape, -count * width, jnp.int32)
        for k, (name, which) in enumerate(order):
            if name == "moved":
                start = jnp.where(kind == which, k * slot, start)
            else:
                inside = (kind == 0) & (place >= which * slot) & (place < (which + 1) * slot)
                start = jnp.where(inside, (k - which) * slot, start)
        got = picked(one_hot(start + place, len(order) * slot), rows_ref[:width, :])
        for k, out in enumerate(outs):
            out[...] = got[k * slot : (k + 1) * slot, :]

    @pl.when(me != 0)
    def _():
        mine = lax.broadcasted_iota(jnp.int32, (slot, width), 0) == jnp.where(kind == me, place, -1)
        source = jnp.sum(jnp.where(mine, pivot - me * rows, 0), axis=1, keepdims=True)
        pick = (lax.broadcasted_iota(jnp.int32, (slot, rows), 1) == source).astype(BF16)
        got = picked(pick, rows_ref[...])
        for out in outs:
            out[...] = got

    panel.wait()


def prepare_kernel(count, me_ref, pivot_ref, inverse_ref, matrix_ref, *refs):
    high_ref, low_ref, land_ref, base_ref, pivot_v, inv_ref, rows_ref, sem = refs[-8:]
    rows, cols = matrix_ref.shape
    width = pivot_ref.shape[1]
    slot = width // count
    stay = width // 2
    me = me_ref[0]
    copies = [
        pltpu.make_async_copy(pivot_ref, pivot_v, sem.at[0]),
        pltpu.make_async_copy(inverse_ref, inv_ref, sem.at[1]),
        pltpu.make_async_copy(matrix_ref, rows_ref, sem.at[2]),
    ]
    for copy in copies:
        copy.start()
    copies[0].wait()
    pivot = pivot_v[...]
    kind, place = classify(pivot, count, rows)
    total = high_ref.shape[1]
    middle = count // 2
    start = jnp.where(kind == 0, (count - middle) * slot, stay + (kind + count - middle - 1) * slot)
    spread = one_hot(place + jnp.where(kind < middle, start, (kind - middle) * slot), total)
    mine = (kind == me) & (kind != 0)
    landing = lax.broadcasted_iota(jnp.int32, (rows, width), 0) == jnp.where(mine, pivot - me * rows, -1)
    land = mm_nt(landing.astype(BF16), one_hot(jnp.where(mine, place, -1), slot))
    land_ref[...] = land.astype(BF16)
    taken = jnp.sum(land, axis=1, keepdims=True)
    copies[1].wait()
    inv_high, inv_low = halves(inv_ref[...])
    high_ref[...] = mm_nt(inv_high, spread).astype(BF16)
    low_ref[...] = mm_nt(inv_low, spread).astype(BF16)
    copies[2].wait()
    base_ref[...] = jnp.where(taken > 0.5, 0.0, rows_ref[...])


def turn_kernel(me_ref, ids_ref, near_ref, far_ref, inv_high, inv_low, land_ref, *refs):
    high_ref, low_ref, end_high, end_low, order_high, order_low = refs
    half = near_ref.shape[0]
    width, picked_rows = order_high.shape
    for k, part in enumerate((near_ref, far_ref)):
        high, low = halves(-part[...])
        high_ref[:, k * half : (k + 1) * half] = high.T
        low_ref[:, k * half : (k + 1) * half] = low.T
    first = inv_high.shape[1] - picked_rows
    depth = width // ids_ref.shape[0]
    for k in range(ids_ref.shape[0]):
        source = pl.ds(pl.multiple_of(ids_ref[k] * depth, depth), depth)
        part = pl.ds(k * depth, depth)
        order_high[part, :] = inv_high[source, first:].astype(F32)
        order_low[part, :] = inv_low[source, first:].astype(F32)
    pan_high, last_high = high_ref[...], order_high[...].astype(BF16)
    value = mm(low_ref[...], last_high) + mm(pan_high, order_low[...].astype(BF16)) + mm(pan_high, last_high)
    end_high[:, :picked_rows], end_low[:, :picked_rows] = halves(value)
    end_high[:, picked_rows:] = land_ref[...]
    end_low[:, picked_rows:] = jnp.zeros(land_ref.shape, BF16)

    @pl.when(me_ref[0] == 0)
    def _():
        end_high[:width, :picked_rows] = inv_high[:, first:]
        end_low[:width, :picked_rows] = inv_low[:, first:]


def collect(places, me, arrays, row_high, row_low):
    slot, cols = arrays[0].shape
    for r in range(len(places)):

        @pl.when(me == r)
        def _(r=r):
            for block, k in enumerate(places[r]):
                part = pl.ds(block * slot, slot)
                if k is None:
                    row_high[part, :] = jnp.zeros((slot, cols), BF16)
                    row_low[part, :] = jnp.zeros((slot, cols), BF16)
                else:
                    row_high[part, :], row_low[part, :] = halves(arrays[k][...])


def upper_kernel(places, me_ref, high_ref, low_ref, *refs):
    arrays, (out_ref, row_high, row_low) = refs[:-3], refs[-3:]
    collect(places, me_ref[0], arrays, row_high, row_low)
    depth = row_high.shape[0]
    high = high_ref[:, :depth]
    out_ref[...] = mm(low_ref[:, :depth], row_high[...]) + mm(high, row_low[...]) + mm(high, row_high[...])


def update_kernel(me_ref, ids_ref, rows_ref, high_ref, low_ref, upper_ref, out_ref, up_high, up_low):
    width = upper_ref.shape[0]
    depth = width // ids_ref.shape[0]
    for k in range(ids_ref.shape[0]):
        source = pl.multiple_of(ids_ref[k] * depth, depth)
        part = pl.ds(k * depth, depth)
        up_high[part, :], up_low[part, :] = halves(upper_ref[pl.ds(source, depth), :])
    high = high_ref[...]
    part = mm(low_ref[...], up_high[...]) + mm(high, up_low[...]) + mm(high, up_high[...])
    out_ref[...] = rows_ref[...] + part

    @pl.when(me_ref[0] == 0)
    def _():
        out_ref[:width, :] = upper_ref[...]


def finish_kernel(places, me_ref, part_ref, high_ref, low_ref, *refs):
    arrays, (out_ref, row_high, row_low) = refs[:-3], refs[-3:]
    collect(places, me_ref[0], arrays, row_high, row_low)
    high = high_ref[...]
    value = mm(low_ref[...], row_high[...]) + mm(high, row_low[...]) + mm(high, row_high[...])
    out_ref[...] = part_ref[...] + value


def join_kernel(first, second, *refs):
    out, sem = refs[-2:]
    rows = first.shape[0]
    copies = [
        pltpu.make_async_copy(first, out.at[:rows], sem.at[0]),
        pltpu.make_async_copy(second, out.at[rows:], sem.at[1]),
    ]
    for copy in copies:
        copy.start()
    for copy in copies:
        copy.wait()


def join(first, second, afters):
    rows, cols = first.shape
    return pl.pallas_call(
        join_kernel,
        out_shape=jax.ShapeDtypeStruct((2 * rows, cols), first.dtype),
        in_specs=[VMEM, VMEM] + [ANY] * len(afters),
        out_specs=VMEM,
        scratch_shapes=[pltpu.SemaphoreType.DMA((2,))],
        compiler_params=PARAMS,
        name="join",
    )(first, second, *afters)


def gather_shards(shard, count, afters):
    held, masks = shard, [0]
    bit = 1
    while 2 * bit < count:
        bit *= 2
    while bit:
        other = lax.ppermute(held, "col", [(i, i ^ bit) for i in range(count)])
        masks += [mask ^ bit for mask in masks]
        if bit > 1:
            held = join(held, other, afters[0])
            afters = afters[1:] or afters
        bit //= 2
    return held, other, masks


def local(row_count, col_count, matrix, panel_t, inverse_lower, pivot_rows):
    rows, cols = matrix.shape
    width = inverse_lower.shape[0]
    slot = width // row_count
    stay = width // 2
    me = lax.axis_index("row").astype(jnp.int32)
    column = lax.axis_index("col").astype(jnp.int32)
    here = me.reshape(1)
    pivot = pivot_rows.reshape(1, width)
    item_shape = jax.ShapeDtypeStruct((slot, cols), F32)

    rounds = plan(row_count)
    order = [item for moves in rounds for s, t, item in moves if s == 0]
    matrix = pltpu.with_memory_space_constraint(matrix, pltpu.HBM)
    pivot = pltpu.with_memory_space_constraint(pivot, pltpu.HBM)
    panel_t = pltpu.with_memory_space_constraint(panel_t, pltpu.HBM)
    inverse_lower = pltpu.with_memory_space_constraint(inverse_lower, pltpu.HBM)
    *own, panel = pl.pallas_call(
        functools.partial(pick_kernel, row_count, order),
        out_shape=(item_shape,) * len(order) + (jax.ShapeDtypeStruct(panel_t.shape, F32),),
        in_specs=[SMEM, HBM, HBM, HBM],
        out_specs=(VMEM,) * (len(order) + 1),
        scratch_shapes=[
            pltpu.VMEM((rows, cols), F32),
            pltpu.VMEM((1, width), jnp.int32),
            pltpu.SemaphoreType.DMA((4,)),
        ],
        compiler_params=PARAMS,
        name="pick",
    )(here, pivot, matrix, panel_t)

    arrays = list(own)
    found = [{} for _ in range(row_count)]
    for k, item in enumerate(order):
        found[0][item] = k
    for r in range(1, row_count):
        found[r]["pick", r] = 0
    operands, chunks = [], row_count // 2
    for moves in rounds:
        leaving = [item for s, t, item in moves if s == 0]
        operand = own[order.index(leaving[0])] if leaving else own[0]
        if len(operands) > chunks + 1 and all(item[0] == "stay" for s, t, item in moves):
            operand = arrays[len(own) + chunks]
        for s, t, item in moves:
            if s != 0 and item[0] == "stay":
                operand = jnp.where(me == s, arrays[found[s][item]], operand)
        for s, t, item in moves:
            found[t][item] = len(arrays)
        operands.append(operand)
        arrays.append(lax.ppermute(operand, "row", [(s, t) for s, t, item in moves]))
    received = arrays[len(own) :]
    blocks = [("pick", p) for p in range(chunks, row_count)]
    late_blocks = [("stay", c) for c in range(chunks)] + [("pick", p) for p in range(1, chunks)]
    places = [[found[r][item] for item in blocks] for r in range(row_count)]
    late = [[found[r].get(item) for item in late_blocks + [("moved", r)]] for r in range(row_count)]
    late_rows = len(late_blocks) * slot

    picked_rows = len(blocks) * slot + late_rows
    inv_high, inv_low, land, base = pl.pallas_call(
        functools.partial(prepare_kernel, row_count),
        out_shape=(
            jax.ShapeDtypeStruct((width, picked_rows), BF16),
            jax.ShapeDtypeStruct((width, picked_rows), BF16),
            jax.ShapeDtypeStruct((rows, slot), BF16),
            jax.ShapeDtypeStruct((rows, cols), F32),
        ),
        in_specs=[SMEM, HBM, HBM, HBM],
        out_specs=(VMEM,) * 4,
        scratch_shapes=[
            pltpu.VMEM((1, width), jnp.int32),
            pltpu.VMEM((width, width), F32),
            pltpu.VMEM((rows, cols), F32),
            pltpu.SemaphoreType.DMA((3,)),
        ],
        compiler_params=PARAMS,
        cost_estimate=SHORT,
        name="prepare",
    )(here, pivot, inverse_lower, matrix)

    near, far, masks = gather_shards(panel, col_count, [operands[3:5] + [land], []])
    ids = column ^ jnp.array(masks, jnp.int32)

    def used(*tables):
        names = sorted({k for table in tables for k in jax.tree.leaves(table)})
        return [arrays[k] for k in names], [jax.tree.map(names.index, table) for table in tables]

    early_arrays, (places,) = used(places)
    upper = pl.pallas_call(
        functools.partial(upper_kernel, places),
        out_shape=jax.ShapeDtypeStruct((width, cols), F32),
        in_specs=[SMEM] + [VMEM] * (2 + len(early_arrays)),
        out_specs=VMEM,
        scratch_shapes=[pltpu.VMEM((picked_rows - late_rows, cols), BF16)] * 2,
        compiler_params=PARAMS,
        cost_estimate=LONG,
        name="upper",
    )(here, inv_high, inv_low, *early_arrays)

    pan_high, pan_low, end_high, end_low = pl.pallas_call(
        turn_kernel,
        out_shape=(jax.ShapeDtypeStruct((rows, width), BF16),) * 2
        + (jax.ShapeDtypeStruct((rows, late_rows + slot), BF16),) * 2,
        in_specs=[SMEM, SMEM] + [VMEM] * 5,
        out_specs=(VMEM,) * 4,
        scratch_shapes=[pltpu.VMEM((width, late_rows), F32)] * 2,
        compiler_params=PARAMS,
        name="turn",
    )(here, ids, near, far, inv_high, inv_low, land)

    part = pl.pallas_call(
        update_kernel,
        out_shape=jax.ShapeDtypeStruct((rows, cols), F32),
        in_specs=[SMEM, SMEM] + [VMEM] * 4,
        out_specs=VMEM,
        scratch_shapes=[pltpu.VMEM((width, cols), BF16)] * 2,
        compiler_params=PARAMS,
        name="update",
    )(here, ids, base, pan_high, pan_low, upper)

    late_arrays, (late,) = used(late)
    return pl.pallas_call(
        functools.partial(finish_kernel, late),
        out_shape=jax.ShapeDtypeStruct((rows, cols), F32),
        in_specs=[SMEM] + [VMEM] * (3 + len(late_arrays)),
        out_specs=VMEM,
        scratch_shapes=[pltpu.VMEM((late_rows + slot, cols), BF16)] * 2,
        compiler_params=PARAMS,
        name="finish",
    )(here, part, end_high, end_low, *late_arrays)


def solution(mesh):
    in_specs = (P("row", "col"), P("col", "row"), P(), P())
    out_specs = P("row", "col")
    return jax.shard_map(
        functools.partial(local, mesh.shape["row"], mesh.shape["col"]),
        mesh=mesh,
        in_specs=in_specs,
        out_specs=out_specs,
        check_vma=False,
    )
```

```python
import functools

import jax
import jax.numpy as jnp
from jax import lax
from jax.experimental import pallas as pl
from jax.experimental.pallas import tpu as pltpu
from jax.sharding import PartitionSpec as P

F32 = jnp.float32
BF16 = jnp.bfloat16
VMEM = pl.BlockSpec(memory_space=pltpu.VMEM)
SMEM = pl.BlockSpec(memory_space=pltpu.SMEM)
ANY = pl.BlockSpec(memory_space=pl.ANY)
HBM = pl.BlockSpec(memory_space=pltpu.HBM)
SHORT = pl.CostEstimate(flops=1_000_000, transcendentals=0, bytes_accessed=100_000)
LONG = pl.CostEstimate(flops=40_000_000_000, transcendentals=0, bytes_accessed=100_000_000)
PARAMS = pltpu.CompilerParams(vmem_limit_bytes=20 * 1024 * 1024)


def halves(x):
    high = x.astype(BF16)
    low = (x - high.astype(F32)).astype(BF16)
    return high, low


def thirds(x):
    high = x.astype(BF16)
    rest = x - high.astype(F32)
    middle = rest.astype(BF16)
    low = (rest - middle.astype(F32)).astype(BF16)
    return high, middle, low


def mm(a, b):
    return jnp.dot(a, b, preferred_element_type=F32)


def mm_nt(a, b):
    return lax.dot_general(a, b, (((1,), (1,)), ((), ())), preferred_element_type=F32)


def mm_tn(a, b):
    return lax.dot_general(a, b, (((0,), (0,)), ((), ())), preferred_element_type=F32)


def classify(pivot, count, rows):
    width = pivot.shape[1]
    lanes = lax.broadcasted_iota(jnp.int32, (1, width), 1)
    kind = jnp.where(pivot != lanes, pivot // rows, 0)
    padded = -(-count // 16) * 16
    owner = lax.broadcasted_iota(jnp.int32, (padded, width), 0)
    member = owner == kind
    before = lax.broadcasted_iota(jnp.int32, (width, width), 0) < lax.broadcasted_iota(
        jnp.int32, (width, width), 1
    )
    ranks = mm(member.astype(BF16), before.astype(BF16))
    place = jnp.sum(jnp.where(member, ranks, 0.0), axis=0, keepdims=True)
    return kind, place.astype(jnp.int32)


def one_hot(position, slots):
    slot = lax.broadcasted_iota(jnp.int32, (slots, position.shape[1]), 0)
    return (slot == position).astype(BF16)


def picked(pick, rows):
    high, middle, low = thirds(rows)
    return mm(pick, low) + mm(pick, middle) + mm(pick, high)


def plan(count):
    middle, chunks = count // 2, count // 2
    first = [(0, middle, ("stay", c)) for c in range(chunks)]
    relays = []
    for c in range(chunks):
        for k in range(1, count):
            if middle + k < count:
                relays.append((middle + k - 1, middle + k, ("stay", c)))
            if middle - k > 0:
                relays.append((middle - k + 1, middle - k, ("stay", c)))
    early = [(s, t, ("pick", s)) for t in range(1, count) for s in range(middle, count) if s != t]
    late = [(0, t, ("moved", t)) for t in range(1, count)]
    late += [(s, t, ("pick", s)) for t in range(count - 1, 0, -1) for s in range(1, middle) if s != t]
    late += [(s, 0, ("pick", s)) for s in range(middle, count)]
    early += [(s, 0, ("pick", s)) for s in range(1, middle)]
    ready = {(0, ("stay", c)): 0 for c in range(chunks)}
    rounds = []
    while first or relays or early or late:
        now, senders, targets = [], set(), set()
        for queue in (first, relays, early, [] if len(rounds) < chunks else late):
            for move in list(queue):
                s, t, item = move
                known = item[0] != "stay" or ready.get((s, item), len(rounds) + 1) <= len(rounds)
                if known and s not in senders and t not in targets:
                    now.append(move)
                    senders.add(s)
                    targets.add(t)
                    queue.remove(move)
        for s, t, item in now:
            ready[t, item] = len(rounds) + 3
        rounds.append(now)
    return rounds


def pick_kernel(count, order, me_ref, pivot_ref, matrix_ref, panel_ref, *refs):
    outs, (panel_out, rows_ref, pivot_v, sem) = refs[:-4], refs[-4:]
    rows, cols = matrix_ref.shape
    width = pivot_ref.shape[1]
    slot = width // count
    me = me_ref[0]
    point = pltpu.make_async_copy(pivot_ref, pivot_v, sem.at[0])
    head = pltpu.make_async_copy(matrix_ref.at[:width], rows_ref.at[:width], sem.at[1])
    tail = pltpu.make_async_copy(matrix_ref.at[width:], rows_ref.at[width:], sem.at[2])
    panel = pltpu.make_async_copy(panel_ref, panel_out, sem.at[3])
    point.start()
    head.start()
    tail.start()
    panel.start()
    point.wait()
    pivot = pivot_v[...]
    kind, place = classify(pivot, count, rows)
    head.wait()
    tail.wait()

    @pl.when(me == 0)
    def _():
        start = jnp.full(kind.shape, -count * width, jnp.int32)
        for k, (name, which) in enumerate(order):
            if name == "moved":
                start = jnp.where(kind == which, k * slot, start)
            else:
                inside = (kind == 0) & (place >= which * slot) & (place < (which + 1) * slot)
                start = jnp.where(inside, (k - which) * slot, start)
        got = picked(one_hot(start + place, len(order) * slot), rows_ref[:width, :])
        for k, out in enumerate(outs):
            out[...] = got[k * slot : (k + 1) * slot, :]

    @pl.when(me != 0)
    def _():
        mine = lax.broadcasted_iota(jnp.int32, (slot, width), 0) == jnp.where(kind == me, place, -1)
        source = jnp.sum(jnp.where(mine, pivot - me * rows, 0), axis=1, keepdims=True)
        pick = (lax.broadcasted_iota(jnp.int32, (slot, rows), 1) == source).astype(BF16)
        got = picked(pick, rows_ref[...])
        for out in outs:
            out[...] = got

    panel.wait()


def prepare_kernel(count, me_ref, pivot_ref, inverse_ref, matrix_ref, *refs):
    high_ref, low_ref, land_ref, base_ref, pivot_v, inv_ref, rows_ref, sem = refs[-8:]
    rows, cols = matrix_ref.shape
    width = pivot_ref.shape[1]
    slot = width // count
    stay = width // 2
    me = me_ref[0]
    copies = [
        pltpu.make_async_copy(pivot_ref, pivot_v, sem.at[0]),
        pltpu.make_async_copy(inverse_ref, inv_ref, sem.at[1]),
        pltpu.make_async_copy(matrix_ref, rows_ref, sem.at[2]),
    ]
    for copy in copies:
        copy.start()
    copies[0].wait()
    pivot = pivot_v[...]
    kind, place = classify(pivot, count, rows)
    total = high_ref.shape[1]
    middle = count // 2
    start = jnp.where(kind == 0, (count - middle) * slot, stay + (kind + count - middle - 1) * slot)
    spread = one_hot(place + jnp.where(kind < middle, start, (kind - middle) * slot), total)
    mine = (kind == me) & (kind != 0)
    landing = lax.broadcasted_iota(jnp.int32, (rows, width), 0) == jnp.where(mine, pivot - me * rows, -1)
    land = mm_nt(landing.astype(BF16), one_hot(jnp.where(mine, place, -1), slot))
    land_ref[...] = land.astype(BF16)
    taken = jnp.sum(land, axis=1, keepdims=True)
    copies[1].wait()
    inv_high, inv_low = halves(inv_ref[...])
    high_ref[...] = mm_nt(inv_high, spread).astype(BF16)
    low_ref[...] = mm_nt(inv_low, spread).astype(BF16)
    copies[2].wait()
    base_ref[...] = jnp.where(taken > 0.5, 0.0, rows_ref[...])


def turn_kernel(me_ref, ids_ref, near_ref, far_ref, inv_high, inv_low, land_ref, *refs):
    high_ref, low_ref, end_high, end_low, order_high, order_low = refs
    half, rows = near_ref.shape
    width, picked_rows = order_high.shape
    first = inv_high.shape[1] - picked_rows
    depth = width // ids_ref.shape[0]
    for k in range(ids_ref.shape[0]):
        source = pl.ds(pl.multiple_of(ids_ref[k] * depth, depth), depth)
        part = pl.ds(k * depth, depth)
        order_high[part, :] = inv_high[source, first:].astype(F32)
        order_low[part, :] = inv_low[source, first:].astype(F32)
    end_high[:, picked_rows:] = land_ref[...]
    end_low[:, picked_rows:] = jnp.zeros(land_ref.shape, BF16)

    def work(start):
        for k, part in enumerate((near_ref, far_ref)):
            high, low = halves(-part[:, start:])
            high_ref[start:, k * half : (k + 1) * half] = high.T
            low_ref[start:, k * half : (k + 1) * half] = low.T
        pan_high, last_high = high_ref[start:, :], order_high[...].astype(BF16)
        value = mm(low_ref[start:, :], last_high) + mm(pan_high, order_low[...].astype(BF16)) + mm(pan_high, last_high)
        end_high[start:, :picked_rows], end_low[start:, :picked_rows] = halves(value)

    @pl.when(me_ref[0] == 0)
    def _():
        work(width)
        end_high[:width, :picked_rows] = inv_high[:, first:]
        end_low[:width, :picked_rows] = inv_low[:, first:]

    @pl.when(me_ref[0] != 0)
    def _():
        work(0)


def collect(places, me, arrays, row_high, row_low):
    slot, cols = arrays[0].shape
    for r in range(len(places)):

        @pl.when(me == r)
        def _(r=r):
            for block, k in enumerate(places[r]):
                part = pl.ds(block * slot, slot)
                if k is None:
                    row_high[part, :] = jnp.zeros((slot, cols), BF16)
                    row_low[part, :] = jnp.zeros((slot, cols), BF16)
                else:
                    row_high[part, :], row_low[part, :] = halves(arrays[k][...])


def upper_kernel(places, me_ref, high_ref, low_ref, *refs):
    arrays, (out_ref, row_high, row_low) = refs[:-3], refs[-3:]
    collect(places, me_ref[0], arrays, row_high, row_low)
    depth = row_high.shape[0]
    high = high_ref[:, :depth]
    out_ref[...] = mm(low_ref[:, :depth], row_high[...]) + mm(high, row_low[...]) + mm(high, row_high[...])


def update_kernel(me_ref, ids_ref, rows_ref, high_ref, low_ref, upper_ref, out_ref, up_high, up_low):
    width = upper_ref.shape[0]
    depth = width // ids_ref.shape[0]
    for k in range(ids_ref.shape[0]):
        source = pl.multiple_of(ids_ref[k] * depth, depth)
        part = pl.ds(k * depth, depth)
        up_high[part, :], up_low[part, :] = halves(upper_ref[pl.ds(source, depth), :])

    def work(start):
        high = high_ref[start:, :]
        part = mm(low_ref[start:, :], up_high[...]) + mm(high, up_low[...]) + mm(high, up_high[...])
        out_ref[start:, :] = rows_ref[start:, :] + part

    @pl.when(me_ref[0] == 0)
    def _():
        work(width)
        out_ref[:width, :] = upper_ref[...]

    @pl.when(me_ref[0] != 0)
    def _():
        work(0)


def finish_kernel(places, me_ref, part_ref, high_ref, low_ref, *refs):
    arrays, (out_ref, row_high, row_low, total, sem) = refs[:-5], refs[-5:]
    collect(places, me_ref[0], arrays, row_high, row_low)
    rows = part_ref.shape[0]
    step = rows // sem.shape[0]
    copies = []
    for k in range(sem.shape[0]):
        part = pl.ds(k * step, step)
        high = high_ref[part, :]
        value = mm(low_ref[part, :], row_high[...]) + mm(high, row_low[...]) + mm(high, row_high[...])
        total[part, :] = part_ref[part, :] + value
        copies.append(pltpu.make_async_copy(total.at[part], out_ref.at[part], sem.at[k]))
        copies[-1].start()
    for copy in copies:
        copy.wait()


def join_kernel(first, second, *refs):
    out, sem = refs[-2:]
    rows = first.shape[0]
    copies = [
        pltpu.make_async_copy(first, out.at[:rows], sem.at[0]),
        pltpu.make_async_copy(second, out.at[rows:], sem.at[1]),
    ]
    for copy in copies:
        copy.start()
    for copy in copies:
        copy.wait()


def join(first, second, afters):
    rows, cols = first.shape
    return pl.pallas_call(
        join_kernel,
        out_shape=jax.ShapeDtypeStruct((2 * rows, cols), first.dtype),
        in_specs=[VMEM, VMEM] + [ANY] * len(afters),
        out_specs=VMEM,
        scratch_shapes=[pltpu.SemaphoreType.DMA((2,))],
        compiler_params=PARAMS,
        name="join",
    )(first, second, *afters)


def gather_shards(shard, count, afters):
    held, masks = shard, [0]
    bit = 1
    while 2 * bit < count:
        bit *= 2
    while bit:
        other = lax.ppermute(held, "col", [(i, i ^ bit) for i in range(count)])
        masks += [mask ^ bit for mask in masks]
        if bit > 1:
            held = join(held, other, afters[0])
            afters = afters[1:] or afters
        bit //= 2
    return held, other, masks


def local(row_count, col_count, matrix, panel_t, inverse_lower, pivot_rows):
    rows, cols = matrix.shape
    width = inverse_lower.shape[0]
    slot = width // row_count
    stay = width // 2
    me = lax.axis_index("row").astype(jnp.int32)
    column = lax.axis_index("col").astype(jnp.int32)
    here = me.reshape(1)
    pivot = pivot_rows.reshape(1, width)
    item_shape = jax.ShapeDtypeStruct((slot, cols), F32)

    rounds = plan(row_count)
    order = [item for moves in rounds for s, t, item in moves if s == 0]
    matrix = pltpu.with_memory_space_constraint(matrix, pltpu.HBM)
    pivot = pltpu.with_memory_space_constraint(pivot, pltpu.HBM)
    panel_t = pltpu.with_memory_space_constraint(panel_t, pltpu.HBM)
    inverse_lower = pltpu.with_memory_space_constraint(inverse_lower, pltpu.HBM)
    *own, panel = pl.pallas_call(
        functools.partial(pick_kernel, row_count, order),
        out_shape=(item_shape,) * len(order) + (jax.ShapeDtypeStruct(panel_t.shape, F32),),
        in_specs=[SMEM, HBM, HBM, HBM],
        out_specs=(VMEM,) * (len(order) + 1),
        scratch_shapes=[
            pltpu.VMEM((rows, cols), F32),
            pltpu.VMEM((1, width), jnp.int32),
            pltpu.SemaphoreType.DMA((4,)),
        ],
        compiler_params=PARAMS,
        name="pick",
    )(here, pivot, matrix, panel_t)

    arrays = list(own)
    found = [{} for _ in range(row_count)]
    for k, item in enumerate(order):
        found[0][item] = k
    for r in range(1, row_count):
        found[r]["pick", r] = 0
    operands, chunks = [], row_count // 2
    for moves in rounds:
        leaving = [item for s, t, item in moves if s == 0]
        operand = own[order.index(leaving[0])] if leaving else own[0]
        if len(operands) > chunks + 1 and all(item[0] == "stay" for s, t, item in moves):
            operand = arrays[len(own) + chunks]
        for s, t, item in moves:
            if s != 0 and item[0] == "stay":
                operand = jnp.where(me == s, arrays[found[s][item]], operand)
        for s, t, item in moves:
            found[t][item] = len(arrays)
        operands.append(operand)
        arrays.append(lax.ppermute(operand, "row", [(s, t) for s, t, item in moves]))
    received = arrays[len(own) :]
    blocks = [("pick", p) for p in range(chunks, row_count)]
    late_blocks = [("stay", c) for c in range(chunks)] + [("pick", p) for p in range(1, chunks)]
    places = [[found[r][item] for item in blocks] for r in range(row_count)]
    late = [[found[r].get(item) for item in late_blocks + [("moved", r)]] for r in range(row_count)]
    late_rows = len(late_blocks) * slot

    picked_rows = len(blocks) * slot + late_rows
    inv_high, inv_low, land, base = pl.pallas_call(
        functools.partial(prepare_kernel, row_count),
        out_shape=(
            jax.ShapeDtypeStruct((width, picked_rows), BF16),
            jax.ShapeDtypeStruct((width, picked_rows), BF16),
            jax.ShapeDtypeStruct((rows, slot), BF16),
            jax.ShapeDtypeStruct((rows, cols), F32),
        ),
        in_specs=[SMEM, HBM, HBM, HBM],
        out_specs=(VMEM,) * 4,
        scratch_shapes=[
            pltpu.VMEM((1, width), jnp.int32),
            pltpu.VMEM((width, width), F32),
            pltpu.VMEM((rows, cols), F32),
            pltpu.SemaphoreType.DMA((3,)),
        ],
        compiler_params=PARAMS,
        cost_estimate=SHORT,
        name="prepare",
    )(here, pivot, inverse_lower, matrix)

    near, far, masks = gather_shards(panel, col_count, [operands[3:5] + [land], []])
    ids = column ^ jnp.array(masks, jnp.int32)

    def used(*tables):
        names = sorted({k for table in tables for k in jax.tree.leaves(table)})
        return [arrays[k] for k in names], [jax.tree.map(names.index, table) for table in tables]

    early_arrays, (places,) = used(places)
    upper = pl.pallas_call(
        functools.partial(upper_kernel, places),
        out_shape=jax.ShapeDtypeStruct((width, cols), F32),
        in_specs=[SMEM] + [VMEM] * (2 + len(early_arrays)),
        out_specs=VMEM,
        scratch_shapes=[pltpu.VMEM((picked_rows - late_rows, cols), BF16)] * 2,
        compiler_params=PARAMS,
        cost_estimate=LONG,
        name="upper",
    )(here, inv_high, inv_low, *early_arrays)

    pan_high, pan_low, end_high, end_low = pl.pallas_call(
        turn_kernel,
        out_shape=(jax.ShapeDtypeStruct((rows, width), BF16),) * 2
        + (jax.ShapeDtypeStruct((rows, late_rows + slot), BF16),) * 2,
        in_specs=[SMEM, SMEM] + [VMEM] * 5,
        out_specs=(VMEM,) * 4,
        scratch_shapes=[pltpu.VMEM((width, late_rows), F32)] * 2,
        compiler_params=PARAMS,
        name="turn",
    )(here, ids, near, far, inv_high, inv_low, land)

    part = pl.pallas_call(
        update_kernel,
        out_shape=jax.ShapeDtypeStruct((rows, cols), F32),
        in_specs=[SMEM, SMEM] + [VMEM] * 4,
        out_specs=VMEM,
        scratch_shapes=[pltpu.VMEM((width, cols), BF16)] * 2,
        compiler_params=PARAMS,
        name="update",
    )(here, ids, base, pan_high, pan_low, upper)

    late_arrays, (late,) = used(late)
    steps = next(k for k in (3, 2, 1) if rows % (k * 16) == 0)
    return pl.pallas_call(
        functools.partial(finish_kernel, late),
        out_shape=jax.ShapeDtypeStruct((rows, cols), F32),
        in_specs=[SMEM] + [VMEM] * (3 + len(late_arrays)),
        out_specs=HBM,
        scratch_shapes=[pltpu.VMEM((late_rows + slot, cols), BF16)] * 2
        + [pltpu.VMEM((rows, cols), F32), pltpu.SemaphoreType.DMA((steps,))],
        compiler_params=PARAMS,
        name="finish",
    )(here, part, end_high, end_low, *late_arrays)


def solution(mesh):
    in_specs = (P("row", "col"), P("col", "row"), P(), P())
    out_specs = P("row", "col")
    return jax.shard_map(
        functools.partial(local, mesh.shape["row"], mesh.shape["col"]),
        mesh=mesh,
        in_specs=in_specs,
        out_specs=out_specs,
        check_vma=False,
    )
```

```python
import functools

import jax
import jax.numpy as jnp
from jax import lax
from jax.experimental import pallas as pl
from jax.experimental.pallas import tpu as pltpu
from jax.sharding import PartitionSpec as P

F32 = jnp.float32
BF16 = jnp.bfloat16
VMEM = pl.BlockSpec(memory_space=pltpu.VMEM)
SMEM = pl.BlockSpec(memory_space=pltpu.SMEM)
ANY = pl.BlockSpec(memory_space=pl.ANY)
HBM = pl.BlockSpec(memory_space=pltpu.HBM)
SHORT = pl.CostEstimate(flops=1_000_000, transcendentals=0, bytes_accessed=100_000)
LONG = pl.CostEstimate(flops=40_000_000_000, transcendentals=0, bytes_accessed=100_000_000)
PARAMS = pltpu.CompilerParams(vmem_limit_bytes=20 * 1024 * 1024)


def halves(x):
    high = x.astype(BF16)
    low = (x - high.astype(F32)).astype(BF16)
    return high, low


def mm(a, b):
    return jnp.dot(a, b, preferred_element_type=F32)


def mm_nt(a, b):
    return lax.dot_general(a, b, (((1,), (1,)), ((), ())), preferred_element_type=F32)


def mm_tn(a, b):
    return lax.dot_general(a, b, (((0,), (0,)), ((), ())), preferred_element_type=F32)


def classify(pivot, count, rows):
    width = pivot.shape[1]
    lanes = lax.broadcasted_iota(jnp.int32, (1, width), 1)
    kind = jnp.where(pivot != lanes, pivot // rows, 0)
    padded = -(-count // 16) * 16
    owner = lax.broadcasted_iota(jnp.int32, (padded, width), 0)
    member = owner == kind
    before = lax.broadcasted_iota(jnp.int32, (width, width), 0) < lax.broadcasted_iota(
        jnp.int32, (width, width), 1
    )
    ranks = mm(member.astype(BF16), before.astype(BF16))
    place = jnp.sum(jnp.where(member, ranks, 0.0), axis=0, keepdims=True)
    return kind, place.astype(jnp.int32)


def one_hot(position, slots):
    slot = lax.broadcasted_iota(jnp.int32, (slots, position.shape[1]), 0)
    return (slot == position).astype(BF16)


def picked(pick, rows_ref, copies):
    step = rows_ref.shape[0] // len(copies)
    total = None
    for k in range(pick.shape[1] // step):
        copies[k].wait()
        high, low = halves(rows_ref[k * step : (k + 1) * step, :])
        part = pick[:, k * step : (k + 1) * step]
        value = mm(part, low) + mm(part, high)
        total = value if total is None else total + value
    return total


def plan(count):
    middle, chunks = count // 2, count // 2
    first = [(0, middle, ("stay", c)) for c in range(chunks)]
    relays = []
    for c in range(chunks):
        for k in range(1, count):
            if middle + k < count:
                relays.append((middle + k - 1, middle + k, ("stay", c)))
            if middle - k > 0:
                relays.append((middle - k + 1, middle - k, ("stay", c)))
    early = [(s, t, ("pick", s)) for t in range(1, count) for s in range(middle, count) if s != t]
    late = [(0, t, ("moved", t)) for t in range(1, count)]
    late += [(s, t, ("pick", s)) for t in range(count - 1, 0, -1) for s in range(1, middle) if s != t]
    late += [(s, 0, ("pick", s)) for s in range(middle, count)]
    early += [(s, 0, ("pick", s)) for s in range(1, middle)]
    ready = {(0, ("stay", c)): 0 for c in range(chunks)}
    rounds = []
    while first or relays or early or late:
        now, senders, targets = [], set(), set()
        for queue in (first, relays, early, [] if len(rounds) < chunks else late):
            for move in list(queue):
                s, t, item = move
                known = item[0] != "stay" or ready.get((s, item), len(rounds) + 1) <= len(rounds)
                if known and s not in senders and t not in targets:
                    now.append(move)
                    senders.add(s)
                    targets.add(t)
                    queue.remove(move)
        for s, t, item in now:
            ready[t, item] = len(rounds) + 3
        rounds.append(now)
    return rounds


def pick_kernel(count, order, me_ref, pivot_ref, matrix_ref, panel_ref, *refs):
    outs, (panel_out, rows_ref, pivot_v, sem) = refs[:-4], refs[-4:]
    rows, cols = matrix_ref.shape
    width = pivot_ref.shape[1]
    slot = width // count
    me = me_ref[0]
    point = pltpu.make_async_copy(pivot_ref, pivot_v, sem.at[0])
    panel = pltpu.make_async_copy(panel_ref, panel_out, sem.at[1])
    step = rows // (sem.shape[0] - 2)
    copies = [
        pltpu.make_async_copy(matrix_ref.at[pl.ds(k * step, step)], rows_ref.at[pl.ds(k * step, step)], sem.at[2 + k])
        for k in range(rows // step)
    ]
    point.start()
    for copy in copies:
        copy.start()
    panel.start()
    point.wait()
    pivot = pivot_v[...]
    kind, place = classify(pivot, count, rows)

    @pl.when(me == 0)
    def _():
        start = jnp.full(kind.shape, -count * width, jnp.int32)
        for k, (name, which) in enumerate(order):
            if name == "moved":
                start = jnp.where(kind == which, k * slot, start)
            else:
                inside = (kind == 0) & (place >= which * slot) & (place < (which + 1) * slot)
                start = jnp.where(inside, (k - which) * slot, start)
        got = picked(one_hot(start + place, len(order) * slot), rows_ref, copies)
        for k, out in enumerate(outs):
            out[...] = got[k * slot : (k + 1) * slot, :]
        for copy in copies[width // step :]:
            copy.wait()

    @pl.when(me != 0)
    def _():
        mine = lax.broadcasted_iota(jnp.int32, (slot, width), 0) == jnp.where(kind == me, place, -1)
        source = jnp.sum(jnp.where(mine, pivot - me * rows, 0), axis=1, keepdims=True)
        pick = (lax.broadcasted_iota(jnp.int32, (slot, rows), 1) == source).astype(BF16)
        got = picked(pick, rows_ref, copies)
        for out in outs:
            out[...] = got

    panel.wait()


def prepare_kernel(count, me_ref, pivot_ref, inverse_ref, matrix_ref, *refs):
    high_ref, low_ref, land_ref, base_ref, pivot_v, inv_ref, rows_ref, sem = refs[-8:]
    rows, cols = matrix_ref.shape
    width = pivot_ref.shape[1]
    slot = width // count
    stay = width // 2
    me = me_ref[0]
    copies = [
        pltpu.make_async_copy(pivot_ref, pivot_v, sem.at[0]),
        pltpu.make_async_copy(inverse_ref, inv_ref, sem.at[1]),
        pltpu.make_async_copy(matrix_ref, rows_ref, sem.at[2]),
    ]
    for copy in copies:
        copy.start()
    copies[0].wait()
    pivot = pivot_v[...]
    kind, place = classify(pivot, count, rows)
    total = high_ref.shape[1]
    middle = count // 2
    start = jnp.where(kind == 0, (count - middle) * slot, stay + (kind + count - middle - 1) * slot)
    spread = one_hot(place + jnp.where(kind < middle, start, (kind - middle) * slot), total)
    mine = (kind == me) & (kind != 0)
    landing = lax.broadcasted_iota(jnp.int32, (rows, width), 0) == jnp.where(mine, pivot - me * rows, -1)
    land = mm_nt(landing.astype(BF16), one_hot(jnp.where(mine, place, -1), slot))
    land_ref[...] = land.astype(BF16)
    taken = jnp.sum(land, axis=1, keepdims=True)
    copies[1].wait()
    inv_high, inv_low = halves(inv_ref[...])
    high_ref[...] = mm_nt(inv_high, spread).astype(BF16)
    low_ref[...] = mm_nt(inv_low, spread).astype(BF16)
    copies[2].wait()
    base_ref[...] = jnp.where(taken > 0.5, 0.0, rows_ref[...])


def share_kernel(first_shard, last, me_ref, ids_ref, shards_ref, inv_high, inv_low, upper_ref, rows_ref, *refs):
    if last:
        ends_ref, land_ref = refs[:2]
    out_ref, end_high, end_low = refs[2:5] if last else (*refs[:2], None)
    high_ref, low_ref, side_high, side_low = refs[-4:]
    half, rows = shards_ref.shape
    width, cols = upper_ref.shape
    depth = width // ids_ref.shape[0]
    picked_rows = side_high.shape[1] - cols
    first = inv_high.shape[1] - picked_rows
    for k in range(half // depth):
        source = pl.ds(pl.multiple_of(ids_ref[first_shard + k] * depth, depth), depth)
        part = pl.ds(k * depth, depth)
        high, low = halves(upper_ref[source, :])
        side_high[part, :cols], side_low[part, :cols] = high.astype(F32), low.astype(F32)
        side_high[part, cols:] = inv_high[source, first:].astype(F32)
        side_low[part, cols:] = inv_low[source, first:].astype(F32)

    def work(start):
        high, low = halves(-shards_ref[:, start:])
        high_ref[start:, :] = high.T
        low_ref[start:, :] = low.T
        pan_high, right = high_ref[start:, :], side_high[...].astype(BF16)
        value = mm(low_ref[start:, :], right) + mm(pan_high, side_low[...].astype(BF16)) + mm(pan_high, right)
        out_ref[start:, :] = rows_ref[start:, :] + value[:, :cols]
        if last:
            end_high[start:, :picked_rows], end_low[start:, :picked_rows] = halves(
                ends_ref[start:, :] + value[:, cols:]
            )
        else:
            end_high[start:, :] = value[:, cols:]

    @pl.when(me_ref[0] == 0)
    def _():
        work(width)
        if last:
            out_ref[:width, :] = upper_ref[...]
            end_high[:width, :picked_rows] = inv_high[:, first:]
            end_low[:width, :picked_rows] = inv_low[:, first:]

    @pl.when(me_ref[0] != 0)
    def _():
        work(0)

    if last:
        end_high[:, picked_rows:] = land_ref[...]
        end_low[:, picked_rows:] = jnp.zeros(land_ref.shape, BF16)


def collect(places, me, arrays, row_high, row_low):
    slot, cols = arrays[0].shape
    for r in range(len(places)):

        @pl.when(me == r)
        def _(r=r):
            for block, k in enumerate(places[r]):
                part = pl.ds(block * slot, slot)
                if k is None:
                    row_high[part, :] = jnp.zeros((slot, cols), BF16)
                    row_low[part, :] = jnp.zeros((slot, cols), BF16)
                else:
                    row_high[part, :], row_low[part, :] = halves(arrays[k][...])


def upper_kernel(places, me_ref, high_ref, low_ref, *refs):
    arrays, (out_ref, row_high, row_low) = refs[:-3], refs[-3:]
    collect(places, me_ref[0], arrays, row_high, row_low)
    depth = row_high.shape[0]
    high = high_ref[:, :depth]
    out_ref[...] = mm(low_ref[:, :depth], row_high[...]) + mm(high, row_low[...]) + mm(high, row_high[...])


def finish_kernel(places, me_ref, part_ref, high_ref, low_ref, *refs):
    arrays, (out_ref, row_high, row_low, total, sem) = refs[:-5], refs[-5:]
    collect(places, me_ref[0], arrays, row_high, row_low)
    rows = part_ref.shape[0]
    step = rows // sem.shape[0]
    copies = []
    for k in range(sem.shape[0]):
        part = pl.ds(k * step, step)
        high = high_ref[part, :]
        value = mm(low_ref[part, :], row_high[...]) + mm(high, row_low[...]) + mm(high, row_high[...])
        total[part, :] = part_ref[part, :] + value
        copies.append(pltpu.make_async_copy(total.at[part], out_ref.at[part], sem.at[k]))
        copies[-1].start()
    for copy in copies:
        copy.wait()


def join_kernel(first, second, *refs):
    out, sem = refs[-2:]
    rows = first.shape[0]
    copies = [
        pltpu.make_async_copy(first, out.at[:rows], sem.at[0]),
        pltpu.make_async_copy(second, out.at[rows:], sem.at[1]),
    ]
    for copy in copies:
        copy.start()
    for copy in copies:
        copy.wait()


def join(first, second, afters):
    rows, cols = first.shape
    return pl.pallas_call(
        join_kernel,
        out_shape=jax.ShapeDtypeStruct((2 * rows, cols), first.dtype),
        in_specs=[VMEM, VMEM] + [ANY] * len(afters),
        out_specs=VMEM,
        scratch_shapes=[pltpu.SemaphoreType.DMA((2,))],
        compiler_params=PARAMS,
        name="join",
    )(first, second, *afters)


def gather_shards(shard, count, afters):
    held, masks = shard, [0]
    bit = 1
    while 2 * bit < count:
        bit *= 2
    while bit:
        other = lax.ppermute(held, "col", [(i, i ^ bit) for i in range(count)])
        masks += [mask ^ bit for mask in masks]
        if bit > 1:
            held = join(held, other, afters[0])
            afters = afters[1:] or afters
        bit //= 2
    return held, other, masks


def local(row_count, col_count, matrix, panel_t, inverse_lower, pivot_rows):
    rows, cols = matrix.shape
    width = inverse_lower.shape[0]
    slot = width // row_count
    stay = width // 2
    me = lax.axis_index("row").astype(jnp.int32)
    column = lax.axis_index("col").astype(jnp.int32)
    here = me.reshape(1)
    pivot = pivot_rows.reshape(1, width)
    item_shape = jax.ShapeDtypeStruct((slot, cols), F32)

    rounds = plan(row_count)
    order = [item for moves in rounds for s, t, item in moves if s == 0]
    matrix = pltpu.with_memory_space_constraint(matrix, pltpu.HBM)
    pivot = pltpu.with_memory_space_constraint(pivot, pltpu.HBM)
    panel_t = pltpu.with_memory_space_constraint(panel_t, pltpu.HBM)
    inverse_lower = pltpu.with_memory_space_constraint(inverse_lower, pltpu.HBM)
    pieces = next(k for k in range(3, 0, -1) if rows % (16 * k) == 0 and width % (rows // k) == 0)
    *own, panel = pl.pallas_call(
        functools.partial(pick_kernel, row_count, order),
        out_shape=(item_shape,) * len(order) + (jax.ShapeDtypeStruct(panel_t.shape, F32),),
        in_specs=[SMEM, HBM, HBM, HBM],
        out_specs=(VMEM,) * (len(order) + 1),
        scratch_shapes=[
            pltpu.VMEM((rows, cols), F32),
            pltpu.VMEM((1, width), jnp.int32),
            pltpu.SemaphoreType.DMA((2 + pieces,)),
        ],
        compiler_params=PARAMS,
        name="pick",
    )(here, pivot, matrix, panel_t)

    arrays = list(own)
    found = [{} for _ in range(row_count)]
    for k, item in enumerate(order):
        found[0][item] = k
    for r in range(1, row_count):
        found[r]["pick", r] = 0
    operands, chunks = [], row_count // 2
    for moves in rounds:
        leaving = [item for s, t, item in moves if s == 0]
        operand = own[order.index(leaving[0])] if leaving else own[0]
        if len(operands) > chunks + 1 and all(item[0] == "stay" for s, t, item in moves):
            operand = arrays[len(own) + chunks]
        for s, t, item in moves:
            if s != 0 and item[0] == "stay":
                operand = jnp.where(me == s, arrays[found[s][item]], operand)
        for s, t, item in moves:
            found[t][item] = len(arrays)
        operands.append(operand)
        arrays.append(lax.ppermute(operand, "row", [(s, t) for s, t, item in moves]))
    received = arrays[len(own) :]
    blocks = [("pick", p) for p in range(chunks, row_count)]
    late_blocks = [("stay", c) for c in range(chunks)] + [("pick", p) for p in range(1, chunks)]
    places = [[found[r][item] for item in blocks] for r in range(row_count)]
    late = [[found[r].get(item) for item in late_blocks + [("moved", r)]] for r in range(row_count)]
    late_rows = len(late_blocks) * slot

    picked_rows = len(blocks) * slot + late_rows
    inv_high, inv_low, land, base = pl.pallas_call(
        functools.partial(prepare_kernel, row_count),
        out_shape=(
            jax.ShapeDtypeStruct((width, picked_rows), BF16),
            jax.ShapeDtypeStruct((width, picked_rows), BF16),
            jax.ShapeDtypeStruct((rows, slot), BF16),
            jax.ShapeDtypeStruct((rows, cols), F32),
        ),
        in_specs=[SMEM, HBM, HBM, HBM],
        out_specs=(VMEM,) * 4,
        scratch_shapes=[
            pltpu.VMEM((1, width), jnp.int32),
            pltpu.VMEM((width, width), F32),
            pltpu.VMEM((rows, cols), F32),
            pltpu.SemaphoreType.DMA((3,)),
        ],
        compiler_params=PARAMS,
        cost_estimate=SHORT,
        name="prepare",
    )(here, pivot, inverse_lower, matrix)

    near, far, masks = gather_shards(panel, col_count, [operands[3:5] + [land], []])
    ids = column ^ jnp.array(masks, jnp.int32)

    def used(*tables):
        names = sorted({k for table in tables for k in jax.tree.leaves(table)})
        return [arrays[k] for k in names], [jax.tree.map(names.index, table) for table in tables]

    early_arrays, (places,) = used(places)
    upper = pl.pallas_call(
        functools.partial(upper_kernel, places),
        out_shape=jax.ShapeDtypeStruct((width, cols), F32),
        in_specs=[SMEM] + [VMEM] * (2 + len(early_arrays)),
        out_specs=VMEM,
        scratch_shapes=[pltpu.VMEM((picked_rows - late_rows, cols), BF16)] * 2,
        compiler_params=PARAMS,
        cost_estimate=LONG,
        name="upper",
    )(here, inv_high, inv_low, *early_arrays)

    half = width // 2
    share_scratch = [pltpu.VMEM((rows, half), BF16)] * 2 + [pltpu.VMEM((half, cols + late_rows), F32)] * 2
    part, ends = pl.pallas_call(
        functools.partial(share_kernel, 0, False),
        out_shape=(jax.ShapeDtypeStruct((rows, cols), F32), jax.ShapeDtypeStruct((rows, late_rows), F32)),
        in_specs=[SMEM, SMEM] + [VMEM] * 5,
        out_specs=(VMEM, VMEM),
        scratch_shapes=share_scratch,
        compiler_params=PARAMS,
        name="near",
    )(here, ids, near, inv_high, inv_low, upper, base)
    part, end_high, end_low = pl.pallas_call(
        functools.partial(share_kernel, col_count // 2, True),
        out_shape=(jax.ShapeDtypeStruct((rows, cols), F32),)
        + (jax.ShapeDtypeStruct((rows, late_rows + slot), BF16),) * 2,
        in_specs=[SMEM, SMEM] + [VMEM] * 7,
        out_specs=(VMEM,) * 3,
        scratch_shapes=share_scratch,
        compiler_params=PARAMS,
        name="far",
    )(here, ids, far, inv_high, inv_low, upper, part, ends, land)

    late_arrays, (late,) = used(late)
    steps = next(k for k in (3, 2, 1) if rows % (k * 16) == 0)
    return pl.pallas_call(
        functools.partial(finish_kernel, late),
        out_shape=jax.ShapeDtypeStruct((rows, cols), F32),
        in_specs=[SMEM] + [VMEM] * (3 + len(late_arrays)),
        out_specs=HBM,
        scratch_shapes=[pltpu.VMEM((late_rows + slot, cols), BF16)] * 2
        + [pltpu.VMEM((rows, cols), F32), pltpu.SemaphoreType.DMA((steps,))],
        compiler_params=PARAMS,
        name="finish",
    )(here, part, end_high, end_low, *late_arrays)


def solution(mesh):
    in_specs = (P("row", "col"), P("col", "row"), P(), P())
    out_specs = P("row", "col")
    return jax.shard_map(
        functools.partial(local, mesh.shape["row"], mesh.shape["col"]),
        mesh=mesh,
        in_specs=in_specs,
        out_specs=out_specs,
        check_vma=False,
    )
```

```python
import functools

import jax
import jax.numpy as jnp
from jax import lax
from jax.experimental import pallas as pl
from jax.experimental.pallas import tpu as pltpu
from jax.sharding import PartitionSpec as P

F32 = jnp.float32
BF16 = jnp.bfloat16
STEPS = 3
VMEM = pl.BlockSpec(memory_space=pltpu.VMEM)
SMEM = pl.BlockSpec(memory_space=pltpu.SMEM)
ANY = pl.BlockSpec(memory_space=pl.ANY)
HBM = pl.BlockSpec(memory_space=pltpu.HBM)
SHORT = pl.CostEstimate(flops=1_000_000, transcendentals=0, bytes_accessed=100_000)
LONG = pl.CostEstimate(flops=40_000_000_000, transcendentals=0, bytes_accessed=100_000_000)
PARAMS = pltpu.CompilerParams(vmem_limit_bytes=20 * 1024 * 1024)


def halves(x):
    high = x.astype(BF16)
    low = (x - high.astype(F32)).astype(BF16)
    return high, low


def mm(a, b):
    return jnp.dot(a, b, preferred_element_type=F32)


def mm_nt(a, b):
    return lax.dot_general(a, b, (((1,), (1,)), ((), ())), preferred_element_type=F32)


def mm_tn(a, b):
    return lax.dot_general(a, b, (((0,), (0,)), ((), ())), preferred_element_type=F32)


def classify(pivot, count, rows):
    width = pivot.shape[1]
    lanes = lax.broadcasted_iota(jnp.int32, (1, width), 1)
    kind = jnp.where(pivot != lanes, pivot // rows, 0)
    padded = -(-count // 16) * 16
    owner = lax.broadcasted_iota(jnp.int32, (padded, width), 0)
    member = owner == kind
    before = lax.broadcasted_iota(jnp.int32, (width, width), 0) < lax.broadcasted_iota(
        jnp.int32, (width, width), 1
    )
    ranks = mm(member.astype(BF16), before.astype(BF16))
    place = jnp.sum(jnp.where(member, ranks, 0.0), axis=0, keepdims=True)
    return kind, place.astype(jnp.int32)


def one_hot(position, slots):
    slot = lax.broadcasted_iota(jnp.int32, (slots, position.shape[1]), 0)
    return (slot == position).astype(BF16)


def picked(pick, rows_ref, copies):
    step = rows_ref.shape[0] // len(copies)
    total = None
    for k in range(pick.shape[1] // step):
        copies[k].wait()
        high, low = halves(rows_ref[k * step : (k + 1) * step, :])
        part = pick[:, k * step : (k + 1) * step]
        value = mm(part, low) + mm(part, high)
        total = value if total is None else total + value
    return total


def plan(count):
    middle, chunks = count // 2, count // 2
    first = [(0, middle, ("stay", c)) for c in range(chunks)]
    relays = []
    for c in range(chunks):
        for k in range(1, count):
            if middle + k < count:
                relays.append((middle + k - 1, middle + k, ("stay", c)))
            if middle - k > 0:
                relays.append((middle - k + 1, middle - k, ("stay", c)))
    early = [(s, t, ("pick", s)) for t in range(1, count) for s in range(middle, count) if s != t]
    late = [(0, t, ("moved", t)) for t in range(1, count)]
    late += [(s, t, ("pick", s)) for t in range(count - 1, 0, -1) for s in range(1, middle) if s != t]
    late += [(s, 0, ("pick", s)) for s in range(middle, count)]
    early += [(s, 0, ("pick", s)) for s in range(1, middle)]
    ready = {(0, ("stay", c)): 0 for c in range(chunks)}
    rounds = []
    while first or relays or early or late:
        now, senders, targets = [], set(), set()
        for queue in (first, relays, early, [] if len(rounds) < chunks else late):
            for move in list(queue):
                s, t, item = move
                known = item[0] != "stay" or ready.get((s, item), len(rounds) + 1) <= len(rounds)
                if known and s not in senders and t not in targets:
                    now.append(move)
                    senders.add(s)
                    targets.add(t)
                    queue.remove(move)
        for s, t, item in now:
            ready[t, item] = len(rounds) + 3
        rounds.append(now)
    return rounds


def pick_kernel(count, order, me_ref, pivot_ref, matrix_ref, panel_ref, *refs):
    outs, (panel_out, rows_ref, pivot_v, sem) = refs[:-4], refs[-4:]
    rows, cols = matrix_ref.shape
    width = pivot_ref.shape[1]
    slot = width // count
    me = me_ref[0]
    point = pltpu.make_async_copy(pivot_ref, pivot_v, sem.at[0])
    panel = pltpu.make_async_copy(panel_ref, panel_out, sem.at[1])
    step = rows // (sem.shape[0] - 2)
    copies = [
        pltpu.make_async_copy(matrix_ref.at[pl.ds(k * step, step)], rows_ref.at[pl.ds(k * step, step)], sem.at[2 + k])
        for k in range(rows // step)
    ]
    point.start()
    for copy in copies:
        copy.start()
    panel.start()
    point.wait()
    pivot = pivot_v[...]
    kind, place = classify(pivot, count, rows)

    @pl.when(me == 0)
    def _():
        start = jnp.full(kind.shape, -count * width, jnp.int32)
        for k, (name, which) in enumerate(order):
            if name == "moved":
                start = jnp.where(kind == which, k * slot, start)
            else:
                inside = (kind == 0) & (place >= which * slot) & (place < (which + 1) * slot)
                start = jnp.where(inside, (k - which) * slot, start)
        got = picked(one_hot(start + place, len(order) * slot), rows_ref, copies)
        for k, out in enumerate(outs):
            out[...] = got[k * slot : (k + 1) * slot, :]
        for copy in copies[width // step :]:
            copy.wait()

    @pl.when(me != 0)
    def _():
        mine = lax.broadcasted_iota(jnp.int32, (slot, width), 0) == jnp.where(kind == me, place, -1)
        source = jnp.sum(jnp.where(mine, pivot - me * rows, 0), axis=1, keepdims=True)
        pick = (lax.broadcasted_iota(jnp.int32, (slot, rows), 1) == source).astype(BF16)
        got = picked(pick, rows_ref, copies)
        for out in outs:
            out[...] = got

    panel.wait()


def prepare_kernel(count, me_ref, pivot_ref, inverse_ref, matrix_ref, *refs):
    high_ref, low_ref, land_ref, base_ref, pivot_v, inv_ref, rows_ref, sem = refs[-8:]
    rows, cols = matrix_ref.shape
    width = pivot_ref.shape[1]
    slot = width // count
    stay = width // 2
    me = me_ref[0]
    copies = [
        pltpu.make_async_copy(pivot_ref, pivot_v, sem.at[0]),
        pltpu.make_async_copy(inverse_ref, inv_ref, sem.at[1]),
        pltpu.make_async_copy(matrix_ref, rows_ref, sem.at[2]),
    ]
    for copy in copies:
        copy.start()
    copies[0].wait()
    pivot = pivot_v[...]
    kind, place = classify(pivot, count, rows)
    total = high_ref.shape[1]
    middle = count // 2
    start = jnp.where(kind == 0, (count - middle) * slot, stay + (kind + count - middle - 1) * slot)
    spread = one_hot(place + jnp.where(kind < middle, start, (kind - middle) * slot), total)
    mine = (kind == me) & (kind != 0)
    landing = lax.broadcasted_iota(jnp.int32, (rows, width), 0) == jnp.where(mine, pivot - me * rows, -1)
    land = mm_nt(landing.astype(BF16), one_hot(jnp.where(mine, place, -1), slot))
    land_ref[...] = land.astype(BF16)
    taken = jnp.sum(land, axis=1, keepdims=True)
    copies[1].wait()
    inv_high, inv_low = halves(inv_ref[...])
    high_ref[...] = mm_nt(inv_high, spread).astype(BF16)
    low_ref[...] = mm_nt(inv_low, spread).astype(BF16)
    copies[2].wait()
    base_ref[...] = jnp.where(taken > 0.5, 0.0, rows_ref[...])


def turn(shards_ref, start, high_ref, low_ref):
    high, low = halves(-shards_ref[:, start:])
    high_ref[start:, :] = high.T
    low_ref[start:, :] = low.T


def near_kernel(me_ref, ids_ref, shards_ref, inv_high, inv_low, ends_ref, high_ref, low_ref, side_high, side_low):
    half, rows = shards_ref.shape
    width = inv_high.shape[0]
    depth = width // ids_ref.shape[0]
    first = inv_high.shape[1] - side_high.shape[1]
    for k in range(half // depth):
        source = pl.ds(pl.multiple_of(ids_ref[k] * depth, depth), depth)
        part = pl.ds(k * depth, depth)
        side_high[part, :] = inv_high[source, first:].astype(F32)
        side_low[part, :] = inv_low[source, first:].astype(F32)

    def work(start):
        turn(shards_ref, start, high_ref, low_ref)
        high, right = high_ref[start:, :], side_high[...].astype(BF16)
        ends_ref[start:, :] = mm(low_ref[start:, :], right) + mm(high, side_low[...].astype(BF16)) + mm(high, right)

    pl.when(me_ref[0] == 0)(lambda: work(width))
    pl.when(me_ref[0] != 0)(lambda: work(0))


def far_kernel(me_ref, ids_ref, shards_ref, inv_high, inv_low, upper_ref, rows_ref, ends_ref, land_ref, *refs):
    near_high, near_low, out_ref, end_high, end_low, high_ref, low_ref = refs[:7]
    side_high, side_low, up_high, up_low = refs[7:]
    half, rows = shards_ref.shape
    width, cols = upper_ref.shape
    depth = width // ids_ref.shape[0]
    first = inv_high.shape[1] - (side_high.shape[1] - cols)
    stay, slot = width // 2, land_ref.shape[1]
    for k in range(width // depth):
        source = pl.ds(pl.multiple_of(ids_ref[k] * depth, depth), depth)
        high, low = halves(upper_ref[source, :])
        part = pl.ds(k * depth % half, depth)
        if k * depth < half:
            up_high[part, :], up_low[part, :] = high.astype(F32), low.astype(F32)
        else:
            side_high[part, :cols], side_low[part, :cols] = high.astype(F32), low.astype(F32)
            side_high[part, cols:] = inv_high[source, first:].astype(F32)
            side_low[part, cols:] = inv_low[source, first:].astype(F32)

    def work(start):
        turn(shards_ref, start, high_ref, low_ref)
        high, right = high_ref[start:, :], side_high[...].astype(BF16)
        value = mm(low_ref[start:, :], right) + mm(high, side_low[...].astype(BF16)) + mm(high, right)
        high, right = near_high[start:, :], up_high[...].astype(BF16)
        near = mm(near_low[start:, :], right) + mm(high, up_low[...].astype(BF16)) + mm(high, right)
        out_ref[start:, :] = rows_ref[start:, :] + (near + value[:, :cols])
        high, low = halves(ends_ref[start:, :] + value[:, cols:])
        put(end_high, start, high)
        put(end_low, start, low)

    def put(end, start, columns):
        part = pl.ds(start, columns.shape[0])
        end[part, :stay] = columns[:, :stay]
        end[part, stay + slot :] = columns[:, stay:]

    @pl.when(me_ref[0] == 0)
    def _():
        work(width)
        out_ref[:width, :] = upper_ref[...]
        put(end_high, 0, inv_high[:, first:])
        put(end_low, 0, inv_low[:, first:])

    pl.when(me_ref[0] != 0)(lambda: work(0))
    end_high[:, stay : stay + slot] = land_ref[...]
    end_low[:, stay : stay + slot] = jnp.zeros(land_ref.shape, BF16)


def collect(places, me, arrays, row_high, row_low):
    slot, cols = arrays[0].shape
    for r in range(len(places)):

        @pl.when(me == r)
        def _(r=r):
            for block, k in enumerate(places[r]):
                part = pl.ds(block * slot, slot)
                if k is None:
                    row_high[part, :] = jnp.zeros((slot, cols), BF16)
                    row_low[part, :] = jnp.zeros((slot, cols), BF16)
                else:
                    row_high[part, :], row_low[part, :] = halves(arrays[k][...])


def upper_kernel(places, me_ref, high_ref, low_ref, *refs):
    arrays, (out_ref, row_high, row_low) = refs[:-3], refs[-3:]
    collect(places, me_ref[0], arrays, row_high, row_low)
    depth = row_high.shape[0]
    high = high_ref[:, :depth]
    out_ref[...] = mm(low_ref[:, :depth], row_high[...]) + mm(high, row_low[...]) + mm(high, row_high[...])


def share(places, me, part_ref, high_ref, low_ref, arrays, row_high, row_low, give):
    slot, cols = arrays[0].shape
    rows = part_ref.shape[0]
    step = rows // STEPS if rows % (STEPS * 16) == 0 else rows
    for r, table in enumerate(places):

        @pl.when(me == r)
        def _(table=table):
            here = [block for block, k in enumerate(table) if k is not None]
            span = pl.ds(here[0] * slot, (here[-1] + 1 - here[0]) * slot) if here else None
            for block in range(here[0], here[-1] + 1) if here else ():
                part = pl.ds(block * slot, slot)
                if table[block] is None:
                    row_high[part, :] = jnp.zeros((slot, cols), BF16)
                    row_low[part, :] = jnp.zeros((slot, cols), BF16)
                else:
                    row_high[part, :], row_low[part, :] = halves(arrays[table[block]][...])
            for k in range(rows // step):
                part = pl.ds(k * step, step)
                value = part_ref[part, :]
                if here:
                    high = high_ref[part, span]
                    more = mm(low_ref[part, span], row_high[span, :]) + mm(high, row_low[span, :])
                    value = value + (more + mm(high, row_high[span, :]))
                give(k, part, value)


def middle_kernel(places, me_ref, part_ref, high_ref, low_ref, *refs):
    arrays, (out_ref, row_high, row_low) = refs[:-3], refs[-3:]

    def give(k, part, value):
        out_ref[part, :] = value

    share(places, me_ref[0], part_ref, high_ref, low_ref, arrays, row_high, row_low, give)


def finish_kernel(places, me_ref, part_ref, high_ref, low_ref, *refs):
    arrays, (out_ref, row_high, row_low, total, sem) = refs[:-5], refs[-5:]

    def copy(k, part):
        return pltpu.make_async_copy(total.at[part], out_ref.at[part], sem.at[k])

    def give(k, part, value):
        total[part, :] = value
        copy(k, part).start()

    share(places, me_ref[0], part_ref, high_ref, low_ref, arrays, row_high, row_low, give)
    step = total.shape[0] // sem.shape[0]
    for k in range(sem.shape[0]):
        copy(k, pl.ds(k * step, step)).wait()


def join_kernel(first, second, *refs):
    out, sem = refs[-2:]
    rows = first.shape[0]
    copies = [
        pltpu.make_async_copy(first, out.at[:rows], sem.at[0]),
        pltpu.make_async_copy(second, out.at[rows:], sem.at[1]),
    ]
    for copy in copies:
        copy.start()
    for copy in copies:
        copy.wait()


def join(first, second, afters):
    rows, cols = first.shape
    return pl.pallas_call(
        join_kernel,
        out_shape=jax.ShapeDtypeStruct((2 * rows, cols), first.dtype),
        in_specs=[VMEM, VMEM] + [ANY] * len(afters),
        out_specs=VMEM,
        scratch_shapes=[pltpu.SemaphoreType.DMA((2,))],
        compiler_params=PARAMS,
        name="join",
    )(first, second, *afters)


def gather_shards(shard, count, afters):
    held, masks = shard, [0]
    bit = 1
    while 2 * bit < count:
        bit *= 2
    while bit:
        other = lax.ppermute(held, "col", [(i, i ^ bit) for i in range(count)])
        masks += [mask ^ bit for mask in masks]
        if bit > 1:
            held = join(held, other, afters[0])
            afters = afters[1:] or afters
        bit //= 2
    return held, other, masks


def local(row_count, col_count, matrix, panel_t, inverse_lower, pivot_rows):
    rows, cols = matrix.shape
    width = inverse_lower.shape[0]
    slot = width // row_count
    stay = width // 2
    me = lax.axis_index("row").astype(jnp.int32)
    column = lax.axis_index("col").astype(jnp.int32)
    here = me.reshape(1)
    pivot = pivot_rows.reshape(1, width)
    item_shape = jax.ShapeDtypeStruct((slot, cols), F32)

    rounds = plan(row_count)
    order = [item for moves in rounds for s, t, item in moves if s == 0]
    matrix = pltpu.with_memory_space_constraint(matrix, pltpu.HBM)
    pivot = pltpu.with_memory_space_constraint(pivot, pltpu.HBM)
    panel_t = pltpu.with_memory_space_constraint(panel_t, pltpu.HBM)
    inverse_lower = pltpu.with_memory_space_constraint(inverse_lower, pltpu.HBM)
    pieces = next(k for k in range(3, 0, -1) if rows % (16 * k) == 0 and width % (rows // k) == 0)
    *own, panel = pl.pallas_call(
        functools.partial(pick_kernel, row_count, order),
        out_shape=(item_shape,) * len(order) + (jax.ShapeDtypeStruct(panel_t.shape, F32),),
        in_specs=[SMEM, HBM, HBM, HBM],
        out_specs=(VMEM,) * (len(order) + 1),
        scratch_shapes=[
            pltpu.VMEM((rows, cols), F32),
            pltpu.VMEM((1, width), jnp.int32),
            pltpu.SemaphoreType.DMA((2 + pieces,)),
        ],
        compiler_params=PARAMS,
        name="pick",
    )(here, pivot, matrix, panel_t)

    arrays = list(own)
    found = [{} for _ in range(row_count)]
    for k, item in enumerate(order):
        found[0][item] = k
    for r in range(1, row_count):
        found[r]["pick", r] = 0
    operands, chunks = [], row_count // 2
    for moves in rounds:
        leaving = [item for s, t, item in moves if s == 0]
        operand = own[order.index(leaving[0])] if leaving else own[0]
        if len(operands) > chunks + 1 and all(item[0] == "stay" for s, t, item in moves):
            operand = arrays[len(own) + chunks]
        for s, t, item in moves:
            if s != 0 and item[0] == "stay":
                operand = jnp.where(me == s, arrays[found[s][item]], operand)
        for s, t, item in moves:
            found[t][item] = len(arrays)
        operands.append(operand)
        arrays.append(lax.ppermute(operand, "row", [(s, t) for s, t, item in moves]))
    received = arrays[len(own) :]
    blocks = [("pick", p) for p in range(chunks, row_count)]
    late_blocks = [("stay", c) for c in range(chunks)] + [("pick", p) for p in range(1, chunks)]
    soon = len(own) + chunks + 2
    places = [[found[r][item] for item in blocks] for r in range(row_count)]
    late = [
        [found[r].get(item) for item in late_blocks[:chunks] + [("moved", r)] + late_blocks[chunks:]]
        for r in range(row_count)
    ]
    soon_late = [[k if k is not None and k < soon else None for k in table] for table in late]
    late = [[k if k is not None and k >= soon else None for k in table] for table in late]
    late_rows = len(late_blocks) * slot

    picked_rows = len(blocks) * slot + late_rows
    inv_high, inv_low, land, base = pl.pallas_call(
        functools.partial(prepare_kernel, row_count),
        out_shape=(
            jax.ShapeDtypeStruct((width, picked_rows), BF16),
            jax.ShapeDtypeStruct((width, picked_rows), BF16),
            jax.ShapeDtypeStruct((rows, slot), BF16),
            jax.ShapeDtypeStruct((rows, cols), F32),
        ),
        in_specs=[SMEM, HBM, HBM, HBM],
        out_specs=(VMEM,) * 4,
        scratch_shapes=[
            pltpu.VMEM((1, width), jnp.int32),
            pltpu.VMEM((width, width), F32),
            pltpu.VMEM((rows, cols), F32),
            pltpu.SemaphoreType.DMA((3,)),
        ],
        compiler_params=PARAMS,
        cost_estimate=SHORT,
        name="prepare",
    )(here, pivot, inverse_lower, matrix)

    near, far, masks = gather_shards(panel, col_count, [operands[3:5] + [land], []])
    ids = column ^ jnp.array(masks, jnp.int32)

    def used(*tables):
        names = sorted({k for table in tables for k in jax.tree.leaves(table)})
        return [arrays[k] for k in names], [jax.tree.map(names.index, table) for table in tables]

    early_arrays, (places,) = used(places)
    upper = pl.pallas_call(
        functools.partial(upper_kernel, places),
        out_shape=jax.ShapeDtypeStruct((width, cols), F32),
        in_specs=[SMEM] + [VMEM] * (2 + len(early_arrays)),
        out_specs=VMEM,
        scratch_shapes=[pltpu.VMEM((picked_rows - late_rows, cols), BF16)] * 2,
        compiler_params=PARAMS,
        cost_estimate=LONG,
        name="upper",
    )(here, inv_high, inv_low, *early_arrays)

    half = width // 2
    ends, near_high, near_low = pl.pallas_call(
        near_kernel,
        out_shape=(jax.ShapeDtypeStruct((rows, late_rows), F32),) + (jax.ShapeDtypeStruct((rows, half), BF16),) * 2,
        in_specs=[SMEM, SMEM] + [VMEM] * 3,
        out_specs=(VMEM,) * 3,
        scratch_shapes=[pltpu.VMEM((half, late_rows), F32)] * 2,
        compiler_params=PARAMS,
        name="near",
    )(here, ids, near, inv_high, inv_low)
    part, end_high, end_low = pl.pallas_call(
        far_kernel,
        out_shape=(jax.ShapeDtypeStruct((rows, cols), F32),)
        + (jax.ShapeDtypeStruct((rows, late_rows + slot), BF16),) * 2,
        in_specs=[SMEM, SMEM] + [VMEM] * 9,
        out_specs=(VMEM,) * 3,
        scratch_shapes=[pltpu.VMEM((rows, half), BF16)] * 2
        + [pltpu.VMEM((half, cols + late_rows), F32)] * 2
        + [pltpu.VMEM((half, cols), F32)] * 2,
        compiler_params=PARAMS,
        name="far",
    )(here, ids, far, inv_high, inv_low, upper, base, ends, land, near_high, near_low)

    row_scratch = [pltpu.VMEM((late_rows + slot, cols), BF16)] * 2
    soon_arrays, (soon_late,) = used(soon_late)
    part = pl.pallas_call(
        functools.partial(middle_kernel, soon_late),
        out_shape=jax.ShapeDtypeStruct((rows, cols), F32),
        in_specs=[SMEM] + [VMEM] * (3 + len(soon_arrays)),
        out_specs=VMEM,
        scratch_shapes=row_scratch,
        compiler_params=PARAMS,
        name="middle",
    )(here, part, end_high, end_low, *soon_arrays)

    late_arrays, (late,) = used(late)
    steps = STEPS if rows % (STEPS * 16) == 0 else 1
    return pl.pallas_call(
        functools.partial(finish_kernel, late),
        out_shape=jax.ShapeDtypeStruct((rows, cols), F32),
        in_specs=[SMEM] + [VMEM] * (3 + len(late_arrays)),
        out_specs=HBM,
        scratch_shapes=row_scratch + [pltpu.VMEM((rows, cols), F32), pltpu.SemaphoreType.DMA((steps,))],
        compiler_params=PARAMS,
        name="finish",
    )(here, part, end_high, end_low, *late_arrays)


def solution(mesh):
    in_specs = (P("row", "col"), P("col", "row"), P(), P())
    out_specs = P("row", "col")
    return jax.shard_map(
        functools.partial(local, mesh.shape["row"], mesh.shape["col"]),
        mesh=mesh,
        in_specs=in_specs,
        out_specs=out_specs,
        check_vma=False,
    )
```

```python
import functools

import jax
import jax.numpy as jnp
from jax import lax
from jax.experimental import pallas as pl
from jax.experimental.pallas import tpu as pltpu
from jax.sharding import PartitionSpec as P

F32 = jnp.float32
BF16 = jnp.bfloat16
STEPS = 3
VMEM = pl.BlockSpec(memory_space=pltpu.VMEM)
SMEM = pl.BlockSpec(memory_space=pltpu.SMEM)
ANY = pl.BlockSpec(memory_space=pl.ANY)
HBM = pl.BlockSpec(memory_space=pltpu.HBM)
SHORT = pl.CostEstimate(flops=1_000_000, transcendentals=0, bytes_accessed=100_000)
LONG = pl.CostEstimate(flops=40_000_000_000, transcendentals=0, bytes_accessed=100_000_000)
PARAMS = pltpu.CompilerParams(vmem_limit_bytes=20 * 1024 * 1024)


def halves(x):
    high = x.astype(BF16)
    low = (x - high.astype(F32)).astype(BF16)
    return high, low


def mm(a, b):
    return jnp.dot(a, b, preferred_element_type=F32)


def mm_nt(a, b):
    return lax.dot_general(a, b, (((1,), (1,)), ((), ())), preferred_element_type=F32)


def mm_tn(a, b):
    return lax.dot_general(a, b, (((0,), (0,)), ((), ())), preferred_element_type=F32)


def classify(pivot, count, rows):
    width = pivot.shape[1]
    lanes = lax.broadcasted_iota(jnp.int32, (1, width), 1)
    kind = jnp.where(pivot != lanes, pivot // rows, 0)
    padded = -(-count // 16) * 16
    owner = lax.broadcasted_iota(jnp.int32, (padded, width), 0)
    member = owner == kind
    before = lax.broadcasted_iota(jnp.int32, (width, width), 0) < lax.broadcasted_iota(
        jnp.int32, (width, width), 1
    )
    ranks = mm(member.astype(BF16), before.astype(BF16))
    place = jnp.sum(jnp.where(member, ranks, 0.0), axis=0, keepdims=True)
    return kind, place.astype(jnp.int32)


def one_hot(position, slots):
    slot = lax.broadcasted_iota(jnp.int32, (slots, position.shape[1]), 0)
    return (slot == position).astype(BF16)


def picked(pick, rows_ref, copies):
    step = rows_ref.shape[0] // len(copies)
    total = None
    for k in range(pick.shape[1] // step):
        copies[k].wait()
        high, low = halves(rows_ref[k * step : (k + 1) * step, :])
        part = pick[:, k * step : (k + 1) * step]
        value = mm(part, low) + mm(part, high)
        total = value if total is None else total + value
    return total


def plan(count):
    middle, chunks = count // 2, count // 2
    first = [(0, middle, ("stay", c)) for c in range(chunks)]
    relays = []
    for c in range(chunks):
        for k in range(1, count):
            if middle + k < count:
                relays.append((middle + k - 1, middle + k, ("stay", c)))
            if middle - k > 0:
                relays.append((middle - k + 1, middle - k, ("stay", c)))
    early = [(s, t, ("pick", s)) for t in range(1, count) for s in range(middle, count) if s != t]
    late = [(0, t, ("moved", t)) for t in range(1, count)]
    late += [(s, t, ("pick", s)) for t in range(count - 1, 0, -1) for s in range(1, middle) if s != t]
    late += [(s, 0, ("pick", s)) for s in range(middle, count)]
    early += [(s, 0, ("pick", s)) for s in range(1, middle)]
    ready = {(0, ("stay", c)): 0 for c in range(chunks)}
    rounds = []
    while first or relays or early or late:
        now, senders, targets = [], set(), set()
        for queue in (first, relays, early, [] if len(rounds) < chunks else late):
            for move in list(queue):
                s, t, item = move
                known = item[0] != "stay" or ready.get((s, item), len(rounds) + 1) <= len(rounds)
                if known and s not in senders and t not in targets:
                    now.append(move)
                    senders.add(s)
                    targets.add(t)
                    queue.remove(move)
        for s, t, item in now:
            ready[t, item] = len(rounds) + 3
        rounds.append(now)
    return rounds


def pick_kernel(count, order, me_ref, pivot_ref, matrix_ref, panel_ref, *refs):
    outs, (panel_out, rows_ref, pivot_v, sem) = refs[:-4], refs[-4:]
    rows, cols = matrix_ref.shape
    width = pivot_ref.shape[1]
    slot = width // count
    me = me_ref[0]
    point = pltpu.make_async_copy(pivot_ref, pivot_v, sem.at[0])
    panel = pltpu.make_async_copy(panel_ref, panel_out, sem.at[1])
    step = rows // (sem.shape[0] - 2)
    copies = [
        pltpu.make_async_copy(matrix_ref.at[pl.ds(k * step, step)], rows_ref.at[pl.ds(k * step, step)], sem.at[2 + k])
        for k in range(rows // step)
    ]
    point.start()
    for copy in copies:
        copy.start()
    panel.start()
    point.wait()
    pivot = pivot_v[...]
    kind, place = classify(pivot, count, rows)

    @pl.when(me == 0)
    def _():
        start = jnp.full(kind.shape, -count * width, jnp.int32)
        for k, (name, which) in enumerate(order):
            if name == "moved":
                start = jnp.where(kind == which, k * slot, start)
            else:
                inside = (kind == 0) & (place >= which * slot) & (place < (which + 1) * slot)
                start = jnp.where(inside, (k - which) * slot, start)
        got = picked(one_hot(start + place, len(order) * slot), rows_ref, copies)
        for k, out in enumerate(outs):
            out[...] = got[k * slot : (k + 1) * slot, :]
        for copy in copies[width // step :]:
            copy.wait()

    @pl.when(me != 0)
    def _():
        mine = lax.broadcasted_iota(jnp.int32, (slot, width), 0) == jnp.where(kind == me, place, -1)
        source = jnp.sum(jnp.where(mine, pivot - me * rows, 0), axis=1, keepdims=True)
        pick = (lax.broadcasted_iota(jnp.int32, (slot, rows), 1) == source).astype(BF16)
        got = picked(pick, rows_ref, copies)
        for out in outs:
            out[...] = got

    panel.wait()


def prepare_kernel(count, me_ref, pivot_ref, inverse_ref, matrix_ref, *refs):
    high_ref, low_ref, land_ref, base_ref, pivot_v, inv_ref, rows_ref, sem = refs[-8:]
    rows, cols = matrix_ref.shape
    width = pivot_ref.shape[1]
    slot = width // count
    stay = width // 2
    me = me_ref[0]
    copies = [
        pltpu.make_async_copy(pivot_ref, pivot_v, sem.at[0]),
        pltpu.make_async_copy(inverse_ref, inv_ref, sem.at[1]),
        pltpu.make_async_copy(matrix_ref, rows_ref, sem.at[2]),
    ]
    for copy in copies:
        copy.start()
    copies[0].wait()
    pivot = pivot_v[...]
    kind, place = classify(pivot, count, rows)
    total = high_ref.shape[1]
    middle = count // 2
    start = jnp.where(kind == 0, (count - middle) * slot, stay + (kind + count - middle - 1) * slot)
    spread = one_hot(place + jnp.where(kind < middle, start, (kind - middle) * slot), total)
    mine = (kind == me) & (kind != 0)
    landing = lax.broadcasted_iota(jnp.int32, (rows, width), 0) == jnp.where(mine, pivot - me * rows, -1)
    land = mm_nt(landing.astype(BF16), one_hot(jnp.where(mine, place, -1), slot))
    land_ref[...] = land.astype(BF16)
    taken = jnp.sum(land, axis=1, keepdims=True)
    copies[1].wait()
    inv_high, inv_low = halves(inv_ref[...])
    high_ref[...] = mm_nt(inv_high, spread).astype(BF16)
    low_ref[...] = mm_nt(inv_low, spread).astype(BF16)
    copies[2].wait()
    base_ref[...] = jnp.where(taken > 0.5, 0.0, rows_ref[...])


def turn(shards_ref, start, high_ref, low_ref):
    high, low = halves(-shards_ref[:, start:])
    high_ref[start:, :] = high.T
    low_ref[start:, :] = low.T


def near_kernel(me_ref, ids_ref, shards_ref, inv_high, inv_low, ends_ref, high_ref, low_ref, side_high, side_low):
    half, rows = shards_ref.shape
    width = inv_high.shape[0]
    depth = width // ids_ref.shape[0]
    first = inv_high.shape[1] - side_high.shape[1]
    for k in range(half // depth):
        source = pl.ds(pl.multiple_of(ids_ref[k] * depth, depth), depth)
        part = pl.ds(k * depth, depth)
        side_high[part, :] = inv_high[source, first:].astype(F32)
        side_low[part, :] = inv_low[source, first:].astype(F32)

    def work(start):
        turn(shards_ref, start, high_ref, low_ref)
        high, right = high_ref[start:, :], side_high[...].astype(BF16)
        ends_ref[start:, :] = mm(low_ref[start:, :], right) + mm(high, side_low[...].astype(BF16)) + mm(high, right)

    pl.when(me_ref[0] == 0)(lambda: work(width))
    pl.when(me_ref[0] != 0)(lambda: work(0))


def far_kernel(me_ref, ids_ref, shards_ref, inv_high, inv_low, upper_ref, rows_ref, ends_ref, land_ref, *refs):
    near_high, near_low, out_ref, end_high, end_low, high_ref, low_ref = refs[:7]
    side_high, side_low, up_high, up_low = refs[7:]
    half, rows = shards_ref.shape
    width, cols = upper_ref.shape
    depth = width // ids_ref.shape[0]
    first = inv_high.shape[1] - (side_high.shape[1] - cols)
    stay, slot = width // 2, land_ref.shape[1]
    for k in range(width // depth):
        source = pl.ds(pl.multiple_of(ids_ref[k] * depth, depth), depth)
        high, low = halves(upper_ref[source, :])
        part = pl.ds(k * depth % half, depth)
        if k * depth < half:
            up_high[part, :], up_low[part, :] = high.astype(F32), low.astype(F32)
        else:
            side_high[part, :cols], side_low[part, :cols] = high.astype(F32), low.astype(F32)
            side_high[part, cols:] = inv_high[source, first:].astype(F32)
            side_low[part, cols:] = inv_low[source, first:].astype(F32)

    def work(start):
        turn(shards_ref, start, high_ref, low_ref)
        high, right = high_ref[start:, :], side_high[...].astype(BF16)
        value = mm(low_ref[start:, :], right) + mm(high, side_low[...].astype(BF16)) + mm(high, right)
        high, right = near_high[start:, :], up_high[...].astype(BF16)
        near = mm(near_low[start:, :], right) + mm(high, up_low[...].astype(BF16)) + mm(high, right)
        out_ref[start:, :] = rows_ref[start:, :] + (near + value[:, :cols])
        high, low = halves(ends_ref[start:, :] + value[:, cols:])
        put(end_high, start, high)
        put(end_low, start, low)

    def put(end, start, columns):
        part = pl.ds(start, columns.shape[0])
        end[part, :stay] = columns[:, :stay]
        end[part, stay + slot :] = columns[:, stay:]

    @pl.when(me_ref[0] == 0)
    def _():
        work(width)
        out_ref[:width, :] = upper_ref[...]
        put(end_high, 0, inv_high[:, first:])
        put(end_low, 0, inv_low[:, first:])

    pl.when(me_ref[0] != 0)(lambda: work(0))
    end_high[:, stay : stay + slot] = land_ref[...]
    end_low[:, stay : stay + slot] = jnp.zeros(land_ref.shape, BF16)


def collect(places, me, arrays, row_high, row_low):
    slot, cols = arrays[0].shape
    for r in range(len(places)):

        @pl.when(me == r)
        def _(r=r):
            for block, k in enumerate(places[r]):
                part = pl.ds(block * slot, slot)
                if k is None:
                    row_high[part, :] = jnp.zeros((slot, cols), BF16)
                    row_low[part, :] = jnp.zeros((slot, cols), BF16)
                else:
                    row_high[part, :], row_low[part, :] = halves(arrays[k][...])


def upper_kernel(places, me_ref, high_ref, low_ref, *refs):
    arrays, (out_ref, row_high, row_low) = refs[:-4], refs[-3:]
    collect(places, me_ref[0], arrays, row_high, row_low)
    depth = row_high.shape[0]
    high = high_ref[:, :depth]
    out_ref[...] = mm(low_ref[:, :depth], row_high[...]) + mm(high, row_low[...]) + mm(high, row_high[...])


def share(places, me, part_ref, high_ref, low_ref, arrays, row_high, row_low, give):
    slot, cols = arrays[0].shape
    rows = part_ref.shape[0]
    step = rows // STEPS if rows % (STEPS * 16) == 0 else rows
    for r, table in enumerate(places):

        @pl.when(me == r)
        def _(table=table):
            here = [block for block, k in enumerate(table) if k is not None]
            span = pl.ds(here[0] * slot, (here[-1] + 1 - here[0]) * slot) if here else None
            for block in range(here[0], here[-1] + 1) if here else ():
                part = pl.ds(block * slot, slot)
                if table[block] is None:
                    row_high[part, :] = jnp.zeros((slot, cols), BF16)
                    row_low[part, :] = jnp.zeros((slot, cols), BF16)
                else:
                    row_high[part, :], row_low[part, :] = halves(arrays[table[block]][...])
            for k in range(rows // step):
                part = pl.ds(k * step, step)
                value = part_ref[part, :]
                if here:
                    high = high_ref[part, span]
                    more = mm(low_ref[part, span], row_high[span, :]) + mm(high, row_low[span, :])
                    value = value + (more + mm(high, row_high[span, :]))
                give(k, part, value)


def middle_kernel(places, me_ref, part_ref, high_ref, low_ref, *refs):
    arrays, (out_ref, row_high, row_low) = refs[:-3], refs[-3:]

    def give(k, part, value):
        out_ref[part, :] = value

    share(places, me_ref[0], part_ref, high_ref, low_ref, arrays, row_high, row_low, give)


def finish_kernel(places, me_ref, part_ref, high_ref, low_ref, *refs):
    arrays, (out_ref, row_high, row_low, total, sem) = refs[:-5], refs[-5:]

    def copy(k, part):
        return pltpu.make_async_copy(total.at[part], out_ref.at[part], sem.at[k])

    def give(k, part, value):
        total[part, :] = value
        copy(k, part).start()

    share(places, me_ref[0], part_ref, high_ref, low_ref, arrays, row_high, row_low, give)
    step = total.shape[0] // sem.shape[0]
    for k in range(sem.shape[0]):
        copy(k, pl.ds(k * step, step)).wait()


def join_kernel(first, second, *refs):
    out, sem = refs[-2:]
    rows = first.shape[0]
    copies = [
        pltpu.make_async_copy(first, out.at[:rows], sem.at[0]),
        pltpu.make_async_copy(second, out.at[rows:], sem.at[1]),
    ]
    for copy in copies:
        copy.start()
    for copy in copies:
        copy.wait()


def join(first, second, afters):
    rows, cols = first.shape
    return pl.pallas_call(
        join_kernel,
        out_shape=jax.ShapeDtypeStruct((2 * rows, cols), first.dtype),
        in_specs=[VMEM, VMEM] + [ANY] * len(afters),
        out_specs=VMEM,
        scratch_shapes=[pltpu.SemaphoreType.DMA((2,))],
        compiler_params=PARAMS,
        name="join",
    )(first, second, *afters)


def gather_shards(shard, count, afters):
    held, masks = shard, [0]
    bit = 1
    while 2 * bit < count:
        bit *= 2
    while bit:
        other = lax.ppermute(held, "col", [(i, i ^ bit) for i in range(count)])
        masks += [mask ^ bit for mask in masks]
        if bit > 1:
            held = join(held, other, afters[0])
            afters = afters[1:] or afters
        bit //= 2
    return held, other, masks


def local(row_count, col_count, matrix, panel_t, inverse_lower, pivot_rows):
    rows, cols = matrix.shape
    width = inverse_lower.shape[0]
    slot = width // row_count
    stay = width // 2
    me = lax.axis_index("row").astype(jnp.int32)
    column = lax.axis_index("col").astype(jnp.int32)
    here = me.reshape(1)
    pivot = pivot_rows.reshape(1, width)
    item_shape = jax.ShapeDtypeStruct((slot, cols), F32)

    rounds = plan(row_count)
    order = [item for moves in rounds for s, t, item in moves if s == 0]
    matrix = pltpu.with_memory_space_constraint(matrix, pltpu.HBM)
    pivot = pltpu.with_memory_space_constraint(pivot, pltpu.HBM)
    panel_t = pltpu.with_memory_space_constraint(panel_t, pltpu.HBM)
    inverse_lower = pltpu.with_memory_space_constraint(inverse_lower, pltpu.HBM)
    pieces = next(k for k in range(3, 0, -1) if rows % (16 * k) == 0 and width % (rows // k) == 0)
    *own, panel = pl.pallas_call(
        functools.partial(pick_kernel, row_count, order),
        out_shape=(item_shape,) * len(order) + (jax.ShapeDtypeStruct(panel_t.shape, F32),),
        in_specs=[SMEM, HBM, HBM, HBM],
        out_specs=(VMEM,) * (len(order) + 1),
        scratch_shapes=[
            pltpu.VMEM((rows, cols), F32),
            pltpu.VMEM((1, width), jnp.int32),
            pltpu.SemaphoreType.DMA((2 + pieces,)),
        ],
        compiler_params=PARAMS,
        name="pick",
    )(here, pivot, matrix, panel_t)

    arrays = list(own)
    found = [{} for _ in range(row_count)]
    for k, item in enumerate(order):
        found[0][item] = k
    for r in range(1, row_count):
        found[r]["pick", r] = 0
    operands, chunks = [], row_count // 2
    for moves in rounds:
        leaving = [item for s, t, item in moves if s == 0]
        operand = own[order.index(leaving[0])] if leaving else own[0]
        if len(operands) > chunks + 3 and all(item[0] == "stay" for s, t, item in moves):
            operand = arrays[len(own) + chunks]
        for s, t, item in moves:
            if s != 0 and item[0] == "stay":
                operand = jnp.where(me == s, arrays[found[s][item]], operand)
        for s, t, item in moves:
            found[t][item] = len(arrays)
        operands.append(operand)
        arrays.append(lax.ppermute(operand, "row", [(s, t) for s, t, item in moves]))
    received = arrays[len(own) :]
    blocks = [("pick", p) for p in range(chunks, row_count)]
    late_blocks = [("stay", c) for c in range(chunks)] + [("pick", p) for p in range(1, chunks)]
    soon = len(own) + chunks + 2
    places = [[found[r][item] for item in blocks] for r in range(row_count)]
    late = [
        [found[r].get(item) for item in late_blocks[:chunks] + [("moved", r)] + late_blocks[chunks:]]
        for r in range(row_count)
    ]
    soon_late = [[k if k is not None and k < soon else None for k in table] for table in late]
    late = [[k if k is not None and k >= soon else None for k in table] for table in late]
    late_rows = len(late_blocks) * slot

    picked_rows = len(blocks) * slot + late_rows
    inv_high, inv_low, land, base = pl.pallas_call(
        functools.partial(prepare_kernel, row_count),
        out_shape=(
            jax.ShapeDtypeStruct((width, picked_rows), BF16),
            jax.ShapeDtypeStruct((width, picked_rows), BF16),
            jax.ShapeDtypeStruct((rows, slot), BF16),
            jax.ShapeDtypeStruct((rows, cols), F32),
        ),
        in_specs=[SMEM, HBM, HBM, HBM],
        out_specs=(VMEM,) * 4,
        scratch_shapes=[
            pltpu.VMEM((1, width), jnp.int32),
            pltpu.VMEM((width, width), F32),
            pltpu.VMEM((rows, cols), F32),
            pltpu.SemaphoreType.DMA((3,)),
        ],
        compiler_params=PARAMS,
        cost_estimate=SHORT,
        name="prepare",
    )(here, pivot, inverse_lower, matrix)

    near, far, masks = gather_shards(panel, col_count, [operands[3:5] + [land], []])
    ids = column ^ jnp.array(masks, jnp.int32)

    def used(*tables):
        names = sorted({k for table in tables for k in jax.tree.leaves(table)})
        return [arrays[k] for k in names], [jax.tree.map(names.index, table) for table in tables]

    half = width // 2
    ends, near_high, near_low = pl.pallas_call(
        near_kernel,
        out_shape=(jax.ShapeDtypeStruct((rows, late_rows), F32),) + (jax.ShapeDtypeStruct((rows, half), BF16),) * 2,
        in_specs=[SMEM, SMEM] + [VMEM] * 3,
        out_specs=(VMEM,) * 3,
        scratch_shapes=[pltpu.VMEM((half, late_rows), F32)] * 2,
        compiler_params=PARAMS,
        name="near",
    )(here, ids, near, inv_high, inv_low)
    early_arrays, (places,) = used(places)
    upper = pl.pallas_call(
        functools.partial(upper_kernel, places),
        out_shape=jax.ShapeDtypeStruct((width, cols), F32),
        in_specs=[SMEM] + [VMEM] * (2 + len(early_arrays)) + [ANY],
        out_specs=VMEM,
        scratch_shapes=[pltpu.VMEM((picked_rows - late_rows, cols), BF16)] * 2,
        compiler_params=PARAMS,
        cost_estimate=LONG,
        name="upper",
    )(here, inv_high, inv_low, *early_arrays, ends)

    part, end_high, end_low = pl.pallas_call(
        far_kernel,
        out_shape=(jax.ShapeDtypeStruct((rows, cols), F32),)
        + (jax.ShapeDtypeStruct((rows, late_rows + slot), BF16),) * 2,
        in_specs=[SMEM, SMEM] + [VMEM] * 9,
        out_specs=(VMEM,) * 3,
        scratch_shapes=[pltpu.VMEM((rows, half), BF16)] * 2
        + [pltpu.VMEM((half, cols + late_rows), F32)] * 2
        + [pltpu.VMEM((half, cols), F32)] * 2,
        compiler_params=PARAMS,
        name="far",
    )(here, ids, far, inv_high, inv_low, upper, base, ends, land, near_high, near_low)

    row_scratch = [pltpu.VMEM((late_rows + slot, cols), BF16)] * 2
    soon_arrays, (soon_late,) = used(soon_late)
    part = pl.pallas_call(
        functools.partial(middle_kernel, soon_late),
        out_shape=jax.ShapeDtypeStruct((rows, cols), F32),
        in_specs=[SMEM] + [VMEM] * (3 + len(soon_arrays)),
        out_specs=VMEM,
        scratch_shapes=row_scratch,
        compiler_params=PARAMS,
        name="middle",
    )(here, part, end_high, end_low, *soon_arrays)

    late_arrays, (late,) = used(late)
    steps = STEPS if rows % (STEPS * 16) == 0 else 1
    return pl.pallas_call(
        functools.partial(finish_kernel, late),
        out_shape=jax.ShapeDtypeStruct((rows, cols), F32),
        in_specs=[SMEM] + [VMEM] * (3 + len(late_arrays)),
        out_specs=HBM,
        scratch_shapes=row_scratch + [pltpu.VMEM((rows, cols), F32), pltpu.SemaphoreType.DMA((steps,))],
        compiler_params=PARAMS,
        name="finish",
    )(here, part, end_high, end_low, *late_arrays)


def solution(mesh):
    in_specs = (P("row", "col"), P("col", "row"), P(), P())
    out_specs = P("row", "col")
    return jax.shard_map(
        functools.partial(local, mesh.shape["row"], mesh.shape["col"]),
        mesh=mesh,
        in_specs=in_specs,
        out_specs=out_specs,
        check_vma=False,
    )
```

```python
import functools

import jax
import jax.numpy as jnp
from jax import lax
from jax.experimental import pallas as pl
from jax.experimental.pallas import tpu as pltpu
from jax.sharding import PartitionSpec as P

F32 = jnp.float32
BF16 = jnp.bfloat16
STEPS = 3
VMEM = pl.BlockSpec(memory_space=pltpu.VMEM)
SMEM = pl.BlockSpec(memory_space=pltpu.SMEM)
ANY = pl.BlockSpec(memory_space=pl.ANY)
HBM = pl.BlockSpec(memory_space=pltpu.HBM)
SHORT = pl.CostEstimate(flops=1_000_000, transcendentals=0, bytes_accessed=100_000)
LONG = pl.CostEstimate(flops=40_000_000_000, transcendentals=0, bytes_accessed=100_000_000)
PARAMS = pltpu.CompilerParams(vmem_limit_bytes=20 * 1024 * 1024)


def halves(x):
    high = x.astype(BF16)
    low = (x - high.astype(F32)).astype(BF16)
    return high, low


def mm(a, b):
    return jnp.dot(a, b, preferred_element_type=F32)


def mm_nt(a, b):
    return lax.dot_general(a, b, (((1,), (1,)), ((), ())), preferred_element_type=F32)


def mm_tn(a, b):
    return lax.dot_general(a, b, (((0,), (0,)), ((), ())), preferred_element_type=F32)


def classify(pivot, count, rows):
    width = pivot.shape[1]
    lanes = lax.broadcasted_iota(jnp.int32, (1, width), 1)
    kind = jnp.where(pivot != lanes, pivot // rows, 0)
    padded = -(-count // 16) * 16
    owner = lax.broadcasted_iota(jnp.int32, (padded, width), 0)
    member = owner == kind
    before = lax.broadcasted_iota(jnp.int32, (width, width), 0) < lax.broadcasted_iota(
        jnp.int32, (width, width), 1
    )
    ranks = mm(member.astype(BF16), before.astype(BF16))
    place = jnp.sum(jnp.where(member, ranks, 0.0), axis=0, keepdims=True)
    return kind, place.astype(jnp.int32)


def one_hot(position, slots):
    slot = lax.broadcasted_iota(jnp.int32, (slots, position.shape[1]), 0)
    return (slot == position).astype(BF16)


def picked(pick, rows_ref, copies):
    step = rows_ref.shape[0] // len(copies)
    total = None
    for k in range(pick.shape[1] // step):
        copies[k].wait()
        high, low = halves(rows_ref[k * step : (k + 1) * step, :])
        part = pick[:, k * step : (k + 1) * step]
        value = mm(part, low) + mm(part, high)
        total = value if total is None else total + value
    return total


def plan(count):
    middle, chunks = count // 2, count // 2
    first = [(0, middle, ("stay", c)) for c in range(chunks)]
    relays = []
    for c in range(chunks):
        for k in range(1, count):
            step = [(middle + k - 1, middle + k, ("stay", c)), (middle - k + 1, middle - k, ("stay", c))]
            relays += [move for move in (step if c + 1 < chunks else step[::-1]) if 0 < move[1] < count]
    early = [(s, t, ("pick", s)) for t in range(1, count) for s in range(middle, count) if t not in (s, middle)]
    early += [(s, 0, ("pick", s)) for s in range(1, middle)]
    late = [(s, t, ("pick", s)) for s in range(1, middle) for t in range(middle + 1, count)]
    late += [(0, t, ("moved", t)) for t in range(1, count)]
    late += [(s, middle, ("pick", s)) for s in range(middle + 1, count)]
    late += [(s, 0, ("pick", s)) for s in range(middle, count)]
    last = [(s, t, ("pick", s)) for s in range(1, middle) for t in range(1, middle + 1) if s != t]
    ready = {(0, ("stay", c)): 0 for c in range(chunks)}
    rounds = []
    while first or relays or early or late or last:
        now, senders, targets = [], set(), set()
        queues = [first, relays, early] + [late] * (len(rounds) >= chunks) + [last] * (len(rounds) > chunks + 2)
        for queue in queues:
            for move in list(queue):
                s, t, item = move
                known = item[0] != "stay" or ready.get((s, item), len(rounds) + 1) <= len(rounds)
                if known and s not in senders and t not in targets:
                    now.append(move)
                    senders.add(s)
                    targets.add(t)
                    queue.remove(move)
        for s, t, item in now:
            ready[t, item] = len(rounds) + 3
        rounds.append(now)
    return rounds


def pick_kernel(count, order, me_ref, pivot_ref, matrix_ref, panel_ref, *refs):
    outs, (panel_out, rows_ref, pivot_v, sem) = refs[:-4], refs[-4:]
    rows, cols = matrix_ref.shape
    width = pivot_ref.shape[1]
    slot = width // count
    me = me_ref[0]
    point = pltpu.make_async_copy(pivot_ref, pivot_v, sem.at[0])
    panel = pltpu.make_async_copy(panel_ref, panel_out, sem.at[1])
    step = rows // (sem.shape[0] - 2)
    copies = [
        pltpu.make_async_copy(matrix_ref.at[pl.ds(k * step, step)], rows_ref.at[pl.ds(k * step, step)], sem.at[2 + k])
        for k in range(rows // step)
    ]
    point.start()
    for copy in copies:
        copy.start()
    panel.start()
    point.wait()
    pivot = pivot_v[...]
    kind, place = classify(pivot, count, rows)

    @pl.when(me == 0)
    def _():
        start = jnp.full(kind.shape, -count * width, jnp.int32)
        for k, (name, which) in enumerate(order):
            if name == "moved":
                start = jnp.where(kind == which, k * slot, start)
            else:
                inside = (kind == 0) & (place >= which * slot) & (place < (which + 1) * slot)
                start = jnp.where(inside, (k - which) * slot, start)
        got = picked(one_hot(start + place, len(order) * slot), rows_ref, copies)
        for k, out in enumerate(outs):
            out[...] = got[k * slot : (k + 1) * slot, :]
        for copy in copies[width // step :]:
            copy.wait()

    @pl.when(me != 0)
    def _():
        mine = lax.broadcasted_iota(jnp.int32, (slot, width), 0) == jnp.where(kind == me, place, -1)
        source = jnp.sum(jnp.where(mine, pivot - me * rows, 0), axis=1, keepdims=True)
        pick = (lax.broadcasted_iota(jnp.int32, (slot, rows), 1) == source).astype(BF16)
        got = picked(pick, rows_ref, copies)
        for out in outs:
            out[...] = got

    panel.wait()


def prepare_kernel(count, me_ref, pivot_ref, inverse_ref, matrix_ref, *refs):
    high_ref, low_ref, land_ref, base_ref, pivot_v, inv_ref, rows_ref, sem = refs[-8:]
    rows, cols = matrix_ref.shape
    width = pivot_ref.shape[1]
    slot = width // count
    stay = width // 2
    me = me_ref[0]
    copies = [
        pltpu.make_async_copy(pivot_ref, pivot_v, sem.at[0]),
        pltpu.make_async_copy(inverse_ref, inv_ref, sem.at[1]),
        pltpu.make_async_copy(matrix_ref, rows_ref, sem.at[2]),
    ]
    for copy in copies:
        copy.start()
    copies[0].wait()
    pivot = pivot_v[...]
    kind, place = classify(pivot, count, rows)
    total = high_ref.shape[1]
    middle = count // 2
    start = jnp.where(kind == 0, (count - middle) * slot, stay + (kind + count - middle - 1) * slot)
    spread = one_hot(place + jnp.where(kind < middle, start, (kind - middle) * slot), total)
    mine = (kind == me) & (kind != 0)
    landing = lax.broadcasted_iota(jnp.int32, (rows, width), 0) == jnp.where(mine, pivot - me * rows, -1)
    land = mm_nt(landing.astype(BF16), one_hot(jnp.where(mine, place, -1), slot))
    land_ref[...] = land.astype(BF16)
    taken = jnp.sum(land, axis=1, keepdims=True)
    copies[1].wait()
    inv_high, inv_low = halves(inv_ref[...])
    high_ref[...] = mm_nt(inv_high, spread).astype(BF16)
    low_ref[...] = mm_nt(inv_low, spread).astype(BF16)
    copies[2].wait()
    base_ref[...] = jnp.where(taken > 0.5, 0.0, rows_ref[...])


def turn(shards_ref, start, high_ref, low_ref):
    high, low = halves(-shards_ref[:, start:])
    high_ref[start:, :] = high.T
    low_ref[start:, :] = low.T


def near_kernel(me_ref, ids_ref, shards_ref, inv_high, inv_low, ends_ref, high_ref, low_ref, side_high, side_low):
    half, rows = shards_ref.shape
    width = inv_high.shape[0]
    depth = width // ids_ref.shape[0]
    first = inv_high.shape[1] - side_high.shape[1]
    for k in range(half // depth):
        source = pl.ds(pl.multiple_of(ids_ref[k] * depth, depth), depth)
        part = pl.ds(k * depth, depth)
        side_high[part, :] = inv_high[source, first:].astype(F32)
        side_low[part, :] = inv_low[source, first:].astype(F32)

    def work(start):
        turn(shards_ref, start, high_ref, low_ref)
        high, right = high_ref[start:, :], side_high[...].astype(BF16)
        ends_ref[start:, :] = mm(low_ref[start:, :], right) + mm(high, side_low[...].astype(BF16)) + mm(high, right)

    pl.when(me_ref[0] == 0)(lambda: work(width))
    pl.when(me_ref[0] != 0)(lambda: work(0))


def far_kernel(me_ref, ids_ref, shards_ref, inv_high, inv_low, upper_ref, rows_ref, ends_ref, land_ref, *refs):
    near_high, near_low, out_ref, end_high, end_low, high_ref, low_ref = refs[:7]
    side_high, side_low, up_high, up_low = refs[7:]
    half, rows = shards_ref.shape
    width, cols = upper_ref.shape
    depth = width // ids_ref.shape[0]
    first = inv_high.shape[1] - (side_high.shape[1] - cols)
    stay, slot = width // 2, land_ref.shape[1]
    for k in range(width // depth):
        source = pl.ds(pl.multiple_of(ids_ref[k] * depth, depth), depth)
        high, low = halves(upper_ref[source, :])
        part = pl.ds(k * depth % half, depth)
        if k * depth < half:
            up_high[part, :], up_low[part, :] = high.astype(F32), low.astype(F32)
        else:
            side_high[part, :cols], side_low[part, :cols] = high.astype(F32), low.astype(F32)
            side_high[part, cols:] = inv_high[source, first:].astype(F32)
            side_low[part, cols:] = inv_low[source, first:].astype(F32)

    def work(start):
        turn(shards_ref, start, high_ref, low_ref)
        high, right = high_ref[start:, :], side_high[...].astype(BF16)
        value = mm(low_ref[start:, :], right) + mm(high, side_low[...].astype(BF16)) + mm(high, right)
        high, right = near_high[start:, :], up_high[...].astype(BF16)
        near = mm(near_low[start:, :], right) + mm(high, up_low[...].astype(BF16)) + mm(high, right)
        out_ref[start:, :] = rows_ref[start:, :] + (near + value[:, :cols])
        high, low = halves(ends_ref[start:, :] + value[:, cols:])
        put(end_high, start, high)
        put(end_low, start, low)

    def put(end, start, columns):
        part = pl.ds(start, columns.shape[0])
        end[part, :stay] = columns[:, :stay]
        end[part, stay + slot :] = columns[:, stay:]

    @pl.when(me_ref[0] == 0)
    def _():
        work(width)
        out_ref[:width, :] = upper_ref[...]
        put(end_high, 0, inv_high[:, first:])
        put(end_low, 0, inv_low[:, first:])

    pl.when(me_ref[0] != 0)(lambda: work(0))
    end_high[:, stay : stay + slot] = land_ref[...]
    end_low[:, stay : stay + slot] = jnp.zeros(land_ref.shape, BF16)


def collect(places, me, arrays, row_high, row_low):
    slot, cols = arrays[0].shape
    for r in range(len(places)):

        @pl.when(me == r)
        def _(r=r):
            for block, k in enumerate(places[r]):
                part = pl.ds(block * slot, slot)
                if k is None:
                    row_high[part, :] = jnp.zeros((slot, cols), BF16)
                    row_low[part, :] = jnp.zeros((slot, cols), BF16)
                else:
                    row_high[part, :], row_low[part, :] = halves(arrays[k][...])


def upper_kernel(places, me_ref, high_ref, low_ref, *refs):
    arrays, (out_ref, row_high, row_low) = refs[:-4], refs[-3:]
    collect(places, me_ref[0], arrays, row_high, row_low)
    depth = row_high.shape[0]
    high = high_ref[:, :depth]
    out_ref[...] = mm(low_ref[:, :depth], row_high[...]) + mm(high, row_low[...]) + mm(high, row_high[...])


def share(places, me, part_ref, high_ref, low_ref, arrays, row_high, row_low, give):
    slot, cols = arrays[0].shape
    rows = part_ref.shape[0]
    step = rows // STEPS if rows % (STEPS * 16) == 0 else rows
    for r, table in enumerate(places):

        @pl.when(me == r)
        def _(table=table):
            here = [block for block, k in enumerate(table) if k is not None]
            span = pl.ds(here[0] * slot, (here[-1] + 1 - here[0]) * slot) if here else None
            for block in range(here[0], here[-1] + 1) if here else ():
                part = pl.ds(block * slot, slot)
                if table[block] is None:
                    row_high[part, :] = jnp.zeros((slot, cols), BF16)
                    row_low[part, :] = jnp.zeros((slot, cols), BF16)
                else:
                    row_high[part, :], row_low[part, :] = halves(arrays[table[block]][...])
            for k in range(rows // step):
                part = pl.ds(k * step, step)
                value = part_ref[part, :]
                if here:
                    high = high_ref[part, span]
                    more = mm(low_ref[part, span], row_high[span, :]) + mm(high, row_low[span, :])
                    value = value + (more + mm(high, row_high[span, :]))
                give(k, part, value)


def middle_kernel(places, me_ref, part_ref, high_ref, low_ref, *refs):
    arrays, (out_ref, row_high, row_low) = refs[:-3], refs[-3:]

    def give(k, part, value):
        out_ref[part, :] = value

    share(places, me_ref[0], part_ref, high_ref, low_ref, arrays, row_high, row_low, give)


def finish_kernel(places, me_ref, part_ref, high_ref, low_ref, *refs):
    arrays, (out_ref, row_high, row_low, total, sem) = refs[:-5], refs[-5:]

    def copy(k, part):
        return pltpu.make_async_copy(total.at[part], out_ref.at[part], sem.at[k])

    def give(k, part, value):
        total[part, :] = value
        copy(k, part).start()

    share(places, me_ref[0], part_ref, high_ref, low_ref, arrays, row_high, row_low, give)
    step = total.shape[0] // sem.shape[0]
    for k in range(sem.shape[0]):
        copy(k, pl.ds(k * step, step)).wait()


def join_kernel(first, second, *refs):
    out, sem = refs[-2:]
    rows = first.shape[0]
    copies = [
        pltpu.make_async_copy(first, out.at[:rows], sem.at[0]),
        pltpu.make_async_copy(second, out.at[rows:], sem.at[1]),
    ]
    for copy in copies:
        copy.start()
    for copy in copies:
        copy.wait()


def join(first, second, afters):
    rows, cols = first.shape
    return pl.pallas_call(
        join_kernel,
        out_shape=jax.ShapeDtypeStruct((2 * rows, cols), first.dtype),
        in_specs=[VMEM, VMEM] + [ANY] * len(afters),
        out_specs=VMEM,
        scratch_shapes=[pltpu.SemaphoreType.DMA((2,))],
        compiler_params=PARAMS,
        name="join",
    )(first, second, *afters)


def gather_shards(shard, count, afters):
    held, masks = shard, [0]
    bit = 1
    while 2 * bit < count:
        bit *= 2
    while bit:
        other = lax.ppermute(held, "col", [(i, i ^ bit) for i in range(count)])
        masks += [mask ^ bit for mask in masks]
        if bit > 1:
            held = join(held, other, afters[0])
            afters = afters[1:] or afters
        bit //= 2
    return held, other, masks


def local(row_count, col_count, matrix, panel_t, inverse_lower, pivot_rows):
    rows, cols = matrix.shape
    width = inverse_lower.shape[0]
    slot = width // row_count
    stay = width // 2
    me = lax.axis_index("row").astype(jnp.int32)
    column = lax.axis_index("col").astype(jnp.int32)
    here = me.reshape(1)
    pivot = pivot_rows.reshape(1, width)
    item_shape = jax.ShapeDtypeStruct((slot, cols), F32)

    rounds = plan(row_count)
    order = [item for moves in rounds for s, t, item in moves if s == 0]
    matrix = pltpu.with_memory_space_constraint(matrix, pltpu.HBM)
    pivot = pltpu.with_memory_space_constraint(pivot, pltpu.HBM)
    panel_t = pltpu.with_memory_space_constraint(panel_t, pltpu.HBM)
    inverse_lower = pltpu.with_memory_space_constraint(inverse_lower, pltpu.HBM)
    pieces = next(k for k in range(3, 0, -1) if rows % (16 * k) == 0 and width % (rows // k) == 0)
    *own, panel = pl.pallas_call(
        functools.partial(pick_kernel, row_count, order),
        out_shape=(item_shape,) * len(order) + (jax.ShapeDtypeStruct(panel_t.shape, F32),),
        in_specs=[SMEM, HBM, HBM, HBM],
        out_specs=(VMEM,) * (len(order) + 1),
        scratch_shapes=[
            pltpu.VMEM((rows, cols), F32),
            pltpu.VMEM((1, width), jnp.int32),
            pltpu.SemaphoreType.DMA((2 + pieces,)),
        ],
        compiler_params=PARAMS,
        name="pick",
    )(here, pivot, matrix, panel_t)

    arrays = list(own)
    found = [{} for _ in range(row_count)]
    for k, item in enumerate(order):
        found[0][item] = k
    for r in range(1, row_count):
        found[r]["pick", r] = 0
    operands, chunks = [], row_count // 2
    for moves in rounds:
        leaving = [item for s, t, item in moves if s == 0]
        operand = own[order.index(leaving[0])] if leaving else own[0]
        if len(operands) > chunks + 3 and all(item[0] == "stay" for s, t, item in moves):
            operand = arrays[len(own) + chunks]
        for s, t, item in moves:
            if s != 0 and item[0] == "stay":
                operand = jnp.where(me == s, arrays[found[s][item]], operand)
        for s, t, item in moves:
            found[t][item] = len(arrays)
        operands.append(operand)
        arrays.append(lax.ppermute(operand, "row", [(s, t) for s, t, item in moves]))
    received = arrays[len(own) :]
    blocks = [("pick", p) for p in range(chunks, row_count)]
    late_blocks = [("stay", c) for c in range(chunks)] + [("pick", p) for p in range(1, chunks)]
    soon = len(own) + chunks + 2
    places = [[found[r][item] for item in blocks] for r in range(row_count)]
    late = [
        [found[r].get(item) for item in late_blocks[:chunks] + [("moved", r)] + late_blocks[chunks:]]
        for r in range(row_count)
    ]
    soon_late = [[k if k is not None and k < soon else None for k in table] for table in late]
    late = [[k if k is not None and k >= soon else None for k in table] for table in late]
    late_rows = len(late_blocks) * slot

    picked_rows = len(blocks) * slot + late_rows
    inv_high, inv_low, land, base = pl.pallas_call(
        functools.partial(prepare_kernel, row_count),
        out_shape=(
            jax.ShapeDtypeStruct((width, picked_rows), BF16),
            jax.ShapeDtypeStruct((width, picked_rows), BF16),
            jax.ShapeDtypeStruct((rows, slot), BF16),
            jax.ShapeDtypeStruct((rows, cols), F32),
        ),
        in_specs=[SMEM, HBM, HBM, HBM],
        out_specs=(VMEM,) * 4,
        scratch_shapes=[
            pltpu.VMEM((1, width), jnp.int32),
            pltpu.VMEM((width, width), F32),
            pltpu.VMEM((rows, cols), F32),
            pltpu.SemaphoreType.DMA((3,)),
        ],
        compiler_params=PARAMS,
        cost_estimate=SHORT,
        name="prepare",
    )(here, pivot, inverse_lower, matrix)

    near, far, masks = gather_shards(panel, col_count, [operands[3:5] + [land], []])
    ids = column ^ jnp.array(masks, jnp.int32)

    def used(*tables):
        names = sorted({k for table in tables for k in jax.tree.leaves(table)})
        return [arrays[k] for k in names], [jax.tree.map(names.index, table) for table in tables]

    half = width // 2
    ends, near_high, near_low = pl.pallas_call(
        near_kernel,
        out_shape=(jax.ShapeDtypeStruct((rows, late_rows), F32),) + (jax.ShapeDtypeStruct((rows, half), BF16),) * 2,
        in_specs=[SMEM, SMEM] + [VMEM] * 3,
        out_specs=(VMEM,) * 3,
        scratch_shapes=[pltpu.VMEM((half, late_rows), F32)] * 2,
        compiler_params=PARAMS,
        name="near",
    )(here, ids, near, inv_high, inv_low)
    early_arrays, (places,) = used(places)
    upper = pl.pallas_call(
        functools.partial(upper_kernel, places),
        out_shape=jax.ShapeDtypeStruct((width, cols), F32),
        in_specs=[SMEM] + [VMEM] * (2 + len(early_arrays)) + [ANY],
        out_specs=VMEM,
        scratch_shapes=[pltpu.VMEM((picked_rows - late_rows, cols), BF16)] * 2,
        compiler_params=PARAMS,
        cost_estimate=LONG,
        name="upper",
    )(here, inv_high, inv_low, *early_arrays, ends)

    part, end_high, end_low = pl.pallas_call(
        far_kernel,
        out_shape=(jax.ShapeDtypeStruct((rows, cols), F32),)
        + (jax.ShapeDtypeStruct((rows, late_rows + slot), BF16),) * 2,
        in_specs=[SMEM, SMEM] + [VMEM] * 9,
        out_specs=(VMEM,) * 3,
        scratch_shapes=[pltpu.VMEM((rows, half), BF16)] * 2
        + [pltpu.VMEM((half, cols + late_rows), F32)] * 2
        + [pltpu.VMEM((half, cols), F32)] * 2,
        compiler_params=PARAMS,
        name="far",
    )(here, ids, far, inv_high, inv_low, upper, base, ends, land, near_high, near_low)

    row_scratch = [pltpu.VMEM((late_rows + slot, cols), BF16)] * 2
    soon_arrays, (soon_late,) = used(soon_late)
    part = pl.pallas_call(
        functools.partial(middle_kernel, soon_late),
        out_shape=jax.ShapeDtypeStruct((rows, cols), F32),
        in_specs=[SMEM] + [VMEM] * (3 + len(soon_arrays)),
        out_specs=VMEM,
        scratch_shapes=row_scratch,
        compiler_params=PARAMS,
        name="middle",
    )(here, part, end_high, end_low, *soon_arrays)

    late_arrays, (late,) = used(late)
    steps = STEPS if rows % (STEPS * 16) == 0 else 1
    return pl.pallas_call(
        functools.partial(finish_kernel, late),
        out_shape=jax.ShapeDtypeStruct((rows, cols), F32),
        in_specs=[SMEM] + [VMEM] * (3 + len(late_arrays)),
        out_specs=HBM,
        scratch_shapes=row_scratch + [pltpu.VMEM((rows, cols), F32), pltpu.SemaphoreType.DMA((steps,))],
        compiler_params=PARAMS,
        name="finish",
    )(here, part, end_high, end_low, *late_arrays)


def solution(mesh):
    in_specs = (P("row", "col"), P("col", "row"), P(), P())
    out_specs = P("row", "col")
    return jax.shard_map(
        functools.partial(local, mesh.shape["row"], mesh.shape["col"]),
        mesh=mesh,
        in_specs=in_specs,
        out_specs=out_specs,
        check_vma=False,
    )
```

```python
import functools

import jax
import jax.numpy as jnp
from jax import lax
from jax.experimental import pallas as pl
from jax.experimental.pallas import tpu as pltpu
from jax.sharding import PartitionSpec as P

F32 = jnp.float32
BF16 = jnp.bfloat16
STEPS = 3
VMEM = pl.BlockSpec(memory_space=pltpu.VMEM)
SMEM = pl.BlockSpec(memory_space=pltpu.SMEM)
ANY = pl.BlockSpec(memory_space=pl.ANY)
HBM = pl.BlockSpec(memory_space=pltpu.HBM)
SHORT = pl.CostEstimate(flops=1_000_000, transcendentals=0, bytes_accessed=100_000)
LONG = pl.CostEstimate(flops=40_000_000_000, transcendentals=0, bytes_accessed=100_000_000)
PARAMS = pltpu.CompilerParams(vmem_limit_bytes=20 * 1024 * 1024)


def halves(x):
    high = x.astype(BF16)
    low = (x - high.astype(F32)).astype(BF16)
    return high, low


def mm(a, b):
    return jnp.dot(a, b, preferred_element_type=F32)


def mm_nt(a, b):
    return lax.dot_general(a, b, (((1,), (1,)), ((), ())), preferred_element_type=F32)


def mm_tn(a, b):
    return lax.dot_general(a, b, (((0,), (0,)), ((), ())), preferred_element_type=F32)


def classify(pivot, count, rows):
    width = pivot.shape[1]
    lanes = lax.broadcasted_iota(jnp.int32, (1, width), 1)
    kind = jnp.where(pivot != lanes, pivot // rows, 0)
    padded = -(-count // 16) * 16
    owner = lax.broadcasted_iota(jnp.int32, (padded, width), 0)
    member = owner == kind
    before = lax.broadcasted_iota(jnp.int32, (width, width), 0) < lax.broadcasted_iota(
        jnp.int32, (width, width), 1
    )
    ranks = mm(member.astype(BF16), before.astype(BF16))
    place = jnp.sum(jnp.where(member, ranks, 0.0), axis=0, keepdims=True)
    return kind, place.astype(jnp.int32)


def one_hot(position, slots):
    slot = lax.broadcasted_iota(jnp.int32, (slots, position.shape[1]), 0)
    return (slot == position).astype(BF16)


def picked(pick, rows_ref, copies):
    step = rows_ref.shape[0] // len(copies)
    total = None
    for k in range(pick.shape[1] // step):
        copies[k].wait()
        high, low = halves(rows_ref[k * step : (k + 1) * step, :])
        part = pick[:, k * step : (k + 1) * step]
        value = mm(part, low) + mm(part, high)
        total = value if total is None else total + value
    return total


def plan(count):
    middle, chunks = count // 2, count // 2
    first = [(0, middle, ("stay", c)) for c in range(chunks)]
    relays = []
    for c in range(chunks):
        for k in range(1, count):
            step = [(middle + k - 1, middle + k, ("stay", c)), (middle - k + 1, middle - k, ("stay", c))]
            relays += [move for move in (step if c + 1 < chunks else step[::-1]) if 0 < move[1] < count]
    early = [(s, t, ("pick", s)) for t in range(1, count) for s in range(middle, count) if t not in (s, middle)]
    early += [(s, 0, ("pick", s)) for s in range(1, middle)]
    late = [(s, t, ("pick", s)) for s in range(1, middle) for t in range(middle + 1, count)]
    late += [(0, t, ("moved", t)) for t in range(1, count)]
    late += [(s, middle, ("pick", s)) for s in range(middle + 1, count)]
    late += [(s, 0, ("pick", s)) for s in range(middle, count)]
    last = [(s, t, ("pick", s)) for s in range(1, middle) for t in range(1, middle + 1) if s != t]
    ready = {(0, ("stay", c)): 0 for c in range(chunks)}
    rounds = []
    while first or relays or early or late or last:
        now, senders, targets = [], set(), set()
        queues = [first, relays, early] + [late] * (len(rounds) >= chunks) + [last] * (len(rounds) > chunks + 2)
        for queue in queues:
            for move in list(queue):
                s, t, item = move
                known = item[0] != "stay" or ready.get((s, item), len(rounds) + 1) <= len(rounds)
                if known and s not in senders and t not in targets:
                    now.append(move)
                    senders.add(s)
                    targets.add(t)
                    queue.remove(move)
        for s, t, item in now:
            ready[t, item] = len(rounds) + 3
        rounds.append(now)
    return rounds


def pick_kernel(count, order, me_ref, pivot_ref, matrix_ref, panel_ref, *refs):
    outs, (panel_out, rows_ref, pivot_v, sem) = refs[:-4], refs[-4:]
    rows, cols = matrix_ref.shape
    width = pivot_ref.shape[1]
    slot = width // count
    me = me_ref[0]
    point = pltpu.make_async_copy(pivot_ref, pivot_v, sem.at[0])
    panel = pltpu.make_async_copy(panel_ref, panel_out, sem.at[1])
    step = rows // (sem.shape[0] - 2)
    copies = [
        pltpu.make_async_copy(matrix_ref.at[pl.ds(k * step, step)], rows_ref.at[pl.ds(k * step, step)], sem.at[2 + k])
        for k in range(rows // step)
    ]
    point.start()
    for copy in copies:
        copy.start()
    panel.start()
    point.wait()
    pivot = pivot_v[...]
    kind, place = classify(pivot, count, rows)

    @pl.when(me == 0)
    def _():
        start = jnp.full(kind.shape, -count * width, jnp.int32)
        for k, (name, which) in enumerate(order):
            if name == "moved":
                start = jnp.where(kind == which, k * slot, start)
            else:
                inside = (kind == 0) & (place >= which * slot) & (place < (which + 1) * slot)
                start = jnp.where(inside, (k - which) * slot, start)
        got = picked(one_hot(start + place, len(order) * slot), rows_ref, copies)
        for k, out in enumerate(outs):
            out[...] = got[k * slot : (k + 1) * slot, :]
        for copy in copies[width // step :]:
            copy.wait()

    @pl.when(me != 0)
    def _():
        mine = lax.broadcasted_iota(jnp.int32, (slot, width), 0) == jnp.where(kind == me, place, -1)
        source = jnp.sum(jnp.where(mine, pivot - me * rows, 0), axis=1, keepdims=True)
        pick = (lax.broadcasted_iota(jnp.int32, (slot, rows), 1) == source).astype(BF16)
        got = picked(pick, rows_ref, copies)
        for out in outs:
            out[...] = got

    panel.wait()


def prepare_kernel(count, me_ref, pivot_ref, inverse_ref, matrix_ref, *refs):
    high_ref, low_ref, land_ref, pivot_v, inv_ref, sem = refs[-6:]
    rows, cols = matrix_ref.shape
    width = pivot_ref.shape[1]
    slot = width // count
    stay = width // 2
    me = me_ref[0]
    copies = [
        pltpu.make_async_copy(pivot_ref, pivot_v, sem.at[0]),
        pltpu.make_async_copy(inverse_ref, inv_ref, sem.at[1]),
    ]
    for copy in copies:
        copy.start()
    copies[0].wait()
    pivot = pivot_v[...]
    kind, place = classify(pivot, count, rows)
    total = high_ref.shape[1]
    middle = count // 2
    start = jnp.where(kind == 0, (count - middle) * slot, stay + (kind + count - middle - 1) * slot)
    spread = one_hot(place + jnp.where(kind < middle, start, (kind - middle) * slot), total)
    mine = (kind == me) & (kind != 0)
    landing = lax.broadcasted_iota(jnp.int32, (rows, width), 0) == jnp.where(mine, pivot - me * rows, -1)
    land = mm_nt(landing.astype(BF16), one_hot(jnp.where(mine, place, -1), slot))
    land_ref[...] = land.astype(BF16)
    copies[1].wait()
    inv_high, inv_low = halves(inv_ref[...])
    high_ref[...] = mm_nt(inv_high, spread).astype(BF16)
    low_ref[...] = mm_nt(inv_low, spread).astype(BF16)


def turn(shards_ref, start, high_ref, low_ref):
    high, low = halves(-shards_ref[:, start:])
    high_ref[start:, :] = high.T
    low_ref[start:, :] = low.T


def near_kernel(me_ref, ids_ref, shards_ref, inv_high, inv_low, ends_ref, high_ref, low_ref, side_high, side_low):
    half, rows = shards_ref.shape
    width = inv_high.shape[0]
    depth = width // ids_ref.shape[0]
    first = inv_high.shape[1] - side_high.shape[1]
    for k in range(half // depth):
        source = pl.ds(pl.multiple_of(ids_ref[k] * depth, depth), depth)
        part = pl.ds(k * depth, depth)
        side_high[part, :] = inv_high[source, first:].astype(F32)
        side_low[part, :] = inv_low[source, first:].astype(F32)

    def work(start):
        turn(shards_ref, start, high_ref, low_ref)
        high, right = high_ref[start:, :], side_high[...].astype(BF16)
        ends_ref[start:, :] = mm(low_ref[start:, :], right) + mm(high, side_low[...].astype(BF16)) + mm(high, right)

    pl.when(me_ref[0] == 0)(lambda: work(width))
    pl.when(me_ref[0] != 0)(lambda: work(0))


def far_kernel(me_ref, ids_ref, shards_ref, inv_high, inv_low, upper_ref, matrix_ref, ends_ref, land_ref, *refs):
    near_high, near_low, out_ref, end_high, end_low, high_ref, low_ref = refs[:7]
    side_high, side_low, up_high, up_low = refs[7:-2]
    rows_ref, sem = refs[-2:]
    fetch = pltpu.make_async_copy(matrix_ref, rows_ref, sem)
    fetch.start()
    half, rows = shards_ref.shape
    width, cols = upper_ref.shape
    depth = width // ids_ref.shape[0]
    first = inv_high.shape[1] - (side_high.shape[1] - cols)
    stay, slot = width // 2, land_ref.shape[1]
    for k in range(width // depth):
        source = pl.ds(pl.multiple_of(ids_ref[k] * depth, depth), depth)
        high, low = halves(upper_ref[source, :])
        part = pl.ds(k * depth % half, depth)
        if k * depth < half:
            up_high[part, :], up_low[part, :] = high.astype(F32), low.astype(F32)
        else:
            side_high[part, :cols], side_low[part, :cols] = high.astype(F32), low.astype(F32)
            side_high[part, cols:] = inv_high[source, first:].astype(F32)
            side_low[part, cols:] = inv_low[source, first:].astype(F32)

    fetch.wait()

    def work(start):
        turn(shards_ref, start, high_ref, low_ref)
        high, right = high_ref[start:, :], side_high[...].astype(BF16)
        value = mm(low_ref[start:, :], right) + mm(high, side_low[...].astype(BF16)) + mm(high, right)
        high, right = near_high[start:, :], up_high[...].astype(BF16)
        near = mm(near_low[start:, :], right) + mm(high, up_low[...].astype(BF16)) + mm(high, right)
        taken = jnp.sum(land_ref[start:, :].astype(F32), axis=1, keepdims=True)
        kept = jnp.where(taken > 0.5, 0.0, rows_ref[start:, :])
        out_ref[start:, :] = kept + (near + value[:, :cols])
        high, low = halves(ends_ref[start:, :] + value[:, cols:])
        put(end_high, start, high)
        put(end_low, start, low)

    def put(end, start, columns):
        part = pl.ds(start, columns.shape[0])
        end[part, :stay] = columns[:, :stay]
        end[part, stay + slot :] = columns[:, stay:]

    @pl.when(me_ref[0] == 0)
    def _():
        work(width)
        out_ref[:width, :] = upper_ref[...]
        put(end_high, 0, inv_high[:, first:])
        put(end_low, 0, inv_low[:, first:])

    pl.when(me_ref[0] != 0)(lambda: work(0))
    end_high[:, stay : stay + slot] = land_ref[...]
    end_low[:, stay : stay + slot] = jnp.zeros(land_ref.shape, BF16)


def collect(places, me, arrays, row_high, row_low):
    slot, cols = arrays[0].shape
    for r in range(len(places)):

        @pl.when(me == r)
        def _(r=r):
            for block, k in enumerate(places[r]):
                part = pl.ds(block * slot, slot)
                if k is None:
                    row_high[part, :] = jnp.zeros((slot, cols), BF16)
                    row_low[part, :] = jnp.zeros((slot, cols), BF16)
                else:
                    row_high[part, :], row_low[part, :] = halves(arrays[k][...])


def upper_kernel(places, me_ref, high_ref, low_ref, *refs):
    arrays, (out_ref, row_high, row_low) = refs[:-4], refs[-3:]
    collect(places, me_ref[0], arrays, row_high, row_low)
    depth = row_high.shape[0]
    high = high_ref[:, :depth]
    out_ref[...] = mm(low_ref[:, :depth], row_high[...]) + mm(high, row_low[...]) + mm(high, row_high[...])


def share(places, me, part_ref, high_ref, low_ref, arrays, row_high, row_low, give):
    slot, cols = arrays[0].shape
    rows = part_ref.shape[0]
    step = rows // STEPS if rows % (STEPS * 16) == 0 else rows
    for r, table in enumerate(places):

        @pl.when(me == r)
        def _(table=table):
            here = [block for block, k in enumerate(table) if k is not None]
            span = pl.ds(here[0] * slot, (here[-1] + 1 - here[0]) * slot) if here else None
            for block in range(here[0], here[-1] + 1) if here else ():
                part = pl.ds(block * slot, slot)
                if table[block] is None:
                    row_high[part, :] = jnp.zeros((slot, cols), BF16)
                    row_low[part, :] = jnp.zeros((slot, cols), BF16)
                else:
                    row_high[part, :], row_low[part, :] = halves(arrays[table[block]][...])
            for k in range(rows // step):
                part = pl.ds(k * step, step)
                value = part_ref[part, :]
                if here:
                    high = high_ref[part, span]
                    more = mm(low_ref[part, span], row_high[span, :]) + mm(high, row_low[span, :])
                    value = value + (more + mm(high, row_high[span, :]))
                give(k, part, value)


def middle_kernel(places, me_ref, part_ref, high_ref, low_ref, *refs):
    arrays, (out_ref, row_high, row_low) = refs[:-3], refs[-3:]

    def give(k, part, value):
        out_ref[part, :] = value

    share(places, me_ref[0], part_ref, high_ref, low_ref, arrays, row_high, row_low, give)


def finish_kernel(places, me_ref, part_ref, high_ref, low_ref, *refs):
    arrays, (out_ref, row_high, row_low, total, sem) = refs[:-5], refs[-5:]

    def copy(k, part):
        return pltpu.make_async_copy(total.at[part], out_ref.at[part], sem.at[k])

    def give(k, part, value):
        total[part, :] = value
        copy(k, part).start()

    share(places, me_ref[0], part_ref, high_ref, low_ref, arrays, row_high, row_low, give)
    step = total.shape[0] // sem.shape[0]
    for k in range(sem.shape[0]):
        copy(k, pl.ds(k * step, step)).wait()


def join_kernel(first, second, *refs):
    out, sem = refs[-2:]
    rows = first.shape[0]
    copies = [
        pltpu.make_async_copy(first, out.at[:rows], sem.at[0]),
        pltpu.make_async_copy(second, out.at[rows:], sem.at[1]),
    ]
    for copy in copies:
        copy.start()
    for copy in copies:
        copy.wait()


def join(first, second, afters):
    rows, cols = first.shape
    return pl.pallas_call(
        join_kernel,
        out_shape=jax.ShapeDtypeStruct((2 * rows, cols), first.dtype),
        in_specs=[VMEM, VMEM] + [ANY] * len(afters),
        out_specs=VMEM,
        scratch_shapes=[pltpu.SemaphoreType.DMA((2,))],
        compiler_params=PARAMS,
        name="join",
    )(first, second, *afters)


def gather_shards(shard, count, afters):
    held, masks = shard, [0]
    bit = 1
    while 2 * bit < count:
        bit *= 2
    while bit:
        other = lax.ppermute(held, "col", [(i, i ^ bit) for i in range(count)])
        masks += [mask ^ bit for mask in masks]
        if bit > 1:
            held = join(held, other, afters[0])
            afters = afters[1:] or afters
        bit //= 2
    return held, other, masks


def local(row_count, col_count, matrix, panel_t, inverse_lower, pivot_rows):
    rows, cols = matrix.shape
    width = inverse_lower.shape[0]
    slot = width // row_count
    stay = width // 2
    me = lax.axis_index("row").astype(jnp.int32)
    column = lax.axis_index("col").astype(jnp.int32)
    here = me.reshape(1)
    pivot = pivot_rows.reshape(1, width)
    item_shape = jax.ShapeDtypeStruct((slot, cols), F32)

    rounds = plan(row_count)
    order = [item for moves in rounds for s, t, item in moves if s == 0]
    matrix = pltpu.with_memory_space_constraint(matrix, pltpu.HBM)
    pivot = pltpu.with_memory_space_constraint(pivot, pltpu.HBM)
    panel_t = pltpu.with_memory_space_constraint(panel_t, pltpu.HBM)
    inverse_lower = pltpu.with_memory_space_constraint(inverse_lower, pltpu.HBM)
    pieces = next(k for k in range(3, 0, -1) if rows % (16 * k) == 0 and width % (rows // k) == 0)
    *own, panel = pl.pallas_call(
        functools.partial(pick_kernel, row_count, order),
        out_shape=(item_shape,) * len(order) + (jax.ShapeDtypeStruct(panel_t.shape, F32),),
        in_specs=[SMEM, HBM, HBM, HBM],
        out_specs=(VMEM,) * (len(order) + 1),
        scratch_shapes=[
            pltpu.VMEM((rows, cols), F32),
            pltpu.VMEM((1, width), jnp.int32),
            pltpu.SemaphoreType.DMA((2 + pieces,)),
        ],
        compiler_params=PARAMS,
        name="pick",
    )(here, pivot, matrix, panel_t)

    arrays = list(own)
    found = [{} for _ in range(row_count)]
    for k, item in enumerate(order):
        found[0][item] = k
    for r in range(1, row_count):
        found[r]["pick", r] = 0
    operands, chunks = [], row_count // 2
    for moves in rounds:
        leaving = [item for s, t, item in moves if s == 0]
        operand = own[order.index(leaving[0])] if leaving else own[0]
        if len(operands) > chunks + 3 and all(item[0] == "stay" for s, t, item in moves):
            operand = arrays[len(own) + chunks]
        for s, t, item in moves:
            if s != 0 and item[0] == "stay":
                operand = jnp.where(me == s, arrays[found[s][item]], operand)
        for s, t, item in moves:
            found[t][item] = len(arrays)
        operands.append(operand)
        arrays.append(lax.ppermute(operand, "row", [(s, t) for s, t, item in moves]))
    received = arrays[len(own) :]
    blocks = [("pick", p) for p in range(chunks, row_count)]
    late_blocks = [("stay", c) for c in range(chunks)] + [("pick", p) for p in range(1, chunks)]
    soon = len(own) + chunks + 2
    places = [[found[r][item] for item in blocks] for r in range(row_count)]
    late = [
        [found[r].get(item) for item in late_blocks[:chunks] + [("moved", r)] + late_blocks[chunks:]]
        for r in range(row_count)
    ]
    soon_late = [[k if k is not None and k < soon else None for k in table] for table in late]
    late = [[k if k is not None and k >= soon else None for k in table] for table in late]
    late_rows = len(late_blocks) * slot

    picked_rows = len(blocks) * slot + late_rows
    inv_high, inv_low, land = pl.pallas_call(
        functools.partial(prepare_kernel, row_count),
        out_shape=(
            jax.ShapeDtypeStruct((width, picked_rows), BF16),
            jax.ShapeDtypeStruct((width, picked_rows), BF16),
            jax.ShapeDtypeStruct((rows, slot), BF16),
        ),
        in_specs=[SMEM, HBM, HBM, HBM],
        out_specs=(VMEM,) * 3,
        scratch_shapes=[
            pltpu.VMEM((1, width), jnp.int32),
            pltpu.VMEM((width, width), F32),
            pltpu.SemaphoreType.DMA((2,)),
        ],
        compiler_params=PARAMS,
        cost_estimate=SHORT,
        name="prepare",
    )(here, pivot, inverse_lower, matrix)

    near, far, masks = gather_shards(panel, col_count, [operands[3:5] + [land], []])
    ids = column ^ jnp.array(masks, jnp.int32)

    def used(*tables):
        names = sorted({k for table in tables for k in jax.tree.leaves(table)})
        return [arrays[k] for k in names], [jax.tree.map(names.index, table) for table in tables]

    half = width // 2
    ends, near_high, near_low = pl.pallas_call(
        near_kernel,
        out_shape=(jax.ShapeDtypeStruct((rows, late_rows), F32),) + (jax.ShapeDtypeStruct((rows, half), BF16),) * 2,
        in_specs=[SMEM, SMEM] + [VMEM] * 3,
        out_specs=(VMEM,) * 3,
        scratch_shapes=[pltpu.VMEM((half, late_rows), F32)] * 2,
        compiler_params=PARAMS,
        name="near",
    )(here, ids, near, inv_high, inv_low)
    early_arrays, (places,) = used(places)
    upper = pl.pallas_call(
        functools.partial(upper_kernel, places),
        out_shape=jax.ShapeDtypeStruct((width, cols), F32),
        in_specs=[SMEM] + [VMEM] * (2 + len(early_arrays)) + [ANY],
        out_specs=VMEM,
        scratch_shapes=[pltpu.VMEM((picked_rows - late_rows, cols), BF16)] * 2,
        compiler_params=PARAMS,
        cost_estimate=LONG,
        name="upper",
    )(here, inv_high, inv_low, *early_arrays, ends)

    part, end_high, end_low = pl.pallas_call(
        far_kernel,
        out_shape=(jax.ShapeDtypeStruct((rows, cols), F32),)
        + (jax.ShapeDtypeStruct((rows, late_rows + slot), BF16),) * 2,
        in_specs=[SMEM, SMEM] + [VMEM] * 4 + [HBM] + [VMEM] * 4,
        out_specs=(VMEM,) * 3,
        scratch_shapes=[pltpu.VMEM((rows, half), BF16)] * 2
        + [pltpu.VMEM((half, cols + late_rows), F32)] * 2
        + [pltpu.VMEM((half, cols), F32)] * 2
        + [pltpu.VMEM((rows, cols), F32), pltpu.SemaphoreType.DMA(())],
        compiler_params=PARAMS,
        name="far",
    )(here, ids, far, inv_high, inv_low, upper, matrix, ends, land, near_high, near_low)

    row_scratch = [pltpu.VMEM((late_rows + slot, cols), BF16)] * 2
    soon_arrays, (soon_late,) = used(soon_late)
    part = pl.pallas_call(
        functools.partial(middle_kernel, soon_late),
        out_shape=jax.ShapeDtypeStruct((rows, cols), F32),
        in_specs=[SMEM] + [VMEM] * (3 + len(soon_arrays)),
        out_specs=VMEM,
        scratch_shapes=row_scratch,
        compiler_params=PARAMS,
        name="middle",
    )(here, part, end_high, end_low, *soon_arrays)

    late_arrays, (late,) = used(late)
    steps = STEPS if rows % (STEPS * 16) == 0 else 1
    return pl.pallas_call(
        functools.partial(finish_kernel, late),
        out_shape=jax.ShapeDtypeStruct((rows, cols), F32),
        in_specs=[SMEM] + [VMEM] * (3 + len(late_arrays)),
        out_specs=HBM,
        scratch_shapes=row_scratch + [pltpu.VMEM((rows, cols), F32), pltpu.SemaphoreType.DMA((steps,))],
        compiler_params=PARAMS,
        name="finish",
    )(here, part, end_high, end_low, *late_arrays)


def solution(mesh):
    in_specs = (P("row", "col"), P("col", "row"), P(), P())
    out_specs = P("row", "col")
    return jax.shard_map(
        functools.partial(local, mesh.shape["row"], mesh.shape["col"]),
        mesh=mesh,
        in_specs=in_specs,
        out_specs=out_specs,
        check_vma=False,
    )
```

```python
import functools

import jax
import jax.numpy as jnp
from jax import lax
from jax.experimental import pallas as pl
from jax.experimental.pallas import tpu as pltpu
from jax.sharding import PartitionSpec as P

F32 = jnp.float32
BF16 = jnp.bfloat16
STEPS = 6
VMEM = pl.BlockSpec(memory_space=pltpu.VMEM)
SMEM = pl.BlockSpec(memory_space=pltpu.SMEM)
ANY = pl.BlockSpec(memory_space=pl.ANY)
HBM = pl.BlockSpec(memory_space=pltpu.HBM)
SHORT = pl.CostEstimate(flops=1_000_000, transcendentals=0, bytes_accessed=100_000)
LONG = pl.CostEstimate(flops=40_000_000_000, transcendentals=0, bytes_accessed=100_000_000)
PARAMS = pltpu.CompilerParams(vmem_limit_bytes=20 * 1024 * 1024)


def halves(x):
    high = x.astype(BF16)
    low = (x - high.astype(F32)).astype(BF16)
    return high, low


def mm(a, b):
    return jnp.dot(a, b, preferred_element_type=F32)


def mm_nt(a, b):
    return lax.dot_general(a, b, (((1,), (1,)), ((), ())), preferred_element_type=F32)


def mm_tn(a, b):
    return lax.dot_general(a, b, (((0,), (0,)), ((), ())), preferred_element_type=F32)


def classify(pivot, count, rows):
    width = pivot.shape[1]
    lanes = lax.broadcasted_iota(jnp.int32, (1, width), 1)
    kind = jnp.where(pivot != lanes, pivot // rows, 0)
    padded = -(-count // 16) * 16
    owner = lax.broadcasted_iota(jnp.int32, (padded, width), 0)
    member = owner == kind
    before = lax.broadcasted_iota(jnp.int32, (width, width), 0) < lax.broadcasted_iota(
        jnp.int32, (width, width), 1
    )
    ranks = mm(member.astype(BF16), before.astype(BF16))
    place = jnp.sum(jnp.where(member, ranks, 0.0), axis=0, keepdims=True)
    return kind, place.astype(jnp.int32)


def one_hot(position, slots):
    slot = lax.broadcasted_iota(jnp.int32, (slots, position.shape[1]), 0)
    return (slot == position).astype(BF16)


def picked(pick, rows_ref, copies):
    step = rows_ref.shape[0] // len(copies)
    total = None
    for k in range(pick.shape[1] // step):
        copies[k].wait()
        high, low = halves(rows_ref[k * step : (k + 1) * step, :])
        part = pick[:, k * step : (k + 1) * step]
        value = mm(part, low) + mm(part, high)
        total = value if total is None else total + value
    return total


def plan(count):
    middle, chunks = count // 2, count // 2
    first = [(0, middle, ("stay", c)) for c in range(chunks)]
    relays = []
    for c in range(chunks):
        for k in range(1, count):
            step = [(middle + k - 1, middle + k, ("stay", c)), (middle - k + 1, middle - k, ("stay", c))]
            relays += [move for move in (step if c + 1 < chunks else step[::-1]) if 0 < move[1] < count]
    early = [(s, t, ("pick", s)) for t in range(1, count) for s in range(middle, count) if t not in (s, middle)]
    early += [(s, 0, ("pick", s)) for s in range(1, middle)]
    late = [(s, t, ("pick", s)) for s in range(1, middle) for t in range(middle + 1, count)]
    late += [(0, t, ("moved", t)) for t in range(1, count)]
    late += [(s, middle, ("pick", s)) for s in range(middle + 1, count)]
    late += [(s, 0, ("pick", s)) for s in range(middle, count)]
    last = [(s, t, ("pick", s)) for s in range(1, middle) for t in range(1, middle + 1) if s != t]
    ready = {(0, ("stay", c)): 0 for c in range(chunks)}
    rounds = []
    while first or relays or early or late or last:
        now, senders, targets = [], set(), set()
        queues = [first, relays, early] + [late] * (len(rounds) >= chunks) + [last] * (len(rounds) > chunks + 2)
        for queue in queues:
            for move in list(queue):
                s, t, item = move
                known = item[0] != "stay" or ready.get((s, item), len(rounds) + 1) <= len(rounds)
                if known and s not in senders and t not in targets:
                    now.append(move)
                    senders.add(s)
                    targets.add(t)
                    queue.remove(move)
        for s, t, item in now:
            ready[t, item] = len(rounds) + 3
        rounds.append(now)
    return rounds


def pick_kernel(count, order, me_ref, pivot_ref, matrix_ref, panel_ref, *refs):
    outs, (panel_out, rows_ref, pivot_v, sem) = refs[:-4], refs[-4:]
    rows, cols = matrix_ref.shape
    width = pivot_ref.shape[1]
    slot = width // count
    me = me_ref[0]
    point = pltpu.make_async_copy(pivot_ref, pivot_v, sem.at[0])
    panel = pltpu.make_async_copy(panel_ref, panel_out, sem.at[1])
    step = rows // (sem.shape[0] - 2)
    copies = [
        pltpu.make_async_copy(matrix_ref.at[pl.ds(k * step, step)], rows_ref.at[pl.ds(k * step, step)], sem.at[2 + k])
        for k in range(rows // step)
    ]
    point.start()
    for copy in copies:
        copy.start()
    panel.start()
    point.wait()
    pivot = pivot_v[...]
    kind, place = classify(pivot, count, rows)

    @pl.when(me == 0)
    def _():
        start = jnp.full(kind.shape, -count * width, jnp.int32)
        for k, (name, which) in enumerate(order):
            if name == "moved":
                start = jnp.where(kind == which, k * slot, start)
            else:
                inside = (kind == 0) & (place >= which * slot) & (place < (which + 1) * slot)
                start = jnp.where(inside, (k - which) * slot, start)
        got = picked(one_hot(start + place, len(order) * slot), rows_ref, copies)
        for k, out in enumerate(outs):
            out[...] = got[k * slot : (k + 1) * slot, :]
        for copy in copies[width // step :]:
            copy.wait()

    @pl.when(me != 0)
    def _():
        mine = lax.broadcasted_iota(jnp.int32, (slot, width), 0) == jnp.where(kind == me, place, -1)
        source = jnp.sum(jnp.where(mine, pivot - me * rows, 0), axis=1, keepdims=True)
        pick = (lax.broadcasted_iota(jnp.int32, (slot, rows), 1) == source).astype(BF16)
        got = picked(pick, rows_ref, copies)
        for out in outs:
            out[...] = got

    panel.wait()


def prepare_kernel(count, me_ref, pivot_ref, inverse_ref, matrix_ref, *refs):
    high_ref, low_ref, land_ref, base_ref, pivot_v, inv_ref, rows_ref, sem = refs[-8:]
    rows, cols = matrix_ref.shape
    width = pivot_ref.shape[1]
    slot = width // count
    stay = width // 2
    me = me_ref[0]
    copies = [
        pltpu.make_async_copy(pivot_ref, pivot_v, sem.at[0]),
        pltpu.make_async_copy(inverse_ref, inv_ref, sem.at[1]),
        pltpu.make_async_copy(matrix_ref, rows_ref, sem.at[2]),
    ]
    for copy in copies:
        copy.start()
    copies[0].wait()
    pivot = pivot_v[...]
    kind, place = classify(pivot, count, rows)
    total = high_ref.shape[1]
    middle = count // 2
    start = jnp.where(kind == 0, (count - middle) * slot, stay + (kind + count - middle - 1) * slot)
    spread = one_hot(place + jnp.where(kind < middle, start, (kind - middle) * slot), total)
    mine = (kind == me) & (kind != 0)
    landing = lax.broadcasted_iota(jnp.int32, (rows, width), 0) == jnp.where(mine, pivot - me * rows, -1)
    land = mm_nt(landing.astype(BF16), one_hot(jnp.where(mine, place, -1), slot))
    land_ref[...] = land.astype(BF16)
    taken = jnp.sum(land, axis=1, keepdims=True)
    copies[1].wait()
    inv_high, inv_low = halves(inv_ref[...])
    high_ref[...] = mm_nt(inv_high, spread).astype(BF16)
    low_ref[...] = mm_nt(inv_low, spread).astype(BF16)
    copies[2].wait()
    base_ref[...] = jnp.where(taken > 0.5, 0.0, rows_ref[...])


def turn(shards_ref, start, high_ref, low_ref):
    high, low = halves(-shards_ref[:, start:])
    high_ref[start:, :] = high.T
    low_ref[start:, :] = low.T


def near_kernel(me_ref, ids_ref, shards_ref, inv_high, inv_low, ends_ref, high_ref, low_ref, side_high, side_low):
    half, rows = shards_ref.shape
    width = inv_high.shape[0]
    depth = width // ids_ref.shape[0]
    first = inv_high.shape[1] - side_high.shape[1]
    for k in range(half // depth):
        source = pl.ds(pl.multiple_of(ids_ref[k] * depth, depth), depth)
        part = pl.ds(k * depth, depth)
        side_high[part, :] = inv_high[source, first:].astype(F32)
        side_low[part, :] = inv_low[source, first:].astype(F32)

    def work(start):
        turn(shards_ref, start, high_ref, low_ref)
        high, right = high_ref[start:, :], side_high[...].astype(BF16)
        ends_ref[start:, :] = mm(low_ref[start:, :], right) + mm(high, side_low[...].astype(BF16)) + mm(high, right)

    pl.when(me_ref[0] == 0)(lambda: work(width))
    pl.when(me_ref[0] != 0)(lambda: work(0))


def far_kernel(me_ref, ids_ref, shards_ref, inv_high, inv_low, upper_ref, rows_ref, ends_ref, land_ref, *refs):
    near_high, near_low, out_ref, end_high, end_low, high_ref, low_ref = refs[:7]
    side_high, side_low, up_high, up_low = refs[7:]
    half, rows = shards_ref.shape
    width, cols = upper_ref.shape
    depth = width // ids_ref.shape[0]
    first = inv_high.shape[1] - (side_high.shape[1] - cols)
    stay, slot = width // 2, land_ref.shape[1]
    for k in range(width // depth):
        source = pl.ds(pl.multiple_of(ids_ref[k] * depth, depth), depth)
        high, low = halves(upper_ref[source, :])
        part = pl.ds(k * depth % half, depth)
        if k * depth < half:
            up_high[part, :], up_low[part, :] = high.astype(F32), low.astype(F32)
        else:
            side_high[part, :cols], side_low[part, :cols] = high.astype(F32), low.astype(F32)
            side_high[part, cols:] = inv_high[source, first:].astype(F32)
            side_low[part, cols:] = inv_low[source, first:].astype(F32)

    def work(start):
        turn(shards_ref, start, high_ref, low_ref)
        high, right = high_ref[start:, :], side_high[...].astype(BF16)
        value = mm(low_ref[start:, :], right) + mm(high, side_low[...].astype(BF16)) + mm(high, right)
        high, right = near_high[start:, :], up_high[...].astype(BF16)
        near = mm(near_low[start:, :], right) + mm(high, up_low[...].astype(BF16)) + mm(high, right)
        out_ref[start:, :] = rows_ref[start:, :] + (near + value[:, :cols])
        high, low = halves(ends_ref[start:, :] + value[:, cols:])
        put(end_high, start, high)
        put(end_low, start, low)

    def put(end, start, columns):
        part = pl.ds(start, columns.shape[0])
        end[part, :stay] = columns[:, :stay]
        end[part, stay + slot :] = columns[:, stay:]

    @pl.when(me_ref[0] == 0)
    def _():
        work(width)
        out_ref[:width, :] = upper_ref[...]
        put(end_high, 0, inv_high[:, first:])
        put(end_low, 0, inv_low[:, first:])

    pl.when(me_ref[0] != 0)(lambda: work(0))
    end_high[:, stay : stay + slot] = land_ref[...]
    end_low[:, stay : stay + slot] = jnp.zeros(land_ref.shape, BF16)


def collect(places, me, arrays, row_high, row_low):
    slot, cols = arrays[0].shape
    for r in range(len(places)):

        @pl.when(me == r)
        def _(r=r):
            for block, k in enumerate(places[r]):
                part = pl.ds(block * slot, slot)
                if k is None:
                    row_high[part, :] = jnp.zeros((slot, cols), BF16)
                    row_low[part, :] = jnp.zeros((slot, cols), BF16)
                else:
                    row_high[part, :], row_low[part, :] = halves(arrays[k][...])


def upper_kernel(places, me_ref, high_ref, low_ref, *refs):
    arrays, (out_ref, row_high, row_low) = refs[:-4], refs[-3:]
    collect(places, me_ref[0], arrays, row_high, row_low)
    depth = row_high.shape[0]
    high = high_ref[:, :depth]
    out_ref[...] = mm(low_ref[:, :depth], row_high[...]) + mm(high, row_low[...]) + mm(high, row_high[...])


def share(places, me, part_ref, high_ref, low_ref, arrays, row_high, row_low, give):
    slot, cols = arrays[0].shape
    rows = part_ref.shape[0]
    step = rows // STEPS if rows % (STEPS * 16) == 0 else rows
    for r, table in enumerate(places):

        @pl.when(me == r)
        def _(table=table):
            here = [block for block, k in enumerate(table) if k is not None]
            span = pl.ds(here[0] * slot, (here[-1] + 1 - here[0]) * slot) if here else None
            for block in range(here[0], here[-1] + 1) if here else ():
                part = pl.ds(block * slot, slot)
                if table[block] is None:
                    row_high[part, :] = jnp.zeros((slot, cols), BF16)
                    row_low[part, :] = jnp.zeros((slot, cols), BF16)
                else:
                    row_high[part, :], row_low[part, :] = halves(arrays[table[block]][...])
            for k in range(rows // step):
                part = pl.ds(k * step, step)
                value = part_ref[part, :]
                if here:
                    high = high_ref[part, span]
                    more = mm(low_ref[part, span], row_high[span, :]) + mm(high, row_low[span, :])
                    value = value + (more + mm(high, row_high[span, :]))
                give(k, part, value)


def middle_kernel(places, me_ref, part_ref, high_ref, low_ref, *refs):
    arrays, (out_ref, row_high, row_low) = refs[:-3], refs[-3:]

    def give(k, part, value):
        out_ref[part, :] = value

    share(places, me_ref[0], part_ref, high_ref, low_ref, arrays, row_high, row_low, give)


def finish_kernel(places, me_ref, part_ref, high_ref, low_ref, *refs):
    arrays, (out_ref, row_high, row_low, total, sem) = refs[:-5], refs[-5:]

    def copy(k, part):
        return pltpu.make_async_copy(total.at[part], out_ref.at[part], sem.at[k])

    def give(k, part, value):
        total[part, :] = value
        copy(k, part).start()

    share(places, me_ref[0], part_ref, high_ref, low_ref, arrays, row_high, row_low, give)
    step = total.shape[0] // sem.shape[0]
    for k in range(sem.shape[0]):
        copy(k, pl.ds(k * step, step)).wait()


def join_kernel(first, second, *refs):
    out, sem = refs[-2:]
    rows = first.shape[0]
    copies = [
        pltpu.make_async_copy(first, out.at[:rows], sem.at[0]),
        pltpu.make_async_copy(second, out.at[rows:], sem.at[1]),
    ]
    for copy in copies:
        copy.start()
    for copy in copies:
        copy.wait()


def join(first, second, afters):
    rows, cols = first.shape
    return pl.pallas_call(
        join_kernel,
        out_shape=jax.ShapeDtypeStruct((2 * rows, cols), first.dtype),
        in_specs=[VMEM, VMEM] + [ANY] * len(afters),
        out_specs=VMEM,
        scratch_shapes=[pltpu.SemaphoreType.DMA((2,))],
        compiler_params=PARAMS,
        name="join",
    )(first, second, *afters)


def gather_shards(shard, count, afters):
    held, masks = shard, [0]
    bit = 1
    while 2 * bit < count:
        bit *= 2
    while bit:
        other = lax.ppermute(held, "col", [(i, i ^ bit) for i in range(count)])
        masks += [mask ^ bit for mask in masks]
        if bit > 1:
            held = join(held, other, afters[0])
            afters = afters[1:] or afters
        bit //= 2
    return held, other, masks


def local(row_count, col_count, matrix, panel_t, inverse_lower, pivot_rows):
    rows, cols = matrix.shape
    width = inverse_lower.shape[0]
    slot = width // row_count
    stay = width // 2
    me = lax.axis_index("row").astype(jnp.int32)
    column = lax.axis_index("col").astype(jnp.int32)
    here = me.reshape(1)
    pivot = pivot_rows.reshape(1, width)
    item_shape = jax.ShapeDtypeStruct((slot, cols), F32)

    rounds = plan(row_count)
    order = [item for moves in rounds for s, t, item in moves if s == 0]
    matrix = pltpu.with_memory_space_constraint(matrix, pltpu.HBM)
    pivot = pltpu.with_memory_space_constraint(pivot, pltpu.HBM)
    panel_t = pltpu.with_memory_space_constraint(panel_t, pltpu.HBM)
    inverse_lower = pltpu.with_memory_space_constraint(inverse_lower, pltpu.HBM)
    pieces = next(k for k in range(3, 0, -1) if rows % (16 * k) == 0 and width % (rows // k) == 0)
    *own, panel = pl.pallas_call(
        functools.partial(pick_kernel, row_count, order),
        out_shape=(item_shape,) * len(order) + (jax.ShapeDtypeStruct(panel_t.shape, F32),),
        in_specs=[SMEM, HBM, HBM, HBM],
        out_specs=(VMEM,) * (len(order) + 1),
        scratch_shapes=[
            pltpu.VMEM((rows, cols), F32),
            pltpu.VMEM((1, width), jnp.int32),
            pltpu.SemaphoreType.DMA((2 + pieces,)),
        ],
        compiler_params=PARAMS,
        name="pick",
    )(here, pivot, matrix, panel_t)

    arrays = list(own)
    found = [{} for _ in range(row_count)]
    for k, item in enumerate(order):
        found[0][item] = k
    for r in range(1, row_count):
        found[r]["pick", r] = 0
    operands, chunks = [], row_count // 2
    for moves in rounds:
        leaving = [item for s, t, item in moves if s == 0]
        operand = own[order.index(leaving[0])] if leaving else own[0]
        if len(operands) > chunks + 3 and all(item[0] == "stay" for s, t, item in moves):
            operand = arrays[len(own) + chunks]
        for s, t, item in moves:
            if s != 0 and item[0] == "stay":
                operand = jnp.where(me == s, arrays[found[s][item]], operand)
        for s, t, item in moves:
            found[t][item] = len(arrays)
        operands.append(operand)
        arrays.append(lax.ppermute(operand, "row", [(s, t) for s, t, item in moves]))
    received = arrays[len(own) :]
    blocks = [("pick", p) for p in range(chunks, row_count)]
    late_blocks = [("stay", c) for c in range(chunks)] + [("pick", p) for p in range(1, chunks)]
    soon = len(own) + chunks + 2
    places = [[found[r][item] for item in blocks] for r in range(row_count)]
    late = [
        [found[r].get(item) for item in late_blocks[:chunks] + [("moved", r)] + late_blocks[chunks:]]
        for r in range(row_count)
    ]
    soon_late = [[k if k is not None and k < soon else None for k in table] for table in late]
    late = [[k if k is not None and k >= soon else None for k in table] for table in late]
    late_rows = len(late_blocks) * slot

    picked_rows = len(blocks) * slot + late_rows
    inv_high, inv_low, land, base = pl.pallas_call(
        functools.partial(prepare_kernel, row_count),
        out_shape=(
            jax.ShapeDtypeStruct((width, picked_rows), BF16),
            jax.ShapeDtypeStruct((width, picked_rows), BF16),
            jax.ShapeDtypeStruct((rows, slot), BF16),
            jax.ShapeDtypeStruct((rows, cols), F32),
        ),
        in_specs=[SMEM, HBM, HBM, HBM],
        out_specs=(VMEM,) * 4,
        scratch_shapes=[
            pltpu.VMEM((1, width), jnp.int32),
            pltpu.VMEM((width, width), F32),
            pltpu.VMEM((rows, cols), F32),
            pltpu.SemaphoreType.DMA((3,)),
        ],
        compiler_params=PARAMS,
        cost_estimate=SHORT,
        name="prepare",
    )(here, pivot, inverse_lower, matrix)

    near, far, masks = gather_shards(panel, col_count, [operands[3:5] + [land], []])
    ids = column ^ jnp.array(masks, jnp.int32)

    def used(*tables):
        names = sorted({k for table in tables for k in jax.tree.leaves(table)})
        return [arrays[k] for k in names], [jax.tree.map(names.index, table) for table in tables]

    half = width // 2
    ends, near_high, near_low = pl.pallas_call(
        near_kernel,
        out_shape=(jax.ShapeDtypeStruct((rows, late_rows), F32),) + (jax.ShapeDtypeStruct((rows, half), BF16),) * 2,
        in_specs=[SMEM, SMEM] + [VMEM] * 3,
        out_specs=(VMEM,) * 3,
        scratch_shapes=[pltpu.VMEM((half, late_rows), F32)] * 2,
        compiler_params=PARAMS,
        name="near",
    )(here, ids, near, inv_high, inv_low)
    early_arrays, (places,) = used(places)
    upper = pl.pallas_call(
        functools.partial(upper_kernel, places),
        out_shape=jax.ShapeDtypeStruct((width, cols), F32),
        in_specs=[SMEM] + [VMEM] * (2 + len(early_arrays)) + [ANY],
        out_specs=VMEM,
        scratch_shapes=[pltpu.VMEM((picked_rows - late_rows, cols), BF16)] * 2,
        compiler_params=PARAMS,
        cost_estimate=LONG,
        name="upper",
    )(here, inv_high, inv_low, *early_arrays, ends)

    part, end_high, end_low = pl.pallas_call(
        far_kernel,
        out_shape=(jax.ShapeDtypeStruct((rows, cols), F32),)
        + (jax.ShapeDtypeStruct((rows, late_rows + slot), BF16),) * 2,
        in_specs=[SMEM, SMEM] + [VMEM] * 9,
        out_specs=(VMEM,) * 3,
        scratch_shapes=[pltpu.VMEM((rows, half), BF16)] * 2
        + [pltpu.VMEM((half, cols + late_rows), F32)] * 2
        + [pltpu.VMEM((half, cols), F32)] * 2,
        compiler_params=PARAMS,
        name="far",
    )(here, ids, far, inv_high, inv_low, upper, base, ends, land, near_high, near_low)

    row_scratch = [pltpu.VMEM((late_rows + slot, cols), BF16)] * 2
    soon_arrays, (soon_late,) = used(soon_late)
    part = pl.pallas_call(
        functools.partial(middle_kernel, soon_late),
        out_shape=jax.ShapeDtypeStruct((rows, cols), F32),
        in_specs=[SMEM] + [VMEM] * (3 + len(soon_arrays)),
        out_specs=VMEM,
        scratch_shapes=row_scratch,
        compiler_params=PARAMS,
        name="middle",
    )(here, part, end_high, end_low, *soon_arrays)

    late_arrays, (late,) = used(late)
    steps = STEPS if rows % (STEPS * 16) == 0 else 1
    return pl.pallas_call(
        functools.partial(finish_kernel, late),
        out_shape=jax.ShapeDtypeStruct((rows, cols), F32),
        in_specs=[SMEM] + [VMEM] * (3 + len(late_arrays)),
        out_specs=HBM,
        scratch_shapes=row_scratch + [pltpu.VMEM((rows, cols), F32), pltpu.SemaphoreType.DMA((steps,))],
        compiler_params=PARAMS,
        name="finish",
    )(here, part, end_high, end_low, *late_arrays)


def solution(mesh):
    in_specs = (P("row", "col"), P("col", "row"), P(), P())
    out_specs = P("row", "col")
    return jax.shard_map(
        functools.partial(local, mesh.shape["row"], mesh.shape["col"]),
        mesh=mesh,
        in_specs=in_specs,
        out_specs=out_specs,
        check_vma=False,
    )
```

```python
import functools

import jax
import jax.numpy as jnp
from jax import lax
from jax.experimental import pallas as pl
from jax.experimental.pallas import tpu as pltpu
from jax.sharding import PartitionSpec as P

F32 = jnp.float32
BF16 = jnp.bfloat16
STEPS = 2
VMEM = pl.BlockSpec(memory_space=pltpu.VMEM)
SMEM = pl.BlockSpec(memory_space=pltpu.SMEM)
ANY = pl.BlockSpec(memory_space=pl.ANY)
HBM = pl.BlockSpec(memory_space=pltpu.HBM)
SHORT = pl.CostEstimate(flops=1_000_000, transcendentals=0, bytes_accessed=100_000)
LONG = pl.CostEstimate(flops=40_000_000_000, transcendentals=0, bytes_accessed=100_000_000)
PARAMS = pltpu.CompilerParams(vmem_limit_bytes=20 * 1024 * 1024)


def halves(x):
    high = x.astype(BF16)
    low = (x - high.astype(F32)).astype(BF16)
    return high, low


def mm(a, b):
    return jnp.dot(a, b, preferred_element_type=F32)


def mm_nt(a, b):
    return lax.dot_general(a, b, (((1,), (1,)), ((), ())), preferred_element_type=F32)


def mm_tn(a, b):
    return lax.dot_general(a, b, (((0,), (0,)), ((), ())), preferred_element_type=F32)


def classify(pivot, count, rows):
    width = pivot.shape[1]
    lanes = lax.broadcasted_iota(jnp.int32, (1, width), 1)
    kind = jnp.where(pivot != lanes, pivot // rows, 0)
    padded = -(-count // 16) * 16
    owner = lax.broadcasted_iota(jnp.int32, (padded, width), 0)
    member = owner == kind
    before = lax.broadcasted_iota(jnp.int32, (width, width), 0) < lax.broadcasted_iota(
        jnp.int32, (width, width), 1
    )
    ranks = mm(member.astype(BF16), before.astype(BF16))
    place = jnp.sum(jnp.where(member, ranks, 0.0), axis=0, keepdims=True)
    return kind, place.astype(jnp.int32)


def one_hot(position, slots):
    slot = lax.broadcasted_iota(jnp.int32, (slots, position.shape[1]), 0)
    return (slot == position).astype(BF16)


def picked(pick, rows_ref, copies):
    step = rows_ref.shape[0] // len(copies)
    total = None
    for k in range(pick.shape[1] // step):
        copies[k].wait()
        high, low = halves(rows_ref[k * step : (k + 1) * step, :])
        part = pick[:, k * step : (k + 1) * step]
        value = mm(part, low) + mm(part, high)
        total = value if total is None else total + value
    return total


def plan(count):
    middle, chunks = count // 2, count // 2
    first = [(0, middle, ("stay", c)) for c in range(chunks)]
    relays = []
    for c in range(chunks):
        for k in range(1, count):
            step = [(middle + k - 1, middle + k, ("stay", c)), (middle - k + 1, middle - k, ("stay", c))]
            relays += [move for move in (step if c + 1 < chunks else step[::-1]) if 0 < move[1] < count]
    early = [(s, t, ("pick", s)) for t in range(1, count) for s in range(middle, count) if t not in (s, middle)]
    early += [(s, 0, ("pick", s)) for s in range(1, middle)]
    late = [(s, t, ("pick", s)) for s in range(1, middle) for t in range(middle + 1, count)]
    late += [(0, t, ("moved", t)) for t in range(1, count)]
    late += [(s, middle, ("pick", s)) for s in range(middle + 1, count)]
    late += [(s, 0, ("pick", s)) for s in range(middle, count)]
    last = [(s, t, ("pick", s)) for s in range(1, middle) for t in range(1, middle + 1) if s != t]
    ready = {(0, ("stay", c)): 0 for c in range(chunks)}
    rounds = []
    while first or relays or early or late or last:
        now, senders, targets = [], set(), set()
        queues = [first, relays, early] + [late] * (len(rounds) >= chunks) + [last] * (len(rounds) > chunks + 2)
        for queue in queues:
            for move in list(queue):
                s, t, item = move
                known = item[0] != "stay" or ready.get((s, item), len(rounds) + 1) <= len(rounds)
                if known and s not in senders and t not in targets:
                    now.append(move)
                    senders.add(s)
                    targets.add(t)
                    queue.remove(move)
        for s, t, item in now:
            ready[t, item] = len(rounds) + 3
        rounds.append(now)
    return rounds


def pick_kernel(count, order, me_ref, pivot_ref, matrix_ref, panel_ref, *refs):
    outs, (panel_out, rows_ref, pivot_v, sem) = refs[:-4], refs[-4:]
    rows, cols = matrix_ref.shape
    width = pivot_ref.shape[1]
    slot = width // count
    me = me_ref[0]
    point = pltpu.make_async_copy(pivot_ref, pivot_v, sem.at[0])
    panel = pltpu.make_async_copy(panel_ref, panel_out, sem.at[1])
    step = rows // (sem.shape[0] - 2)
    copies = [
        pltpu.make_async_copy(matrix_ref.at[pl.ds(k * step, step)], rows_ref.at[pl.ds(k * step, step)], sem.at[2 + k])
        for k in range(rows // step)
    ]
    point.start()
    for copy in copies:
        copy.start()
    panel.start()
    point.wait()
    pivot = pivot_v[...]
    kind, place = classify(pivot, count, rows)

    @pl.when(me == 0)
    def _():
        start = jnp.full(kind.shape, -count * width, jnp.int32)
        for k, (name, which) in enumerate(order):
            if name == "moved":
                start = jnp.where(kind == which, k * slot, start)
            else:
                inside = (kind == 0) & (place >= which * slot) & (place < (which + 1) * slot)
                start = jnp.where(inside, (k - which) * slot, start)
        got = picked(one_hot(start + place, len(order) * slot), rows_ref, copies)
        for k, out in enumerate(outs):
            out[...] = got[k * slot : (k + 1) * slot, :]
        for copy in copies[width // step :]:
            copy.wait()

    @pl.when(me != 0)
    def _():
        mine = lax.broadcasted_iota(jnp.int32, (slot, width), 0) == jnp.where(kind == me, place, -1)
        source = jnp.sum(jnp.where(mine, pivot - me * rows, 0), axis=1, keepdims=True)
        pick = (lax.broadcasted_iota(jnp.int32, (slot, rows), 1) == source).astype(BF16)
        got = picked(pick, rows_ref, copies)
        for out in outs:
            out[...] = got

    panel.wait()


def prepare_kernel(count, me_ref, pivot_ref, inverse_ref, matrix_ref, *refs):
    high_ref, low_ref, land_ref, base_ref, pivot_v, inv_ref, rows_ref, sem = refs[-8:]
    rows, cols = matrix_ref.shape
    width = pivot_ref.shape[1]
    slot = width // count
    stay = width // 2
    me = me_ref[0]
    copies = [
        pltpu.make_async_copy(pivot_ref, pivot_v, sem.at[0]),
        pltpu.make_async_copy(inverse_ref, inv_ref, sem.at[1]),
        pltpu.make_async_copy(matrix_ref, rows_ref, sem.at[2]),
    ]
    for copy in copies:
        copy.start()
    copies[0].wait()
    pivot = pivot_v[...]
    kind, place = classify(pivot, count, rows)
    total = high_ref.shape[1]
    middle = count // 2
    start = jnp.where(kind == 0, (count - middle) * slot, stay + (kind + count - middle - 1) * slot)
    spread = one_hot(place + jnp.where(kind < middle, start, (kind - middle) * slot), total)
    mine = (kind == me) & (kind != 0)
    landing = lax.broadcasted_iota(jnp.int32, (rows, width), 0) == jnp.where(mine, pivot - me * rows, -1)
    land = mm_nt(landing.astype(BF16), one_hot(jnp.where(mine, place, -1), slot))
    land_ref[...] = land.astype(BF16)
    taken = jnp.sum(land, axis=1, keepdims=True)
    copies[1].wait()
    inv_high, inv_low = halves(inv_ref[...])
    high_ref[...] = mm_nt(inv_high, spread).astype(BF16)
    low_ref[...] = mm_nt(inv_low, spread).astype(BF16)
    copies[2].wait()
    base_ref[...] = jnp.where(taken > 0.5, 0.0, rows_ref[...])


def turn(shards_ref, start, high_ref, low_ref):
    high, low = halves(-shards_ref[:, start:])
    high_ref[start:, :] = high.T
    low_ref[start:, :] = low.T


def near_kernel(me_ref, ids_ref, shards_ref, inv_high, inv_low, ends_ref, high_ref, low_ref, side_high, side_low):
    half, rows = shards_ref.shape
    width = inv_high.shape[0]
    depth = width // ids_ref.shape[0]
    first = inv_high.shape[1] - side_high.shape[1]
    for k in range(half // depth):
        source = pl.ds(pl.multiple_of(ids_ref[k] * depth, depth), depth)
        part = pl.ds(k * depth, depth)
        side_high[part, :] = inv_high[source, first:].astype(F32)
        side_low[part, :] = inv_low[source, first:].astype(F32)

    def work(start):
        turn(shards_ref, start, high_ref, low_ref)
        high, right = high_ref[start:, :], side_high[...].astype(BF16)
        ends_ref[start:, :] = mm(low_ref[start:, :], right) + mm(high, side_low[...].astype(BF16)) + mm(high, right)

    pl.when(me_ref[0] == 0)(lambda: work(width))
    pl.when(me_ref[0] != 0)(lambda: work(0))


def far_kernel(me_ref, ids_ref, shards_ref, inv_high, inv_low, upper_ref, rows_ref, ends_ref, land_ref, *refs):
    near_high, near_low, out_ref, end_high, end_low, high_ref, low_ref = refs[:7]
    side_high, side_low, up_high, up_low = refs[7:]
    half, rows = shards_ref.shape
    width, cols = upper_ref.shape
    depth = width // ids_ref.shape[0]
    first = inv_high.shape[1] - (side_high.shape[1] - cols)
    stay, slot = width // 2, land_ref.shape[1]
    for k in range(width // depth):
        source = pl.ds(pl.multiple_of(ids_ref[k] * depth, depth), depth)
        high, low = halves(upper_ref[source, :])
        part = pl.ds(k * depth % half, depth)
        if k * depth < half:
            up_high[part, :], up_low[part, :] = high.astype(F32), low.astype(F32)
        else:
            side_high[part, :cols], side_low[part, :cols] = high.astype(F32), low.astype(F32)
            side_high[part, cols:] = inv_high[source, first:].astype(F32)
            side_low[part, cols:] = inv_low[source, first:].astype(F32)

    def work(start):
        turn(shards_ref, start, high_ref, low_ref)
        high, right = high_ref[start:, :], side_high[...].astype(BF16)
        value = mm(low_ref[start:, :], right) + mm(high, side_low[...].astype(BF16)) + mm(high, right)
        high, right = near_high[start:, :], up_high[...].astype(BF16)
        near = mm(near_low[start:, :], right) + mm(high, up_low[...].astype(BF16)) + mm(high, right)
        out_ref[start:, :] = rows_ref[start:, :] + (near + value[:, :cols])
        high, low = halves(ends_ref[start:, :] + value[:, cols:])
        put(end_high, start, high)
        put(end_low, start, low)

    def put(end, start, columns):
        part = pl.ds(start, columns.shape[0])
        end[part, :stay] = columns[:, :stay]
        end[part, stay + slot :] = columns[:, stay:]

    @pl.when(me_ref[0] == 0)
    def _():
        work(width)
        out_ref[:width, :] = upper_ref[...]
        put(end_high, 0, inv_high[:, first:])
        put(end_low, 0, inv_low[:, first:])

    pl.when(me_ref[0] != 0)(lambda: work(0))
    end_high[:, stay : stay + slot] = land_ref[...]
    end_low[:, stay : stay + slot] = jnp.zeros(land_ref.shape, BF16)


def collect(places, me, arrays, row_high, row_low):
    slot, cols = arrays[0].shape
    for r in range(len(places)):

        @pl.when(me == r)
        def _(r=r):
            for block, k in enumerate(places[r]):
                part = pl.ds(block * slot, slot)
                if k is None:
                    row_high[part, :] = jnp.zeros((slot, cols), BF16)
                    row_low[part, :] = jnp.zeros((slot, cols), BF16)
                else:
                    row_high[part, :], row_low[part, :] = halves(arrays[k][...])


def upper_kernel(places, me_ref, high_ref, low_ref, *refs):
    arrays, (out_ref, row_high, row_low) = refs[:-4], refs[-3:]
    collect(places, me_ref[0], arrays, row_high, row_low)
    depth = row_high.shape[0]
    high = high_ref[:, :depth]
    out_ref[...] = mm(low_ref[:, :depth], row_high[...]) + mm(high, row_low[...]) + mm(high, row_high[...])


def share(places, me, part_ref, high_ref, low_ref, arrays, row_high, row_low, give):
    slot, cols = arrays[0].shape
    rows = part_ref.shape[0]
    step = rows // STEPS if rows % (STEPS * 16) == 0 else rows
    for r, table in enumerate(places):

        @pl.when(me == r)
        def _(table=table):
            here = [block for block, k in enumerate(table) if k is not None]
            span = pl.ds(here[0] * slot, (here[-1] + 1 - here[0]) * slot) if here else None
            for block in range(here[0], here[-1] + 1) if here else ():
                part = pl.ds(block * slot, slot)
                if table[block] is None:
                    row_high[part, :] = jnp.zeros((slot, cols), BF16)
                    row_low[part, :] = jnp.zeros((slot, cols), BF16)
                else:
                    row_high[part, :], row_low[part, :] = halves(arrays[table[block]][...])
            for k in range(rows // step):
                part = pl.ds(k * step, step)
                value = part_ref[part, :]
                if here:
                    high = high_ref[part, span]
                    more = mm(low_ref[part, span], row_high[span, :]) + mm(high, row_low[span, :])
                    value = value + (more + mm(high, row_high[span, :]))
                give(k, part, value)


def middle_kernel(places, me_ref, part_ref, high_ref, low_ref, *refs):
    arrays, (out_ref, row_high, row_low) = refs[:-3], refs[-3:]

    def give(k, part, value):
        out_ref[part, :] = value

    share(places, me_ref[0], part_ref, high_ref, low_ref, arrays, row_high, row_low, give)


def finish_kernel(places, me_ref, part_ref, high_ref, low_ref, *refs):
    arrays, (out_ref, row_high, row_low, total, sem) = refs[:-5], refs[-5:]

    def copy(k, part):
        return pltpu.make_async_copy(total.at[part], out_ref.at[part], sem.at[k])

    def give(k, part, value):
        total[part, :] = value
        copy(k, part).start()

    share(places, me_ref[0], part_ref, high_ref, low_ref, arrays, row_high, row_low, give)
    step = total.shape[0] // sem.shape[0]
    for k in range(sem.shape[0]):
        copy(k, pl.ds(k * step, step)).wait()


def join_kernel(first, second, *refs):
    out, sem = refs[-2:]
    rows = first.shape[0]
    copies = [
        pltpu.make_async_copy(first, out.at[:rows], sem.at[0]),
        pltpu.make_async_copy(second, out.at[rows:], sem.at[1]),
    ]
    for copy in copies:
        copy.start()
    for copy in copies:
        copy.wait()


def join(first, second, afters):
    rows, cols = first.shape
    return pl.pallas_call(
        join_kernel,
        out_shape=jax.ShapeDtypeStruct((2 * rows, cols), first.dtype),
        in_specs=[VMEM, VMEM] + [ANY] * len(afters),
        out_specs=VMEM,
        scratch_shapes=[pltpu.SemaphoreType.DMA((2,))],
        compiler_params=PARAMS,
        name="join",
    )(first, second, *afters)


def gather_shards(shard, count, afters):
    held, masks = shard, [0]
    bit = 1
    while 2 * bit < count:
        bit *= 2
    while bit:
        other = lax.ppermute(held, "col", [(i, i ^ bit) for i in range(count)])
        masks += [mask ^ bit for mask in masks]
        if bit > 1:
            held = join(held, other, afters[0])
            afters = afters[1:] or afters
        bit //= 2
    return held, other, masks


def local(row_count, col_count, matrix, panel_t, inverse_lower, pivot_rows):
    rows, cols = matrix.shape
    width = inverse_lower.shape[0]
    slot = width // row_count
    stay = width // 2
    me = lax.axis_index("row").astype(jnp.int32)
    column = lax.axis_index("col").astype(jnp.int32)
    here = me.reshape(1)
    pivot = pivot_rows.reshape(1, width)
    item_shape = jax.ShapeDtypeStruct((slot, cols), F32)

    rounds = plan(row_count)
    order = [item for moves in rounds for s, t, item in moves if s == 0]
    matrix = pltpu.with_memory_space_constraint(matrix, pltpu.HBM)
    pivot = pltpu.with_memory_space_constraint(pivot, pltpu.HBM)
    panel_t = pltpu.with_memory_space_constraint(panel_t, pltpu.HBM)
    inverse_lower = pltpu.with_memory_space_constraint(inverse_lower, pltpu.HBM)
    pieces = next(k for k in range(3, 0, -1) if rows % (16 * k) == 0 and width % (rows // k) == 0)
    *own, panel = pl.pallas_call(
        functools.partial(pick_kernel, row_count, order),
        out_shape=(item_shape,) * len(order) + (jax.ShapeDtypeStruct(panel_t.shape, F32),),
        in_specs=[SMEM, HBM, HBM, HBM],
        out_specs=(VMEM,) * (len(order) + 1),
        scratch_shapes=[
            pltpu.VMEM((rows, cols), F32),
            pltpu.VMEM((1, width), jnp.int32),
            pltpu.SemaphoreType.DMA((2 + pieces,)),
        ],
        compiler_params=PARAMS,
        name="pick",
    )(here, pivot, matrix, panel_t)

    arrays = list(own)
    found = [{} for _ in range(row_count)]
    for k, item in enumerate(order):
        found[0][item] = k
    for r in range(1, row_count):
        found[r]["pick", r] = 0
    operands, chunks = [], row_count // 2
    for moves in rounds:
        leaving = [item for s, t, item in moves if s == 0]
        operand = own[order.index(leaving[0])] if leaving else own[0]
        if len(operands) > chunks + 3 and all(item[0] == "stay" for s, t, item in moves):
            operand = arrays[len(own) + chunks]
        for s, t, item in moves:
            if s != 0 and item[0] == "stay":
                operand = jnp.where(me == s, arrays[found[s][item]], operand)
        for s, t, item in moves:
            found[t][item] = len(arrays)
        operands.append(operand)
        arrays.append(lax.ppermute(operand, "row", [(s, t) for s, t, item in moves]))
    received = arrays[len(own) :]
    blocks = [("pick", p) for p in range(chunks, row_count)]
    late_blocks = [("stay", c) for c in range(chunks)] + [("pick", p) for p in range(1, chunks)]
    soon = len(own) + chunks + 2
    places = [[found[r][item] for item in blocks] for r in range(row_count)]
    late = [
        [found[r].get(item) for item in late_blocks[:chunks] + [("moved", r)] + late_blocks[chunks:]]
        for r in range(row_count)
    ]
    soon_late = [[k if k is not None and k < soon else None for k in table] for table in late]
    late = [[k if k is not None and k >= soon else None for k in table] for table in late]
    late_rows = len(late_blocks) * slot

    picked_rows = len(blocks) * slot + late_rows
    inv_high, inv_low, land, base = pl.pallas_call(
        functools.partial(prepare_kernel, row_count),
        out_shape=(
            jax.ShapeDtypeStruct((width, picked_rows), BF16),
            jax.ShapeDtypeStruct((width, picked_rows), BF16),
            jax.ShapeDtypeStruct((rows, slot), BF16),
            jax.ShapeDtypeStruct((rows, cols), F32),
        ),
        in_specs=[SMEM, HBM, HBM, HBM],
        out_specs=(VMEM,) * 4,
        scratch_shapes=[
            pltpu.VMEM((1, width), jnp.int32),
            pltpu.VMEM((width, width), F32),
            pltpu.VMEM((rows, cols), F32),
            pltpu.SemaphoreType.DMA((3,)),
        ],
        compiler_params=PARAMS,
        cost_estimate=SHORT,
        name="prepare",
    )(here, pivot, inverse_lower, matrix)

    near, far, masks = gather_shards(panel, col_count, [operands[3:5] + [land], []])
    ids = column ^ jnp.array(masks, jnp.int32)

    def used(*tables):
        names = sorted({k for table in tables for k in jax.tree.leaves(table)})
        return [arrays[k] for k in names], [jax.tree.map(names.index, table) for table in tables]

    half = width // 2
    ends, near_high, near_low = pl.pallas_call(
        near_kernel,
        out_shape=(jax.ShapeDtypeStruct((rows, late_rows), F32),) + (jax.ShapeDtypeStruct((rows, half), BF16),) * 2,
        in_specs=[SMEM, SMEM] + [VMEM] * 3,
        out_specs=(VMEM,) * 3,
        scratch_shapes=[pltpu.VMEM((half, late_rows), F32)] * 2,
        compiler_params=PARAMS,
        name="near",
    )(here, ids, near, inv_high, inv_low)
    early_arrays, (places,) = used(places)
    upper = pl.pallas_call(
        functools.partial(upper_kernel, places),
        out_shape=jax.ShapeDtypeStruct((width, cols), F32),
        in_specs=[SMEM] + [VMEM] * (2 + len(early_arrays)) + [ANY],
        out_specs=VMEM,
        scratch_shapes=[pltpu.VMEM((picked_rows - late_rows, cols), BF16)] * 2,
        compiler_params=PARAMS,
        cost_estimate=LONG,
        name="upper",
    )(here, inv_high, inv_low, *early_arrays, ends)

    part, end_high, end_low = pl.pallas_call(
        far_kernel,
        out_shape=(jax.ShapeDtypeStruct((rows, cols), F32),)
        + (jax.ShapeDtypeStruct((rows, late_rows + slot), BF16),) * 2,
        in_specs=[SMEM, SMEM] + [VMEM] * 9,
        out_specs=(VMEM,) * 3,
        scratch_shapes=[pltpu.VMEM((rows, half), BF16)] * 2
        + [pltpu.VMEM((half, cols + late_rows), F32)] * 2
        + [pltpu.VMEM((half, cols), F32)] * 2,
        compiler_params=PARAMS,
        name="far",
    )(here, ids, far, inv_high, inv_low, upper, base, ends, land, near_high, near_low)

    row_scratch = [pltpu.VMEM((late_rows + slot, cols), BF16)] * 2
    soon_arrays, (soon_late,) = used(soon_late)
    part = pl.pallas_call(
        functools.partial(middle_kernel, soon_late),
        out_shape=jax.ShapeDtypeStruct((rows, cols), F32),
        in_specs=[SMEM] + [VMEM] * (3 + len(soon_arrays)),
        out_specs=VMEM,
        scratch_shapes=row_scratch,
        compiler_params=PARAMS,
        name="middle",
    )(here, part, end_high, end_low, *soon_arrays)

    late_arrays, (late,) = used(late)
    steps = STEPS if rows % (STEPS * 16) == 0 else 1
    return pl.pallas_call(
        functools.partial(finish_kernel, late),
        out_shape=jax.ShapeDtypeStruct((rows, cols), F32),
        in_specs=[SMEM] + [VMEM] * (3 + len(late_arrays)),
        out_specs=HBM,
        scratch_shapes=row_scratch + [pltpu.VMEM((rows, cols), F32), pltpu.SemaphoreType.DMA((steps,))],
        compiler_params=PARAMS,
        name="finish",
    )(here, part, end_high, end_low, *late_arrays)


def solution(mesh):
    in_specs = (P("row", "col"), P("col", "row"), P(), P())
    out_specs = P("row", "col")
    return jax.shard_map(
        functools.partial(local, mesh.shape["row"], mesh.shape["col"]),
        mesh=mesh,
        in_specs=in_specs,
        out_specs=out_specs,
        check_vma=False,
    )
```
